32 devices in a mesh: crop: 16 (over z, x, core), seq: 2 (over y).
Axes of the slice: x: 2, y: 2, z: 4, core: 2. Of those that a mesh axis runs over, the one named last changes fastest.
Arguments:
- token_ids: int32 [16, 1024], P('crop', 'seq'), may hold values from 0 to 32
- embedding: float32 [33, 640], replicated, may hold values from -6 to 6
- first_gain: float32 [640], replicated, may hold values from 0.5 to 1.5
- first_shift: float32 [640], replicated, may hold values from -4 to 4
- query_weight: float32 [640, 640], replicated, may hold values from -0.3125 to 0.3125
- query_bias: float32 [640], replicated, may hold values from -4 to 4
- key_weight: float32 [640, 640], replicated, may hold values from -0.3125 to 0.3125
- key_bias: float32 [640], replicated, may hold values from -4 to 4
- value_weight: float32 [640, 640], replicated, may hold values from -0.25 to 0.25
- value_bias: float32 [640], replicated, may hold values from -4 to 4
- out_weight: float32 [640, 640], replicated, may hold values from -1 to 1
- out_bias: float32 [640], replicated, may hold values from -4 to 4
- second_gain: float32 [640], replicated, may hold values from 0.5 to 1.5
- second_shift: float32 [640], replicated, may hold values from -4 to 4
- up_weight: float32 [640, 2560], replicated, may hold values from -0.25 to 0.25
- up_bias: float32 [2560], replicated, may hold values from -4 to 4
- down_weight: float32 [2560, 640], replicated, may hold values from -0.125 to 0.125
- down_bias: float32 [640], replicated, may hold values from -4 to 4
- cotangent: float32 [16, 1024, 640], P('crop', 'seq'), may hold values from -6 to 6
- crop_cluster: int32 [16], P('crop'), may hold values from 0 to 4095
- cluster_weight: float32 [4096], replicated, may hold values from 0.25 to 4
Outputs:
- block_out: float32 [16, 1024, 640], P('crop', 'seq')
- grad_embedding: float32 [33, 640], replicated
- grad_first_gain: float32 [640], replicated
- grad_first_shift: float32 [640], replicated
- grad_query_weight: float32 [640, 640], replicated
- grad_query_bias: float32 [640], replicated
- grad_key_weight: float32 [640, 640], replicated
- grad_key_bias: float32 [640], replicated
- grad_value_weight: float32 [640, 640], replicated
- grad_value_bias: float32 [640], replicated
- grad_out_weight: float32 [640, 640], replicated
- grad_out_bias: float32 [640], replicated
- grad_second_gain: float32 [640], replicated
- grad_second_shift: float32 [640], replicated
- grad_up_weight: float32 [640, 2560], replicated
- grad_up_bias: float32 [2560], replicated
- grad_down_weight: float32 [2560, 640], replicated
- grad_down_bias: float32 [640], replicated
The draws below stay inside these ranges and needn't reach their ends.
All inputs are finite; a program needn't handle non-finite values.
Results may differ from the reference program's by a relative error of at most 0.0003.
Values sent between devices are 32-bit elements; how exact they have to be, the bound alone decides.
No kernel may reach another device: no remote copies, remote signals or barrier semaphores. Data moves between devices by JAX's collectives and lax.ppermute only.
A program may use at most 192 MiB of HBM per device.

```python
import math
import jax
import jax.numpy as jnp
from jax import lax

D = 640
HEADS = 20
HDIM = 32
FF = 2560
VOCAB = 33
LEN = 1024
CLUSTERS = 4096
CROPS = 16


def touch_ends(entries, rng, least, top_value):
    dims = entries.shape
    place = [jax.random.randint(jax.random.fold_in(rng, axis), (), 0, dims[axis]) for axis in range(len(dims))]
    entries = entries.at[tuple(place)].set(least)
    longest = dims.index(max(dims))
    place[longest] = (place[longest] + 1) % dims[longest]
    return entries.at[tuple(place)].set(top_value)


def shard_levels(stream_key, dims, pieces, least, largest):
    gain = 1.0
    for position, blocks in pieces:
        heights = jax.random.uniform(jax.random.fold_in(jax.random.fold_in(stream_key, 6), position), (blocks,), jnp.float32, least / len(pieces), largest / len(pieces))
        gain = gain * jnp.repeat(jnp.exp(heights), dims[position] // blocks).reshape((-1,) + (1,) * (len(dims) - 1 - position))
    return gain


def bell_draw(own_key, dims, deviation, reach, split=(), held_as=jnp.bfloat16):
    level = shard_levels(own_key, dims, split, -0.22, 0.18) if split else 1.0
    drawn = jax.random.normal(own_key, dims, jnp.float32) * deviation * level
    return jnp.minimum(jnp.maximum(drawn, -reach), reach).astype(held_as)


def setup_inputs(seed: int = 0) -> dict:
    streams_of = jax.random.split(jax.random.key(seed), 22)
    token_ids = touch_ends(jax.random.randint(streams_of[0], (CROPS, LEN), 0, VOCAB), jax.random.fold_in(streams_of[0], 1), 0, VOCAB - 1).astype(jnp.int32)
    embedding = bell_draw(streams_of[1], (VOCAB, D), 1.0, 6.0, (), jnp.float32)
    first_gain = jnp.clip(1.0 + 0.1 * jax.random.normal(streams_of[2], (D,), jnp.float32), 0.5, 1.5)
    first_shift = bell_draw(streams_of[3], (D,), 0.3, 4.0, (), jnp.float32)
    query_weight = bell_draw(streams_of[4], (D, D), (D // 2) ** -0.5, 0.3125, (), jnp.float32)
    query_bias = bell_draw(streams_of[5], (D,), 0.3, 4.0, (), jnp.float32)
    key_weight = bell_draw(streams_of[6], (D, D), (D // 2) ** -0.5, 0.3125, (), jnp.float32)
    key_bias = bell_draw(streams_of[7], (D,), 0.3, 4.0, (), jnp.float32)
    value_weight = bell_draw(streams_of[8], (D, D), D ** -0.5, 0.25, (), jnp.float32)
    value_bias = bell_draw(streams_of[9], (D,), 0.3, 4.0, (), jnp.float32)
    out_weight = bell_draw(streams_of[10], (D, D), (D // 16) ** -0.5, 1.0, (), jnp.float32)
    out_bias = bell_draw(streams_of[11], (D,), 0.3, 4.0, (), jnp.float32)
    second_gain = jnp.clip(1.0 + 0.1 * jax.random.normal(streams_of[12], (D,), jnp.float32), 0.5, 1.5)
    second_shift = bell_draw(streams_of[13], (D,), 0.3, 4.0, (), jnp.float32)
    up_weight = bell_draw(streams_of[14], (D, FF), D ** -0.5, 0.25, (), jnp.float32)
    up_bias = bell_draw(streams_of[15], (FF,), 0.3, 4.0, (), jnp.float32)
    down_weight = bell_draw(streams_of[16], (FF, D), FF ** -0.5, 0.125, (), jnp.float32)
    down_bias = bell_draw(streams_of[17], (D,), 0.3, 4.0, (), jnp.float32)
    cotangent = bell_draw(streams_of[18], (CROPS, LEN, D), 1.0, 6.0, ((0, 16), (1, 2)), jnp.float32)
    crop_cluster = touch_ends(jax.random.randint(streams_of[19], (CROPS,), 0, CLUSTERS), jax.random.fold_in(streams_of[19], 1), 0, CLUSTERS - 1).astype(jnp.int32)
    cluster_weight = jnp.clip(jnp.exp(jax.random.uniform(streams_of[20], (CLUSTERS,), jnp.float32, math.log(0.25), math.log(4.0))), 0.25, 4.0)
    return dict(token_ids=token_ids, embedding=embedding, first_gain=first_gain, first_shift=first_shift, query_weight=query_weight, query_bias=query_bias, key_weight=key_weight, key_bias=key_bias, value_weight=value_weight, value_bias=value_bias, out_weight=out_weight, out_bias=out_bias, second_gain=second_gain, second_shift=second_shift, up_weight=up_weight, up_bias=up_bias, down_weight=down_weight, down_bias=down_bias, cotangent=cotangent, crop_cluster=crop_cluster, cluster_weight=cluster_weight)


highest = lax.Precision.HIGHEST
epsilon = 1e-05

@jax.custom_vjp
def low(v):
    return lax.optimization_barrier(v.astype(jnp.bfloat16)).astype(jnp.float32)

@jax.custom_vjp
def low_back(v):
    return v

def low_keep(v):
    return (low(v), None)

def low_pass(kept, grad):
    return (grad,)

def back_keep(v):
    return (v, None)

def back_low(kept, grad):
    return (low(grad),)
low.defvjp(low_keep, low_pass)
low_back.defvjp(back_keep, back_low)

def layer_norm(inputs, gain_vec, shift_vec):
    row_mean = lax.optimization_barrier(jnp.mean(inputs, axis=-1, keepdims=True))
    centred = inputs - row_mean
    spread = lax.optimization_barrier(jnp.mean(centred * centred, axis=-1, keepdims=True))
    return centred * lax.rsqrt(spread + epsilon) * gain_vec + shift_vec

def rotate(vectors, positions):
    half_dim = vectors.shape[-1] // 2
    frequency = 10000.0 ** (-2.0 * jnp.arange(half_dim, dtype=jnp.float32) / vectors.shape[-1])
    angles = positions.astype(jnp.float32)[:, None] * frequency[None, :]
    cosine = jnp.cos(angles)[:, None, :]
    sine_part = jnp.sin(angles)[:, None, :]
    first_half = vectors[..., :half_dim]
    second_half = vectors[..., half_dim:]
    return jnp.concatenate([first_half * cosine - second_half * sine_part, second_half * cosine + first_half * sine_part], axis=-1)

def matmul(left, right):
    return jnp.dot(left, right, precision=highest)

def crop_forward(params, crop_ids):
    embedding, first_gain, first_shift, query_weight, query_bias, key_weight, key_bias, value_weight, value_bias, out_weight, out_bias, second_gain, second_shift, up_weight, up_bias, down_weight, down_bias = params
    length = crop_ids.shape[0]
    hidden = jnp.take(embedding, crop_ids, axis=0)
    normed = layer_norm(hidden, first_gain, first_shift)
    positions = jnp.arange(length, dtype=jnp.int32)
    shape_heads = (length, HEADS, HDIM)
    queries = rotate((matmul(normed, query_weight) + query_bias).reshape(shape_heads), positions)
    keys_all = rotate((matmul(normed, key_weight) + key_bias).reshape(shape_heads), positions)
    values_all = (matmul(normed, value_weight) + value_bias).reshape(shape_heads)
    scores = jnp.einsum('qhe,khe->hqk', queries, keys_all, precision=highest) * HDIM ** (-0.5)
    attn_probs = jax.nn.softmax(scores, axis=-1)
    attended = jnp.einsum('hqk,khe->qhe', attn_probs, values_all, precision=highest).reshape(length, HEADS * HDIM)
    after_attn = hidden + matmul(attended, out_weight) + out_bias
    normed_two = layer_norm(after_attn, second_gain, second_shift)
    ff_hidden = jax.nn.gelu(matmul(normed_two, up_weight) + up_bias, approximate=False)
    return after_attn + matmul(ff_hidden, down_weight) + down_bias

def reference(token_ids, embedding, first_gain, first_shift, query_weight, query_bias, key_weight, key_bias, value_weight, value_bias, out_weight, out_bias, second_gain, second_shift, up_weight, up_bias, down_weight, down_bias, cotangent, crop_cluster, cluster_weight):
    params = (embedding, first_gain, first_shift, query_weight, query_bias, key_weight, key_bias, value_weight, value_bias, out_weight, out_bias, second_gain, second_shift, up_weight, up_bias, down_weight, down_bias)
    crop_weight = jnp.take(cluster_weight, crop_cluster, axis=0)

    def crop_step(grad_sum, slices):
        crop_ids, crop_grad, weight_one = slices
        crop_out, pull_back = jax.vjp(lambda weights_now: crop_forward(weights_now, crop_ids), params)
        crop_grads = pull_back(crop_grad * weight_one)[0]
        grad_sum = jax.tree.map(lambda total_now, extra: total_now + extra, grad_sum, crop_grads)
        return (grad_sum, crop_out)
    start_sum = jax.tree.map(jnp.zeros_like, params)
    grad_sum, block_out = lax.scan(crop_step, start_sum, (token_ids, cotangent, crop_weight))
    return (block_out, grad_sum[0], grad_sum[1], grad_sum[2], grad_sum[3], grad_sum[4], grad_sum[5], grad_sum[6], grad_sum[7], grad_sum[8], grad_sum[9], grad_sum[10], grad_sum[11], grad_sum[12], grad_sum[13], grad_sum[14], grad_sum[15], grad_sum[16])
```

```python
import math
import jax
import jax.numpy as jnp
from jax import lax
from jax.experimental import pallas as pl
from jax.experimental.pallas import tpu as pltpu
from jax.sharding import PartitionSpec as P

HEADS = 20
HDIM = 32
HALF = 16
VOCAB = 33
ROWS = 40
f32 = jnp.float32
bf16 = jnp.bfloat16
highest = lax.Precision.HIGHEST
high = lax.Precision.HIGH
epsilon = 1e-05
LOG2E = 1.0 / math.log(2.0)
SCALE = HDIM**-0.5

NN = (((1,), (0,)), ((), ()))
NT = (((1,), (1,)), ((), ()))
TN = (((0,), (0,)), ((), ()))


def layer_norm(inputs, gain_vec, shift_vec):
    row_mean = jnp.mean(inputs, axis=-1, keepdims=True)
    centred = inputs - row_mean
    spread = jnp.mean(centred * centred, axis=-1, keepdims=True)
    return centred * lax.rsqrt(spread + epsilon) * gain_vec + shift_vec


def pieces(x, count):
    out = []
    for _ in range(count - 1):
        head = lax.reduce_precision(x, 8, 7)
        out.append(head)
        x = x - head
    out.append(lax.reduce_precision(x, 8, 7))
    return out


def dot(a, b, dims=NN):
    return lax.dot_general(a, b, dims, preferred_element_type=f32)


def split2(x):
    head = x.astype(bf16)
    return head, (x - head.astype(f32)).astype(bf16)


def split3(x):
    head = x.astype(bf16)
    x = x - head.astype(f32)
    mid = x.astype(bf16)
    return head, mid, (x - mid.astype(f32)).astype(bf16)


def turn(u, cos, sin):
    a, b = u[:HALF], u[HALF:]
    return jnp.concatenate([a * cos - b * sin, b * cos + a * sin], axis=0)


def turn_back(u, cos, sin):
    a, b = u[:HALF], u[HALF:]
    return jnp.concatenate([a * cos + b * sin, b * cos - a * sin], axis=0)


def lookup_pack(table_q, table_k, hot_q, hot, cosq, sinq, cosk, sink, tail_q, tail_k):
    q = turn(dot(table_q, hot_q), cosq, sinq) * (SCALE * LOG2E)
    k = turn(dot(table_k, hot), cosk, sink)
    q1, q2 = split2(q)
    k1, k2 = split2(k)
    return (
        jnp.concatenate([q1, q1, q2, tail_q], axis=0),
        jnp.concatenate([k1, k2, k1, tail_k], axis=0),
    )


def forward_kernel(tq, tk, tv, hot_q, hot, cosq, sinq, cosk, sink, att, logs, counts):
    span = hot_q.shape[-1]
    whole = hot.shape[-1]
    qp, kp = lookup_pack(
        tq[0], tk[0], hot_q[0], hot[0], cosq[...], sinq[...], cosk[...], sink[...],
        jnp.zeros((32, span), bf16), jnp.zeros((32, whole), bf16),
    )
    ids = hot[0, :ROWS, :]
    step = min(256, span)
    for c in range(0, span, step):
        s = dot(kp, qp[:, c : c + step], TN)
        top = jnp.max(s, axis=0, keepdims=True)
        p = jnp.exp2(s - top)
        p1, p2 = split2(p)
        cnt = dot(ids, p1) + dot(ids, p2)
        total = jnp.sum(cnt, axis=0, keepdims=True)
        cnt = cnt / total
        counts[0, 0, :, c : c + step] = cnt
        logs[0, 0, :, c : c + step] = top + jnp.log2(total)
        c1, c2 = split2(cnt)
        att[0, :, c : c + step] = dot(
            tv[0], jnp.concatenate([c1.astype(f32), c1.astype(f32), c2.astype(f32)], axis=0).astype(bf16)
        )


def backward_kernel(
    tq, tk, tvt, hot_q, hot, hot3, cosq, sinq, cosk, sink, logs, counts, datt, gq, gk, gv
):
    span = hot_q.shape[-1]
    whole = hot.shape[-1]

    @pl.when(pl.program_id(1) == 0)
    def _():
        gq[...] = jnp.zeros_like(gq)
        gk[...] = jnp.zeros_like(gk)
        gv[...] = jnp.zeros_like(gv)

    l1, l2, l3 = split3(-logs[0, 0])
    row = lax.broadcasted_iota(jnp.int32, (32, span), 0)
    tail_q = jnp.where(
        row == 0,
        l1.astype(f32),
        jnp.where(row == 1, l2.astype(f32), jnp.where(row == 2, l3.astype(f32), 0.0)),
    ).astype(bf16)
    tail_k = jnp.where(lax.broadcasted_iota(jnp.int32, (32, whole), 0) < 3, 1.0, 0.0).astype(bf16)
    qp, kp = lookup_pack(
        tq[0], tk[0], hot_q[0], hot[0], cosq[...], sinq[...], cosk[...], sink[...], tail_q, tail_k
    )
    d_out = datt[0]
    d1, d2 = split2(d_out)
    cnt = counts[0, 0]
    e = dot(tvt[0], jnp.concatenate([d1, d1, d2], axis=0))
    e = e - jnp.sum(e * cnt, axis=0, keepdims=True)
    e1, e2, e3 = split3(e)
    e_pack = jnp.concatenate(
        [e1.astype(f32), e2.astype(f32), e3.astype(f32), jnp.zeros((8, span), f32)], axis=0
    ).astype(bf16)
    c1, c2 = split2(cnt)
    gv_full = dot(jnp.concatenate([d1, d2], axis=0), c1, NT)
    gv[0] += gv_full[:HDIM] + gv_full[HDIM:] + dot(d1, c2, NT)
    step = min(256, span)
    dq_parts = []
    dk = jnp.zeros((HDIM, whole), f32)
    for c in range(0, span, step):
        p = jnp.exp2(dot(kp, qp[:, c : c + step], TN))
        ds = p * dot(hot3[0], e_pack[:, c : c + step])
        s1, s2 = split2(ds)
        a = dot(kp[: 2 * HDIM], s1)
        dq_parts.append(a[:HDIM] + a[HDIM:] + dot(kp[:HDIM], s2))
        b = dot(qp[HDIM : 3 * HDIM, c : c + step], s1, NT)
        dk += b[:HDIM] + b[HDIM:] + dot(qp[:HDIM, c : c + step], s2, NT)
    dq = dq_parts[0] if len(dq_parts) == 1 else jnp.concatenate(dq_parts, axis=1)
    dq = turn_back(dq, cosq[...], sinq[...]) * SCALE
    dk = turn_back(dk, cosk[...], sink[...]) * (1.0 / LOG2E)
    a = dot(jnp.concatenate(split2(dq), axis=0), hot_q[0, :ROWS, :], NT)
    gq[0] += a[:HDIM] + a[HDIM:]
    b = dot(jnp.concatenate(split2(dk), axis=0), hot[0, :ROWS, :], NT)
    gk[0] += b[:HDIM] + b[HDIM:]


def per_head(*dims):
    return pl.BlockSpec((1,) + dims, lambda h, c: (h,) + (0,) * len(dims))


def per_crop(*dims):
    return pl.BlockSpec((1,) + dims, lambda h, c: (c,) + (0,) * len(dims))


def fixed(*dims):
    return pl.BlockSpec(dims, lambda h, c: (0,) * len(dims))


def attention_forward(tq, tk, tv, hot_q, hot, cosq, sinq, cosk, sink):
    crops, _, span = hot_q.shape
    whole = hot.shape[-1]
    return pl.pallas_call(
        forward_kernel,
        grid=(HEADS, crops),
        in_specs=[
            per_head(HDIM, 128),
            per_head(HDIM, 128),
            per_head(HDIM, 3 * ROWS),
            per_crop(128, span),
            per_crop(128, whole),
            fixed(HALF, span),
            fixed(HALF, span),
            fixed(HALF, whole),
            fixed(HALF, whole),
        ],
        out_specs=[
            pl.BlockSpec((1, HDIM, span), lambda h, c: (c, h, 0)),
            pl.BlockSpec((1, 1, 1, span), lambda h, c: (c, h, 0, 0)),
            pl.BlockSpec((1, 1, ROWS, span), lambda h, c: (c, h, 0, 0)),
        ],
        out_shape=[
            jax.ShapeDtypeStruct((crops, HEADS * HDIM, span), f32),
            jax.ShapeDtypeStruct((crops, HEADS, 1, span), f32),
            jax.ShapeDtypeStruct((crops, HEADS, ROWS, span), f32),
        ],
        compiler_params=pltpu.CompilerParams(vmem_limit_bytes=40 << 20),
    )(tq, tk, tv, hot_q, hot, cosq, sinq, cosk, sink)


def attention_backward(tq, tk, tvt, hot_q, hot, hot3, cosq, sinq, cosk, sink, logs, counts, datt):
    crops, _, span = hot_q.shape
    whole = hot.shape[-1]
    table = jax.ShapeDtypeStruct((HEADS, HDIM, ROWS), f32)
    return pl.pallas_call(
        backward_kernel,
        grid=(HEADS, crops),
        in_specs=[
            per_head(HDIM, 128),
            per_head(HDIM, 128),
            per_head(ROWS, 3 * HDIM),
            per_crop(128, span),
            per_crop(128, whole),
            per_crop(whole, 128),
            fixed(HALF, span),
            fixed(HALF, span),
            fixed(HALF, whole),
            fixed(HALF, whole),
            pl.BlockSpec((1, 1, 1, span), lambda h, c: (c, h, 0, 0)),
            pl.BlockSpec((1, 1, ROWS, span), lambda h, c: (c, h, 0, 0)),
            pl.BlockSpec((1, HDIM, span), lambda h, c: (c, h, 0)),
        ],
        out_specs=[per_head(HDIM, ROWS)] * 3,
        out_shape=[table] * 3,
        compiler_params=pltpu.CompilerParams(vmem_limit_bytes=40 << 20),
    )(tq, tk, tvt, hot_q, hot, hot3, cosq, sinq, cosk, sink, logs, counts, datt)


def bits_of(axis):
    size = lax.axis_size(axis)
    return [(axis, 1 << i) for i in range(size.bit_length() - 1)]


def swap(x, stage):
    axis, bit = stage
    return lax.ppermute(x, axis, [(i, i ^ bit) for i in range(lax.axis_size(axis))])


def side(stage):
    axis, bit = stage
    return (lax.axis_index(axis) // bit) % 2


def reduce_scatter(x, stages):
    for stage in stages:
        half = x.shape[0] // 2
        me = side(stage)
        away = lax.dynamic_slice_in_dim(x, (1 - me) * half, half, 0)
        here = lax.dynamic_slice_in_dim(x, me * half, half, 0)
        x = here + swap(away, stage)
    return x


def all_gather(x, stages):
    for stage in reversed(stages):
        other = swap(x, stage)
        x = jnp.where(
            side(stage) == 0,
            jnp.concatenate([x, other], axis=0),
            jnp.concatenate([other, x], axis=0),
        )
    return x


def all_reduce(x, orders):
    count = 1
    for _ in orders[0]:
        count *= 2
    rows = x.shape[0]
    unit = count * 8
    if rows % (unit * len(orders)):
        return lax.psum(x, ("crop", "seq"))
    part = rows // len(orders)
    sums = [
        reduce_scatter(x[i * part : (i + 1) * part], order) for i, order in enumerate(orders)
    ]
    return jnp.concatenate([all_gather(s, order) for s, order in zip(sums, orders)], axis=0)


def local(
    token_ids,
    embedding,
    first_gain,
    first_shift,
    query_weight,
    query_bias,
    key_weight,
    key_bias,
    value_weight,
    value_bias,
    out_weight,
    out_bias,
    second_gain,
    second_shift,
    up_weight,
    up_bias,
    down_weight,
    down_bias,
    cotangent,
    crop_cluster,
    cluster_weight,
):
    crops, span = token_ids.shape
    width = embedding.shape[1]
    ring = lax.axis_size("seq")
    whole = span * ring
    here = lax.axis_index("seq")

    if ring == 2:
        other = swap(token_ids, ("seq", 1))
        ids = jnp.where(
            here == 0,
            jnp.concatenate([token_ids, other], axis=1),
            jnp.concatenate([other, token_ids], axis=1),
        )
    else:
        ids = lax.all_gather(token_ids, "seq", axis=1, tiled=True)

    def table_rows(embedding, first_gain, first_shift, wq, bq, wk, bk, wv, bv):
        normed = layer_norm(embedding, first_gain, first_shift)
        return tuple(
            jnp.dot(normed, w, precision=highest) + b for w, b in ((wq, bq), (wk, bk), (wv, bv))
        )

    (rows_q, rows_k, rows_v), pull_rows = jax.vjp(
        table_rows, embedding, first_gain, first_shift, query_weight, query_bias, key_weight, key_bias,
        value_weight, value_bias,
    )

    def by_head(rows):
        rows = jnp.pad(rows, ((0, ROWS - VOCAB), (0, 0)))
        return jnp.transpose(rows.reshape(ROWS, HEADS, HDIM), (1, 0, 2))

    def lookup_table(rows):
        t = jnp.transpose(by_head(rows), (0, 2, 1))
        return jnp.pad(jnp.concatenate(pieces(t, 3), axis=2), ((0, 0), (0, 0), (0, 8))).astype(bf16)

    tq, tk = lookup_table(rows_q), lookup_table(rows_k)
    heads_v = by_head(rows_v)
    v1, v2 = pieces(heads_v, 2)
    tvt = jnp.concatenate([v1, v2, v1], axis=2).astype(bf16)
    t1, t2 = jnp.transpose(v1, (0, 2, 1)), jnp.transpose(v2, (0, 2, 1))
    tv = jnp.concatenate([t1, t2, t1], axis=2).astype(bf16)

    spots = jnp.arange(128, dtype=jnp.int32)
    code = jnp.where(spots < 3 * ROWS, spots % ROWS, -1)
    hot = (ids[:, None, :] == code[None, :, None]).astype(bf16)
    hot_q = (token_ids[:, None, :] == code[None, :, None]).astype(bf16)
    hot3 = (ids[:, :, None] == code[None, None, :]).astype(bf16)
    onehot = (token_ids[..., None] == jnp.arange(VOCAB, dtype=jnp.int32)).astype(f32)

    frequency = 10000.0 ** (-2.0 * jnp.arange(HALF, dtype=f32) / HDIM)
    angles = frequency[:, None] * jnp.arange(whole, dtype=jnp.int32).astype(f32)[None, :]
    cosk, sink = jnp.cos(angles), jnp.sin(angles)
    cosq = lax.dynamic_slice_in_dim(cosk, here * span, span, 1)
    sinq = lax.dynamic_slice_in_dim(sink, here * span, span, 1)

    att, logs, counts = attention_forward(tq, tk, tv, hot_q, hot, cosq, sinq, cosk, sink)

    hidden = jnp.einsum("csv,vd->csd", onehot, embedding, precision=highest)

    def after(
        hidden, att, out_weight, out_bias, second_gain, second_shift, up_weight, up_bias, down_weight, down_bias
    ):
        after_attn = hidden + jnp.einsum("cds,df->csf", att, out_weight, precision=high) + out_bias
        normed_two = layer_norm(after_attn, second_gain, second_shift)
        ff = jnp.einsum("csd,df->csf", normed_two, up_weight, precision=high) + up_bias
        ff = jax.nn.gelu(ff, approximate=False)
        return after_attn + jnp.einsum("csf,fd->csd", ff, down_weight, precision=high) + down_bias

    block_out, pull_after = jax.vjp(
        after, hidden, att, out_weight, out_bias, second_gain, second_shift, up_weight, up_bias,
        down_weight, down_bias,
    )
    matches = crop_cluster[:, None] == jnp.arange(cluster_weight.shape[0], dtype=jnp.int32)[None, :]
    crop_weight = jnp.sum(jnp.where(matches, cluster_weight[None, :], 0.0), axis=1)
    grad_out = cotangent * crop_weight[:, None, None]
    d_hidden, d_att, g_ow, g_ob, g_sg, g_ss, g_uw, g_ub, g_dw, g_db = pull_after(grad_out)

    gq, gk, gv = attention_backward(
        tq, tk, tvt, hot_q, hot, hot3, cosq, sinq, cosk, sink, logs, counts, d_att
    )
    residual = jnp.einsum("csv,csd->vd", onehot, d_hidden, precision=highest)

    seq_bits, crop_bits = bits_of("seq"), bits_of("crop")
    core, rest = crop_bits[:1], crop_bits[1:]
    order_a = core + rest[:1] + seq_bits + rest[1:]
    order_b = core + seq_bits + rest
    orders = (order_a, order_b)
    g_dw = all_reduce(g_dw, orders)
    g_uw = all_reduce(g_uw.T, orders).T

    small = [gq, gk, gv, residual, g_ow, g_ob, g_sg, g_ss, g_ub, g_db]
    flat = jnp.concatenate([g.reshape(-1) for g in small])
    size = flat.shape[0]
    count = lax.axis_size("seq") * lax.axis_size("crop")
    unit = 128 * 16 * count
    flat = jnp.pad(flat, (0, -size % unit)).reshape(-1, 128)
    flat = all_reduce(flat, orders).reshape(-1)
    out, at = [], 0
    for g in small:
        out.append(flat[at : at + g.size].reshape(g.shape))
        at += g.size
    gq, gk, gv, residual, g_ow, g_ob, g_sg, g_ss, g_ub, g_db = out

    def rows_of(g):
        return jnp.transpose(g, (2, 0, 1)).reshape(ROWS, width)[:VOCAB]

    g_e, g_fg, g_fs, g_qw, g_qb, g_kw, g_kb, g_vw, g_vb = pull_rows(
        (rows_of(gq), rows_of(gk), rows_of(gv))
    )
    return (
        block_out, g_e + residual, g_fg, g_fs, g_qw, g_qb, g_kw, g_kb, g_vw, g_vb, g_ow, g_ob, g_sg, g_ss,
        g_uw, g_ub, g_dw, g_db,
    )


def solution(mesh):
    in_specs = (
        (P("crop", "seq"),) + (P(),) * 17 + (P("crop", "seq", None), P("crop"), P())
    )
    out_specs = (P("crop", "seq", None),) + (P(),) * 17
    return jax.shard_map(local, mesh=mesh, in_specs=in_specs, out_specs=out_specs, check_vma=False)
```

```python
import math
import jax
import jax.numpy as jnp
import numpy as np
from jax import lax
from jax.experimental import pallas as pl
from jax.experimental.pallas import tpu as pltpu
from jax.sharding import PartitionSpec as P

HEADS = 20
HDIM = 32
HALF = 16
VOCAB = 33
ROWS = 40
GROUP = 4
f32 = jnp.float32
bf16 = jnp.bfloat16
epsilon = 1e-05
LOG2E = 1.0 / math.log(2.0)
SCALE = HDIM**-0.5

NN = (((1,), (0,)), ((), ()))
NT = (((1,), (1,)), ((), ()))
TN = (((0,), (0,)), ((), ()))
ANY = pl.BlockSpec(memory_space=pl.ANY)


def params(mib):
    return pltpu.CompilerParams(vmem_limit_bytes=mib << 20)


def cost(us):
    return pl.CostEstimate(flops=int(us * COST), bytes_accessed=0, transcendentals=0)


COST = 2e8


def dot(a, b, dims=NN):
    return lax.dot_general(a, b, dims, preferred_element_type=f32)


def split2(x):
    head = x.astype(bf16)
    return head, (x - head.astype(f32)).astype(bf16)


def split3(x):
    head = x.astype(bf16)
    x = x - head.astype(f32)
    mid = x.astype(bf16)
    return head, mid, (x - mid.astype(f32)).astype(bf16)


def three(a, b, dims=NN):
    return dot(a[0], b[0], dims) + dot(a[0], b[1], dims) + dot(a[1], b[0], dims)


def turn(u, cos, sin):
    a, b = u[:HALF], u[HALF:]
    return jnp.concatenate([a * cos - b * sin, b * cos + a * sin], axis=0)


def turn_back(u, cos, sin):
    a, b = u[:HALF], u[HALF:]
    return jnp.concatenate([a * cos + b * sin, b * cos - a * sin], axis=0)


def stack(*rows):
    return jnp.concatenate([r.astype(f32) for r in rows], axis=0).astype(bf16)


def norm_stats(x):
    centred = x - jnp.mean(x, axis=-1, keepdims=True)
    scale = lax.rsqrt(jnp.mean(centred * centred, axis=-1, keepdims=True) + epsilon)
    return centred * scale, scale


def norm_back(d_normed, unit, scale, gain):
    d = d_normed * gain
    d = d - jnp.mean(d, axis=-1, keepdims=True) - unit * jnp.mean(d * unit, axis=-1, keepdims=True)
    return d * scale


def tall(emb):
    return jnp.concatenate([emb, jnp.zeros((ROWS - VOCAB, emb.shape[1]), f32)], axis=0)


def prepare_kernel(
    ids, emb, gain, shift, wq, bq, wk, bk, wv, bv, tq, tk, tv, hot, hot3, packed, normed
):
    crops, whole = ids.shape
    width = emb.shape[1]
    step = pl.program_id(0)

    @pl.when(step == 0)
    def _():
        rows = tall(emb[...])
        unit, _ = norm_stats(rows)
        normed[...] = stack(*split3(unit * gain[...] + shift[...]), jnp.zeros((8, width), bf16))
        packed[...] = stack(*split3(rows), jnp.zeros((8, width), bf16))
        spot = lax.broadcasted_iota(jnp.int32, (128, whole), 0)
        code = jnp.where(
            spot < ROWS, spot, jnp.where(spot < 2 * ROWS, spot - ROWS, jnp.where(spot < 3 * ROWS, spot - 2 * ROWS, -1))
        )
        for c in range(crops):
            spots = jnp.where(ids[c : c + 1, :] == code, 1.0, 0.0)
            hot[c] = spots.astype(bf16)
            hot3[c] = spots.T.astype(bf16)

    full = normed[...]
    real = lax.broadcasted_iota(jnp.int32, (ROWS, 128), 0) < VOCAB

    def table(w, b):
        w1, w2, w3 = split3(w[...])
        by1 = dot(full, w1)
        by2 = dot(full[: 2 * ROWS], w2)
        t = by1[:ROWS] + (
            (by1[ROWS : 2 * ROWS] + by2[:ROWS])
            + (by1[2 * ROWS : 3 * ROWS] + by2[ROWS:] + dot(full[:ROWS], w3))
        )
        return jnp.where(real, t + b[...], 0.0)

    def lay(a, b, c):
        blank = jnp.zeros((8, 128), f32)
        return jnp.concatenate([a.astype(f32), b.astype(f32), c.astype(f32), blank], axis=0).T.astype(bf16)

    tq[...] = lay(*split3(table(wq, bq)))
    tk[...] = lay(*split3(table(wk, bk)))
    v1, v2 = split2(table(wv, bv))
    tv[...] = lay(v1, v2, v1)


def prepare(ids, emb, gain, shift, wq, bq, wk, bk, wv, bv):
    crops, whole = ids.shape
    width = emb.shape[1]
    full = lambda *dims: pl.BlockSpec(dims, lambda i: (0,) * len(dims))
    weight = pl.BlockSpec((width, 128), lambda i: (0, i))
    bias = pl.BlockSpec((1, 128), lambda i: (0, i))
    table = pl.BlockSpec((128, 128), lambda i: (i, 0))
    like = jax.ShapeDtypeStruct
    return pl.pallas_call(
        prepare_kernel,
        grid=(width // 128,),
        in_specs=[full(crops, whole), full(VOCAB, width), full(1, width), full(1, width)] + [weight, bias] * 3,
        out_specs=[table] * 3 + [full(crops, 128, whole), full(crops, whole, 128), full(128, width)],
        out_shape=[like((width, 128), bf16)] * 3
        + [like((crops, 128, whole), bf16), like((crops, whole, 128), bf16), like((128, width), bf16)],
        scratch_shapes=[pltpu.VMEM((128, width), bf16)],
        compiler_params=params(32),
        cost_estimate=cost(5),
        name="rows",
    )(ids, emb, gain, shift, wq, bq, wk, bk, wv, bv)


def finish_kernel(
    emb, gain, shift, gq, gk, gv, residual, wq, wk, wv, g_wq, g_wk, g_wv, g_bq, g_bk, g_bv, g_emb, g_gain, g_shift,
    normed, d_normed,
):
    step = pl.program_id(0)

    @pl.when(step == 0)
    def _():
        unit, _ = norm_stats(tall(emb[...]))
        n1, n2 = split2(unit * gain[...] + shift[...])
        normed[...] = stack(n1, n1, n2, jnp.zeros((8, n1.shape[1]), bf16))
        d_normed[...] = jnp.zeros_like(d_normed)

    blank = jnp.zeros((8, 128), bf16)
    for g, w, out, bias in ((gq, wq, g_wq, g_bq), (gk, wk, g_wk, g_bk), (gv, wv, g_wv, g_bv)):
        g = g[0]
        g1, g2 = split2(g)
        out[...] = dot(normed[...], stack(g1, g2, g1, blank), TN)
        bias[...] = jnp.sum(g, axis=0, keepdims=True)
        d_normed[...] += three((g1, g2), split2(w[...]), NT)

    @pl.when(step == pl.num_programs(0) - 1)
    def _():
        unit, scale = norm_stats(tall(emb[...]))
        d = d_normed[...]
        g_gain[...] = jnp.sum(d * unit, axis=0, keepdims=True)
        g_shift[...] = jnp.sum(d, axis=0, keepdims=True)
        back = norm_back(d, unit, scale, gain[...])
        for t in range(residual.shape[0]):
            at = slice(t * 128, (t + 1) * 128)
            g_emb[:, at] = (back[:, at] + residual[t])[:VOCAB]


def finish(emb, gain, shift, tables, residual, wq, wk, wv):
    width = emb.shape[1]
    full = lambda *dims: pl.BlockSpec(dims, lambda i: (0,) * len(dims))
    weight = pl.BlockSpec((width, 128), lambda i: (0, i))
    bias = pl.BlockSpec((1, 128), lambda i: (0, i))
    like = jax.ShapeDtypeStruct
    return pl.pallas_call(
        finish_kernel,
        grid=(width // 128,),
        in_specs=[full(VOCAB, width), full(1, width), full(1, width)]
        + [pl.BlockSpec((1, ROWS, 128), lambda i: (i, 0, 0))] * 3
        + [full(width // 128, ROWS, 128)]
        + [weight] * 3,
        out_specs=[weight] * 3 + [bias] * 3 + [full(VOCAB, width), full(1, width), full(1, width)],
        out_shape=[like((width, width), f32)] * 3
        + [like((1, width), f32)] * 3
        + [like((VOCAB, width), f32)]
        + [like((1, width), f32)] * 2,
        scratch_shapes=[pltpu.VMEM((128, width), bf16), pltpu.VMEM((ROWS, width), f32)],
        compiler_params=params(32),
        cost_estimate=cost(5),
        name="finish",
    )(emb, gain, shift, *tables, residual, wq, wk, wv)


def rotated(tq, tk, hot_q, hot, cosq, sinq, cosk, sink):
    q = dot(tq, hot_q)
    k = dot(tk, hot)
    heads = [slice(h * HDIM, (h + 1) * HDIM) for h in range(GROUP)]
    qs = [turn(q[h], cosq, sinq) * (SCALE * LOG2E) for h in heads]
    ks = [turn(k[h], cosk, sink) for h in heads]
    return qs, ks


def shift_rows(shift):
    s1, s2, s3 = split3(shift)
    row = lax.broadcasted_iota(jnp.int32, (HDIM, shift.shape[1]), 0)
    s1, s2, s3 = s1.astype(f32), s2.astype(f32), s3.astype(f32)
    return jnp.where(row == 0, s1, jnp.where(row == 1, s2, jnp.where(row == 2, s3, 0.0))).astype(bf16)


def ones_rows(n):
    return jnp.where(lax.broadcasted_iota(jnp.int32, (HDIM, n), 0) < 3, 1.0, 0.0).astype(bf16)


def forward_kernel(here, tq, tk, tv, hot_q, hot, cosq, sinq, cosk, sink, att, logs, counts):
    span = hot_q.shape[-1]
    whole = hot.shape[-1]
    step = min(256, span)
    qs, ks = rotated(
        tq[...], tk[...], hot_q[0], hot[0], cosq[...], sinq[...], cosk[...], sink[...]
    )
    ids = hot[0, :ROWS, :]
    tail = ones_rows(whole)

    def store(h, c, cnt, total, log):
        cnt = cnt / total
        counts[0, h, :, c : c + step] = cnt
        logs[0, h, :, c : c + step] = log
        c1, c2 = split2(cnt)
        table = tv[h * HDIM : (h + 1) * HDIM, : 3 * ROWS]
        att[0, h * HDIM : (h + 1) * HDIM, c : c + step] = dot(table, stack(c1, c1, c2))

    low = jnp.full((1, step), jnp.inf, f32)
    kept = []
    for h in range(GROUP):
        q, k = qs[h], ks[h]
        longest = jnp.max(jnp.sum(k * k, axis=0, keepdims=True), axis=1, keepdims=True)
        bound = jnp.sqrt(jnp.sum(q * q, axis=0, keepdims=True) * longest)
        q1, q2 = split2(q)
        k1, k2 = split2(k)
        qp = jnp.concatenate([q1, q1, q2, shift_rows(-bound)], axis=0)
        kp = jnp.concatenate([k1, k2, k1, tail], axis=0)
        kept.append((q1, q2, kp))
        for c in range(0, span, step):
            p1, p2 = split2(jnp.exp2(dot(kp, qp[:, c : c + step], TN)))
            cnt = dot(ids, p1) + dot(ids, p2)
            total = jnp.sum(cnt, axis=0, keepdims=True)
            low = jnp.minimum(low, total)
            store(h, c, cnt, total, bound[:, c : c + step] + jnp.log2(total))

    @pl.when(jnp.logical_not(jnp.min(low) > 1e-25))
    def _():
        for h in range(GROUP):
            q1, q2, kp = kept[h]
            qp = jnp.concatenate([q1, q1, q2, jnp.zeros_like(q1)], axis=0)
            for c in range(0, span, step):
                s = dot(kp, qp[:, c : c + step], TN)
                top = jnp.max(s, axis=0, keepdims=True)
                p1, p2 = split2(jnp.exp2(s - top))
                cnt = dot(ids, p1) + dot(ids, p2)
                total = jnp.sum(cnt, axis=0, keepdims=True)
                store(h, c, cnt, total, top + jnp.log2(total))


def backward_kernel(
    here, tq, tk, tv, hot_q, hot, hot3, cosq, sinq, cosk, sink, logs, counts, datt, *refs
):
    grads = refs[-1]
    span = hot_q.shape[-1]
    whole = hot.shape[-1]
    step = min(256, span)

    @pl.when(pl.program_id(1) == 0)
    def _():
        grads[...] = jnp.zeros_like(grads)

    qs, ks = rotated(
        tq[...], tk[...], hot_q[0], hot[0], cosq[...], sinq[...], cosk[...], sink[...]
    )
    tail = ones_rows(whole)
    gqs, gks, gvs = [], [], []
    for h in range(GROUP):
        q1, q2 = split2(qs[h])
        k1, k2 = split2(ks[h])
        qp = jnp.concatenate([q1, q1, q2, shift_rows(-logs[0, h])], axis=0)
        kp = jnp.concatenate([k1, k2, k1, tail], axis=0)
        d1, d2 = split2(datt[0, h * HDIM : (h + 1) * HDIM, :])
        cnt = counts[0, h]
        table = tv[h * HDIM : (h + 1) * HDIM, :]
        e = dot(table[:, : 2 * ROWS], d1, TN)
        e = e[:ROWS] + e[ROWS:] + dot(table[:, :ROWS], d2, TN)
        e = e - jnp.sum(e * cnt, axis=0, keepdims=True)
        e_pack = stack(*split3(e), jnp.zeros((8, span), bf16))
        c1, c2 = split2(cnt)
        both = dot(jnp.concatenate([d1, d2], axis=0), c1, NT)
        gvs.append(both[:HDIM] + both[HDIM:] + dot(d1, c2, NT))
        dqs = []
        dk = None
        for c in range(0, span, step):
            p = jnp.exp2(dot(kp, qp[:, c : c + step], TN))
            ds = p * dot(hot3[0], e_pack[:, c : c + step])
            s1, s2 = split2(ds)
            a = dot(kp[: 2 * HDIM], s1)
            dqs.append(a[:HDIM] + a[HDIM:] + dot(kp[:HDIM], s2))
            b = dot(qp[HDIM : 3 * HDIM, c : c + step], s1, NT)
            b = b[:HDIM] + b[HDIM:] + dot(qp[:HDIM, c : c + step], s2, NT)
            dk = b if dk is None else dk + b
        dq = dqs[0] if len(dqs) == 1 else jnp.concatenate(dqs, axis=1)
        dq = turn_back(dq, cosq[...], sinq[...]) * SCALE
        dk = turn_back(dk, cosk[...], sink[...]) * (1.0 / LOG2E)
        a = dot(jnp.concatenate(split2(dq), axis=0), hot_q[0, :ROWS, :], NT)
        gqs.append(a[:HDIM] + a[HDIM:])
        b = dot(jnp.concatenate(split2(dk), axis=0), hot[0, :ROWS, :], NT)
        gks.append(b[:HDIM] + b[HDIM:])
    for i, gs in enumerate((gqs, gks, gvs)):
        grads[0, i] += jnp.concatenate(gs, axis=0).T


def attention_specs(crops, span, whole, first):
    group = lambda *dims: pl.BlockSpec(dims, lambda g, c, w: (first + g,) + (0,) * (len(dims) - 1))
    rope_q = pl.BlockSpec((HALF, span), lambda g, c, w: (0, w[0]))
    rope_k = pl.BlockSpec((HALF, whole), lambda g, c, w: (0, 0))
    return dict(
        table=group(128, 128),
        hot_q=pl.BlockSpec((1, 128, span), lambda g, c, w: (c, 0, w[0])),
        hot=pl.BlockSpec((1, 128, whole), lambda g, c, w: (c, 0, 0)),
        hot3=pl.BlockSpec((1, whole, 128), lambda g, c, w: (c, 0, 0)),
        rope=[rope_q, rope_q, rope_k, rope_k],
        features=pl.BlockSpec((1, 128, span), lambda g, c, w: (c, first + g, 0)),
        logs=pl.BlockSpec((1, GROUP, 1, span), lambda g, c, w: (c, first + g, 0, 0)),
        counts=pl.BlockSpec((1, GROUP, ROWS, span), lambda g, c, w: (c, first + g, 0, 0)),
    )


def attention_forward(here, tq, tk, tv, hot, cos, sin, span):
    crops, _, whole = hot.shape
    s = attention_specs(crops, span, whole, 0)
    like = jax.ShapeDtypeStruct
    return pl.pallas_call(
        forward_kernel,
        grid_spec=pltpu.PrefetchScalarGridSpec(
            num_scalar_prefetch=1,
            grid=(HEADS // GROUP, crops),
            in_specs=[s["table"]] * 3 + [s["hot_q"], s["hot"]] + s["rope"],
            out_specs=[s["features"], s["logs"], s["counts"]],
        ),
        out_shape=[
            like((crops, HEADS * HDIM, span), f32),
            like((crops, HEADS, 1, span), f32),
            like((crops, HEADS, ROWS, span), f32),
        ],
        compiler_params=params(48),
        cost_estimate=cost(25),
        name="attend",
    )(here, tq, tk, tv, hot, hot, cos, sin, cos, sin)


def attention_backward(here, tq, tk, tv, hot, hot3, cos, sin, logs, counts, datt, first, groups, after):
    crops, _, whole = hot.shape
    span = datt.shape[-1]
    s = attention_specs(crops, span, whole, first)
    return pl.pallas_call(
        backward_kernel,
        grid_spec=pltpu.PrefetchScalarGridSpec(
            num_scalar_prefetch=1,
            grid=(groups, crops),
            in_specs=[s["table"]] * 3
            + [s["hot_q"], s["hot"], s["hot3"]]
            + s["rope"]
            + [s["logs"], s["counts"], s["features"]]
            + [ANY] * len(after),
            out_specs=[pl.BlockSpec((1, 3, ROWS, 128), lambda g, c, w: (g, 0, 0, 0))],
        ),
        out_shape=[jax.ShapeDtypeStruct((groups, 3, ROWS, 128), f32)],
        compiler_params=params(48),
        cost_estimate=cost(10 * groups),
        name="attend_back",
    )(here, tq, tk, tv, hot, hot, hot3, cos, sin, cos, sin, logs, counts, datt, *after)[0]


def middle_kernel(att, wo, bo, hot3, packed, gain, shift, after, normed, weight):
    first = (pl.program_id(0) == 0) & (pl.program_id(1) == 0)

    @pl.when(first)
    def _():
        weight[0], weight[1] = split2(wo[...])

    w = (weight[0], weight[1])
    x = dot(hot3[0], packed[...]) + three(split2(att[0]), w, TN) + bo[...]
    after[...] = x
    normed[...] = norm_stats(x)[0] * gain[...] + shift[...]


def middle(here, att, wo, bo, hot3, packed, gain, shift):
    crops, width, span = att.shape
    block = min(256, span)
    steps = span // block
    full = lambda *dims: pl.BlockSpec(dims, lambda c, i, w: (0,) * len(dims))
    rows = pl.BlockSpec((block, width), lambda c, i, w: (c * steps + i, 0))
    out = jax.ShapeDtypeStruct((crops * span, width), f32)
    return pl.pallas_call(
        lambda w, *refs: middle_kernel(*refs),
        grid_spec=pltpu.PrefetchScalarGridSpec(
            num_scalar_prefetch=1,
            grid=(crops, steps),
            in_specs=[
                pl.BlockSpec((1, width, block), lambda c, i, w: (c, 0, i)),
                full(width, width),
                full(1, width),
                pl.BlockSpec((1, block, 128), lambda c, i, w: (c, w[0] * steps + i, 0)),
                full(128, width),
                full(1, width),
                full(1, width),
            ],
            out_specs=[rows, rows],
            scratch_shapes=[pltpu.VMEM((2, width, width), bf16)],
        ),
        out_shape=[out, out],
        compiler_params=params(32),
        cost_estimate=cost(5),
        name="middle",
    )(here, att, wo, bo, hot3, packed, gain, shift)


def middle_back_kernel(
    after, d_own, d_swapped, grad, gain, att, wo, hot, bias_a, bias_b, bias_c, where, datt, keep, send,
    weight, product, sums, flat,
):
    crops, steps = pl.num_programs(0), pl.num_programs(1)
    step = pl.program_id(0) * steps + pl.program_id(1)
    width = wo.shape[0]
    tiles = width // 128

    @pl.when(step == 0)
    def _():
        weight[0], weight[1] = split2(wo[...])
        product[...] = jnp.zeros_like(product)
        sums[...] = jnp.zeros_like(sums)

    g = grad[...]
    unit, scale = norm_stats(after[...])
    d_normed = d_own[...] + d_swapped[...]
    d = g + norm_back(d_normed, unit, scale, gain[...])
    pair = split2(d)
    datt[0] = three((weight[0], weight[1]), pair, NT)
    product[...] += three(split2(att[0]), pair)
    ids = hot[0, :ROWS, :]
    sums[:ROWS] += dot(ids, pair[0]) + dot(ids, pair[1])
    vectors = [jnp.sum(v, axis=0, keepdims=True) for v in (d, d_normed * unit, d_normed, g)]
    sums[ROWS:] += jnp.concatenate(vectors + [jnp.zeros((4, width), f32)], axis=0)

    @pl.when(step == crops * steps - 1)
    def _():
        flat[...] = jnp.zeros_like(flat)
        for t in range(tiles):
            at = slice(t * 128, (t + 1) * 128)
            flat[t * width : (t + 1) * width, :] = product[:, at]
            base = tiles * width + t * (ROWS + 8)
            flat[base : base + ROWS + 8, :] = sums[:, at]
        base = tiles * (width + ROWS + 8)
        biases = jnp.concatenate([bias_a[...], bias_b[...], bias_c[...]], axis=1)
        count = biases.shape[1] // 128
        core = where[0]
        for t in range(count):
            flat[pl.ds(base + core * count + t, 1), :] = biases[:, t * 128 : (t + 1) * 128]
        half = keep.shape[0]
        keep[...] = flat[pl.ds(pl.multiple_of(core * half, 8), half), :]
        send[...] = flat[pl.ds(pl.multiple_of((1 - core) * half, 8), half), :]


def middle_back(where, after, d_own, d_swapped, grad, gain, att, wo, hot, biases, unit_rows, deps):
    crops, width, span = att.shape
    block = min(256, span)
    steps = span // block
    hidden = 2 * sum(b.shape[1] for b in biases)
    rows = width // 128 * (width + ROWS + 8) + hidden // 128
    rows += -rows % unit_rows
    full = lambda *dims: pl.BlockSpec(dims, lambda c, i, w: (0,) * len(dims))
    token = pl.BlockSpec((block, width), lambda c, i, w: (c * steps + i, 0))
    features = pl.BlockSpec((1, width, block), lambda c, i, w: (c, 0, i))
    like = jax.ShapeDtypeStruct
    count = len(deps)

    def kernel(w, *refs):
        ins = refs[: 11]
        outs = refs[11 + count :]
        middle_back_kernel(*ins, w, *outs)

    return pl.pallas_call(
        kernel,
        grid_spec=pltpu.PrefetchScalarGridSpec(
            num_scalar_prefetch=1,
            grid=(crops, steps),
            in_specs=[token] * 4
            + [
                full(1, width),
                features,
                full(width, width),
                pl.BlockSpec((1, 128, block), lambda c, i, w: (c, 0, w[1] * steps + i)),
            ]
            + [full(*b.shape) for b in biases]
            + [ANY] * count,
            out_specs=[features, full(rows // 2, 128), full(rows // 2, 128)],
            scratch_shapes=[
                pltpu.VMEM((2, width, width), bf16),
                pltpu.VMEM((width, width), f32),
                pltpu.VMEM((ROWS + 8, width), f32),
                pltpu.VMEM((rows, 128), f32),
            ],
        ),
        out_shape=[like((crops, width, span), f32)] + [like((rows // 2, 128), f32)] * 2,
        compiler_params=params(40),
        cost_estimate=cost(8),
        name="middle_back",
    )(where, after, d_own, d_swapped, grad, gain, att, wo, hot, *biases, *deps)


BLOCK = 256


def three_wide(a, b, dims=NN):
    (i,), (j,) = dims[0]
    return dot(
        jnp.concatenate([a[0], a[0], a[1]], axis=i), jnp.concatenate([b[0], b[1], b[0]], axis=j), dims
    )


def ff_kernel(fresh, where, *refs):
    if fresh:
        sources = refs[:4]
        up, up_bias, down = refs[4:7]
        keep, send, bias, h1, h2, p1, p2, nh, nl, gh, gl = refs[-11:]

        @pl.when(pl.program_id(0) == 0)
        def _():
            half = nh.shape[0] // 2
            for i, source in enumerate(sources):
                heads, tails = ((nh, nl), (gh, gl))[i // 2]
                at = slice((i % 2) * half, (i % 2 + 1) * half)
                heads[at], tails[at] = split2(source[...])

    else:
        nh, nl, gh, gl, up, up_bias, down = refs[:7]
        keep, send, bias, h1, h2, p1, p2 = refs[-7:]
    step = pl.program_id(0)
    count = pl.num_programs(0)
    normed, grad = (nh[...], nl[...]), (gh[...], gl[...])
    up2, down2 = split2(up[...]), split2(down[...])
    u = three_wide(normed, up2) + up_bias[...]
    cdf = 0.5 * (1.0 + lax.erf(u * (0.5**0.5)))
    density = jnp.exp(-0.5 * u * u) * (1.0 / math.sqrt(2.0 * math.pi))
    ff = split2(u * cdf)
    d_pre = three_wide(grad, down2, NT) * (cdf + u * density)
    bias[...] = jnp.sum(d_pre, axis=0, keepdims=True)
    d_pre = split2(d_pre)
    h1[...], h2[...] = ff
    p1[...], p2[...] = d_pre
    g_down = three_wide(ff, grad, TN)
    g_up = three_wide(d_pre, normed, TN).T
    width = g_down.shape[1]

    def put(down_ref, up_ref):
        for t in range(width // 128):
            at = pl.multiple_of((t * count + step) * BLOCK, BLOCK)
            down_ref[pl.ds(at, BLOCK), :] = g_down[:, t * 128 : (t + 1) * 128]
        for t in range(BLOCK // 128):
            at = pl.multiple_of((step * (BLOCK // 128) + t) * width, 128)
            up_ref[pl.ds(at, width), :] = g_up[:, t * 128 : (t + 1) * 128]

    @pl.when(where[1] == 0)
    def _():
        put(keep, send)

    @pl.when(where[1] == 1)
    def _():
        put(send, keep)


def ff_chunk(where, sources, up, up_bias, down, first, blocks, buffers, deps):
    fresh = not buffers
    width = sources[0].shape[1]
    tokens = sources[0].shape[0] * (2 if fresh else 1)
    hidden = up.shape[1]
    half = hidden // 2 // BLOCK
    slab = blocks * BLOCK * width // 128
    full = lambda *dims: pl.BlockSpec(dims, lambda j, w: (0,) * len(dims))
    column = pl.BlockSpec((tokens, BLOCK), lambda j, w: (0, first + j))
    like = jax.ShapeDtypeStruct
    pair = [like((tokens, width), bf16)] * 4 if fresh else []
    return pl.pallas_call(
        lambda *refs: ff_kernel(fresh, *refs),
        grid_spec=pltpu.PrefetchScalarGridSpec(
            num_scalar_prefetch=1,
            grid=(blocks,),
            in_specs=[full(*s.shape) for s in sources]
            + [
                pl.BlockSpec((width, BLOCK), lambda j, w: (0, w[0] * half + first + j)),
                pl.BlockSpec((1, BLOCK), lambda j, w: (0, w[0] * half + first + j)),
                pl.BlockSpec((BLOCK, width), lambda j, w: (w[0] * half + first + j, 0)),
            ]
            + [ANY] * (len(buffers) + len(deps)),
            out_specs=[full(slab, 128), full(slab, 128), pl.BlockSpec((1, BLOCK), lambda j, w: (0, j))]
            + [column] * 4
            + [full(tokens, width)] * len(pair),
        ),
        out_shape=[like((slab, 128), f32), like((slab, 128), f32), like((1, blocks * BLOCK), f32)]
        + [like((tokens, hidden // 2), bf16)] * 4
        + pair,
        input_output_aliases={8 + i: 3 + i for i in range(len(buffers))},
        compiler_params=params(58),
        cost_estimate=cost(5 * blocks),
        name="feed",
    )(where, *sources, up, up_bias, down, *buffers, *deps)


def back_product_kernel(dims, where, a1, a2, w, *refs):
    own, other = refs[-2:]
    step = pl.program_id(0)
    out = three_wide((a1[...], a2[...]), split2(w[...]), dims)
    half = own.shape[0]

    @pl.when(step == 0)
    def _():
        own[...] = out[:half]
        other[...] = out[half:]

    @pl.when(step > 0)
    def _():
        own[...] += out[:half]
        other[...] += out[half:]


def back_product(where, a, weight, dims, deps):
    tokens, units = a[0].shape
    steps = units // BLOCK
    up_like = dims is NT
    width = weight.shape[0 if up_like else 1]
    out = jax.ShapeDtypeStruct((tokens // 2, width), f32)
    spec = (
        pl.BlockSpec((width, BLOCK), lambda j, w: (0, w[0] * steps + j))
        if up_like
        else pl.BlockSpec((BLOCK, width), lambda j, w: (w[0] * steps + j, 0))
    )
    return pl.pallas_call(
        lambda *refs: back_product_kernel(dims, *refs),
        grid_spec=pltpu.PrefetchScalarGridSpec(
            num_scalar_prefetch=1,
            grid=(steps,),
            in_specs=[pl.BlockSpec((tokens, BLOCK), lambda j, w: (0, j))] * 2 + [spec] + [ANY] * len(deps),
            out_specs=[pl.BlockSpec((tokens // 2, width), lambda j, w: (0, 0))] * 2,
        ),
        out_shape=[out, out],
        compiler_params=params(48),
        cost_estimate=cost(8),
        name="feed_back" if up_like else "feed_out",
    )(where, *a, weight, *deps)


def bits_of(axis):
    size = lax.axis_size(axis)
    return [(axis, 1 << i) for i in range(size.bit_length() - 1)]


def swap(x, stage):
    axis, bit = stage
    return lax.ppermute(x, axis, [(i, i ^ bit) for i in range(lax.axis_size(axis))])


def side(stage):
    axis, bit = stage
    return ((lax.axis_index(axis) // bit) % 2).astype(jnp.int32)


def add_split_kernel(where, k_here, r_here, k_away, r_away, *refs):
    keep, send = refs[-2:]
    keep[...] = k_here[...] + r_here[...]
    send[...] = k_away[...] + r_away[...]


def add_split(kept, received, stage, deps):
    rows, lanes = kept.shape
    half = rows // 2
    me = side(stage)
    if half % 8:
        total = kept + received
        return (
            lax.dynamic_slice_in_dim(total, me * half, half, 0),
            lax.dynamic_slice_in_dim(total, (1 - me) * half, half, 0),
        )
    steps = 2 if half % 16 == 0 and half >= 512 else 1
    block = (half // steps, lanes)
    here = pl.BlockSpec(block, lambda i, w: (w[0] * steps + i, 0))
    away = pl.BlockSpec(block, lambda i, w: ((1 - w[0]) * steps + i, 0))
    plain = pl.BlockSpec(block, lambda i, w: (i, 0))
    out = jax.ShapeDtypeStruct((half, lanes), f32)
    return pl.pallas_call(
        add_split_kernel,
        grid_spec=pltpu.PrefetchScalarGridSpec(
            num_scalar_prefetch=1,
            grid=(steps,),
            in_specs=[here, here, away, away] + [ANY] * len(deps),
            out_specs=[plain, plain],
        ),
        out_shape=[out, out],
        compiler_params=params(16),
        cost_estimate=cost(1),
        name="add_split",
    )(me.reshape(1), kept, received, kept, received, *deps)


class Sum:
    def __init__(self, keep, send, stages):
        self.keep, self.stages, self.at = keep, stages, 0
        self.coming = swap(send, stages[0])

    def step(self, deps=()):
        self.at += 1
        if self.at == len(self.stages):
            self.keep = self.keep + self.coming
        else:
            self.keep, send = add_split(self.keep, self.coming, self.stages[self.at], deps)
            self.coming = swap(send, self.stages[self.at])
        return self.keep


def join(x, other, stage):
    return jnp.where(
        side(stage) == 0,
        jnp.concatenate([x, other], axis=0),
        jnp.concatenate([other, x], axis=0),
    )


class Spread:
    def __init__(self, x, stages):
        self.x, self.stages = x, list(reversed(stages))
        self.coming = swap(x, self.stages[0])
        self.at = 0

    def step(self):
        self.x = join(self.x, self.coming, self.stages[self.at])
        self.at += 1
        self.coming = swap(self.x, self.stages[self.at])

    def run(self):
        while self.at < len(self.stages) - 1:
            self.step()
        return self.x, self.coming

    def whole(self):
        x, other = self.run()
        return join(x, other, self.stages[-1])


def place_kernel(where, own_d, own_u, other_d, other_u, *refs):
    down, up = refs[-2:]

    def put(d, u):
        for t in range(d.shape[0]):
            down[:, t * 128 : (t + 1) * 128] = d[t]
        for t in range(u.shape[0]):
            up[:, t * 128 : (t + 1) * 128] = u[t]

    @pl.when(where[1] == 0)
    def _():
        put(own_d, other_u)

    @pl.when(where[1] == 1)
    def _():
        put(other_d, own_u)


def place(where, own, other, first, blocks, width, hidden, buffers):
    half = hidden // 2 // BLOCK
    tiles = width // 128
    at = lambda r, w: w[0] * half + first + r
    used = lambda side, r, w: jnp.where(w[1] == side, r, 0)
    down_block = lambda side: pl.BlockSpec((tiles, BLOCK, 128), lambda r, w: (0, used(side, r, w), 0))
    up_block = lambda side: pl.BlockSpec((BLOCK // 128, width, 128), lambda r, w: (used(side, r, w), 0, 0))
    views = []
    for x in (own, other):
        views += [x.reshape(-1, blocks * BLOCK, 128), x.reshape(-1, width, 128)]
    return pl.pallas_call(
        place_kernel,
        grid_spec=pltpu.PrefetchScalarGridSpec(
            num_scalar_prefetch=1,
            grid=(blocks,),
            in_specs=[down_block(0), up_block(1), down_block(1), up_block(0)] + [ANY] * len(buffers),
            out_specs=[
                pl.BlockSpec((BLOCK, width), lambda r, w: (at(r, w), 0)),
                pl.BlockSpec((width, BLOCK), lambda r, w: (0, at(r, w))),
            ],
        ),
        out_shape=[
            jax.ShapeDtypeStruct((hidden, width), f32),
            jax.ShapeDtypeStruct((width, hidden), f32),
        ],
        input_output_aliases={5 + i: i for i in range(len(buffers))},
        compiler_params=params(32),
        cost_estimate=cost(2),
        name="place",
    )(where, *views, *buffers)


def local(
    token_ids,
    embedding,
    first_gain,
    first_shift,
    query_weight,
    query_bias,
    key_weight,
    key_bias,
    value_weight,
    value_bias,
    out_weight,
    out_bias,
    second_gain,
    second_shift,
    up_weight,
    up_bias,
    down_weight,
    down_bias,
    cotangent,
    crop_cluster,
    cluster_weight,
):
    crops, span = token_ids.shape
    width = embedding.shape[1]
    units = up_weight.shape[1]
    ring = lax.axis_size("seq")
    whole = span * ring
    seq_bits, crop_bits = bits_of("seq"), bits_of("crop")
    core_stage, across, along = crop_bits[0], crop_bits[1:2], crop_bits[2:]
    part_a = across + seq_bits + along
    part_b = seq_bits + along + across
    part_c = along + across + seq_bits
    part_d = [core_stage] + part_c
    core = side(core_stage)
    here = lax.axis_index("seq").astype(jnp.int32)
    row = lambda v: v.reshape(1, -1)

    if ring == 2:
        other = swap(token_ids, ("seq", 1))
        ids = jnp.where(
            here == 0,
            jnp.concatenate([token_ids, other], axis=1),
            jnp.concatenate([other, token_ids], axis=1),
        )
    else:
        ids = lax.all_gather(token_ids, "seq", axis=1, tiled=True)

    matches = crop_cluster[:, None] == jnp.arange(cluster_weight.shape[0], dtype=jnp.int32)[None, :]
    crop_weight = jnp.sum(jnp.where(matches, cluster_weight[None, :], 0.0), axis=1)
    grad_out = (cotangent * crop_weight[:, None, None]).reshape(-1, width)
    grad_other = swap(grad_out, core_stage)

    frequency = (10000.0 ** (-2.0 * np.arange(HALF) / HDIM)).astype(np.float32)
    angles = (frequency[:, None] * np.arange(whole, dtype=np.float32)[None, :]).astype(np.float64)
    cos, sin = jnp.asarray(np.cos(angles), f32), jnp.asarray(np.sin(angles), f32)

    tq, tk, tv, hot, hot3, packed = prepare(
        ids, embedding, row(first_gain), row(first_shift), query_weight, row(query_bias), key_weight,
        row(key_bias), value_weight, row(value_bias),
    )
    att, logs, counts = attention_forward(here.reshape(1), tq, tk, tv, hot, cos, sin, span)
    after_attn, normed = middle(
        here.reshape(1), att, out_weight, row(out_bias), hot3, packed, row(second_gain), row(second_shift)
    )
    normed_other = swap(normed, core_stage)

    sums, biases, first = [], [], 0
    sources, buffers, deps = [normed, normed_other, grad_out, grad_other], [], []
    blocks = units // 2 // BLOCK
    third = 2 * (blocks // 5)
    spans = []
    for count, stages in ((third, part_a), (third, part_b), (blocks - 2 * third, part_c)):
        where = jnp.stack([core, side(stages[0])])
        keep, send, bias, *buffers = ff_chunk(
            where, sources, up_weight, row(up_bias), down_weight, first, count, buffers, deps
        )
        if len(buffers) > 4:
            sources, buffers = buffers[4:], buffers[:4]
        sums.append(Sum(keep, send, stages))
        spans.append((first, count, stages))
        biases.append(bias)
        first += count

    h1, h2, p1, p2 = buffers
    where = core.reshape(1)
    d_own, d_other = back_product(where, (p1, p2), up_weight, NT, [])
    d_swapped = swap(d_other, core_stage)
    o_own, o_other = back_product(where, (h1, h2), down_weight, NN, [d_own])
    o_swapped = swap(o_other, core_stage)

    devices = lax.axis_size("seq") * lax.axis_size("crop")
    d_att, keep, send = middle_back(
        jnp.stack([core, here]), after_attn, d_own, d_swapped, grad_out, row(second_gain), att, out_weight, hot,
        biases, 8 * devices, [o_own],
    )
    sums.append(Sum(keep, send, part_d))

    tables, deps = [], [d_att]
    groups = HEADS // GROUP
    for first, count in ((0, 2), (2, 1), (3, 1), (4, 1)):
        kept = [s.step(deps) for s in sums if s.at < len(s.stages)]
        deps = kept + tables[-1:]
        tables.append(
            attention_backward(
                here.reshape(1), tq, tk, tv, hot, hot3, cos, sin, logs, counts, d_att, first, count, deps
            )
        )
        deps = tables[-1:]
    while any(s.at < len(s.stages) for s in sums):
        for s in sums:
            if s.at < len(s.stages):
                s.step(deps)

    block_out = (after_attn + o_own + o_swapped + down_bias).reshape(cotangent.shape)

    flat = jnp.concatenate(tables, axis=0).reshape(-1, 128)
    rows = flat.shape[0]
    flat = jnp.pad(flat, ((0, -rows % (8 * devices)), (0, 0)))
    half = flat.shape[0] // 2
    small = Sum(
        lax.dynamic_slice_in_dim(flat, core * half, half, 0),
        lax.dynamic_slice_in_dim(flat, (1 - core) * half, half, 0),
        part_d,
    )
    while small.at < len(part_d):
        small.step()
    flat = Spread(small.keep, part_d).whole()[:rows].reshape(groups, 3, ROWS, 128)

    outs = []
    for total, (first, count, stages) in zip(sums, spans):
        own, other = Spread(total.keep, stages).run()
        first_side = side(stages[0])
        for k, (x, y) in ((core, (own, other)), (1 - core, (swap(own, core_stage), swap(other, core_stage)))):
            outs = place(jnp.stack([k, first_side]), x, y, first, count, width, units, outs)
    g_dw, g_uw = outs

    rest = Spread(sums[3].keep, part_d).whole()
    tiles = width // 128
    g_ow = jnp.transpose(rest[: tiles * width].reshape(tiles, width, 128), (1, 0, 2)).reshape(width, width)
    base = tiles * (width + ROWS + 8)
    vectors = rest[tiles * width : base].reshape(tiles, ROWS + 8, 128)
    residual = vectors[:, :ROWS]
    g_ob, g_sg, g_ss, g_db = (vectors[:, ROWS + i].reshape(width) for i in range(4))
    g_ub = rest[base : base + units // 128].reshape(units)

    g_wq, g_wk, g_wv, g_bq, g_bk, g_bv, g_emb, g_gain, g_shift = finish(
        embedding, row(first_gain), row(first_shift), [flat[:, i] for i in range(3)], residual,
        query_weight, key_weight, value_weight,
    )
    flat_row = lambda v: v.reshape(-1)
    return (
        block_out, g_emb, flat_row(g_gain), flat_row(g_shift), g_wq, flat_row(g_bq), g_wk, flat_row(g_bk), g_wv,
        flat_row(g_bv), g_ow, g_ob, g_sg, g_ss, g_uw, g_ub, g_dw, g_db,
    )


def solution(mesh):
    in_specs = (
        (P("crop", "seq"),) + (P(),) * 17 + (P("crop", "seq", None), P("crop"), P())
    )
    out_specs = (P("crop", "seq", None),) + (P(),) * 17
    return jax.shard_map(local, mesh=mesh, in_specs=in_specs, out_specs=out_specs, check_vma=False)
```

```python
import math
import jax
import jax.numpy as jnp
import numpy as np
from jax import lax
from jax.experimental import pallas as pl
from jax.experimental.pallas import tpu as pltpu
from jax.sharding import PartitionSpec as P

HEADS = 20
HDIM = 32
HALF = 16
VOCAB = 33
ROWS = 40
GROUP = 4
f32 = jnp.float32
bf16 = jnp.bfloat16
epsilon = 1e-05
LOG2E = 1.0 / math.log(2.0)
SCALE = HDIM**-0.5

NN = (((1,), (0,)), ((), ()))
NT = (((1,), (1,)), ((), ()))
TN = (((0,), (0,)), ((), ()))
ANY = pl.BlockSpec(memory_space=pl.ANY)


def params(mib):
    return pltpu.CompilerParams(vmem_limit_bytes=mib << 20)


def cost(flops=1000000000):
    return pl.CostEstimate(flops=flops, bytes_accessed=0, transcendentals=0)


STEP = 1000000000


def dot(a, b, dims=NN):
    return lax.dot_general(a, b, dims, preferred_element_type=f32)


def split2(x):
    head = x.astype(bf16)
    return head, (x - head.astype(f32)).astype(bf16)


def split3(x):
    head = x.astype(bf16)
    x = x - head.astype(f32)
    mid = x.astype(bf16)
    return head, mid, (x - mid.astype(f32)).astype(bf16)


def three(a, b, dims=NN):
    return dot(a[0], b[0], dims) + dot(a[0], b[1], dims) + dot(a[1], b[0], dims)


def turn(u, cos, sin):
    a, b = u[:HALF], u[HALF:]
    return jnp.concatenate([a * cos - b * sin, b * cos + a * sin], axis=0)


def turn_back(u, cos, sin):
    a, b = u[:HALF], u[HALF:]
    return jnp.concatenate([a * cos + b * sin, b * cos - a * sin], axis=0)


def stack(*rows):
    return jnp.concatenate([r.astype(f32) for r in rows], axis=0).astype(bf16)


def norm_stats(x):
    centred = x - jnp.mean(x, axis=-1, keepdims=True)
    scale = lax.rsqrt(jnp.mean(centred * centred, axis=-1, keepdims=True) + epsilon)
    return centred * scale, scale


def norm_back(d_normed, unit, scale, gain):
    d = d_normed * gain
    d = d - jnp.mean(d, axis=-1, keepdims=True) - unit * jnp.mean(d * unit, axis=-1, keepdims=True)
    return d * scale


def tall(emb):
    return jnp.concatenate([emb, jnp.zeros((ROWS - VOCAB, emb.shape[1]), f32)], axis=0)


def line(v):
    return v[...].reshape(1, -1)


def rows_kernel(emb, gain, shift, wq, bq, wk, bk, wv, bv, tq, tk, tv, packed, normed):
    width = emb.shape[1]
    step = pl.program_id(0)

    @pl.when(step == 0)
    def _():
        rows = tall(emb[...])
        unit, _ = norm_stats(rows)
        normed[...] = stack(*split3(unit * line(gain) + line(shift)), jnp.zeros((8, width), bf16))
        packed[...] = stack(*split3(rows), jnp.zeros((8, width), bf16))

    full = normed[...]
    real = lax.broadcasted_iota(jnp.int32, (ROWS, 128), 0) < VOCAB

    def table(w, b):
        w1, w2, w3 = split3(w[...])
        by1 = dot(full, w1)
        by2 = dot(full[: 2 * ROWS], w2)
        t = by1[:ROWS] + (
            (by1[ROWS : 2 * ROWS] + by2[:ROWS])
            + (by1[2 * ROWS : 3 * ROWS] + by2[ROWS:] + dot(full[:ROWS], w3))
        )
        bias = b[pl.ds(pl.multiple_of(step * 128, 128), 128)].reshape(1, 128)
        return jnp.where(real, t + bias, 0.0)

    def lay(a, b, c):
        blank = jnp.zeros((8, 128), f32)
        return jnp.concatenate([a.astype(f32), b.astype(f32), c.astype(f32), blank], axis=0).T.astype(bf16)

    tq[...] = lay(*split3(table(wq, bq)))
    tk[...] = lay(*split3(table(wk, bk)))
    v1, v2 = split2(table(wv, bv))
    tv[...] = lay(v1, v2, v1)


def project_rows(emb, gain, shift, wq, bq, wk, bk, wv, bv):
    width = emb.shape[1]
    full = lambda *dims: pl.BlockSpec(dims, lambda i: (0,) * len(dims))
    weight = pl.BlockSpec((width, 128), lambda i: (0, i))
    table = pl.BlockSpec((128, 128), lambda i: (i, 0))
    like = jax.ShapeDtypeStruct
    return pl.pallas_call(
        rows_kernel,
        grid=(width // 128,),
        in_specs=[full(VOCAB, width), full(width), full(width)] + [weight, full(width)] * 3,
        out_specs=[table] * 3 + [full(128, width)],
        out_shape=[like((width, 128), bf16)] * 3 + [like((128, width), bf16)],
        scratch_shapes=[pltpu.VMEM((128, width), bf16)],
        compiler_params=params(60),
        cost_estimate=cost(),
        name="rows",
    )(emb, gain, shift, wq, bq, wk, bk, wv, bv)


def spots_kernel(count, where, *refs):
    ids, (hot, hot3) = refs[:count], refs[-2:]
    crops, span = ids[0].shape
    spot = lax.broadcasted_iota(jnp.int32, (128, span), 0)
    code = jnp.where(
        spot < ROWS, spot, jnp.where(spot < 2 * ROWS, spot - ROWS, jnp.where(spot < 3 * ROWS, spot - 2 * ROWS, -1))
    )
    for n in range(count):
        at = 0 if count == 1 else pl.multiple_of((where[1] if n == 0 else 1 - where[1]) * span, span)
        for c in range(crops):
            spots = jnp.where(ids[n][c : c + 1, :] == code, 1.0, 0.0)
            hot[c, :, pl.ds(at, span)] = spots.astype(bf16)
            hot3[c, pl.ds(at, span), :] = spots.T.astype(bf16)


def spots(sides, ids, whole, deps):
    crops = ids[0].shape[0]
    full = lambda *dims: pl.BlockSpec(dims, lambda i, w: (0,) * len(dims))
    count = len(ids)
    like = jax.ShapeDtypeStruct
    return pl.pallas_call(
        lambda *refs: spots_kernel(count, *refs),
        grid_spec=pltpu.PrefetchScalarGridSpec(
            num_scalar_prefetch=1,
            grid=(1,),
            in_specs=[full(*i.shape) for i in ids] + [ANY] * len(deps),
            out_specs=[full(crops, 128, whole), full(crops, whole, 128)],
        ),
        out_shape=[like((crops, 128, whole), bf16), like((crops, whole, 128), bf16)],
        compiler_params=params(32),
        cost_estimate=cost(),
        name="spots",
    )(sides.array, *ids, *deps)


def finish_kernel(
    emb, gain, shift, table, rest, wq, wk, wv, g_wq, g_wk, g_wv, g_ow, g_bq, g_bk, g_bv, g_emb, g_gain, g_shift, g_ob,
    g_sg, g_ss, g_db, g_ub, normed, d_normed,
):
    step = pl.program_id(0)
    width = emb.shape[1]
    tiles = width // 128

    @pl.when(step == 0)
    def _():
        unit, _ = norm_stats(tall(emb[...]))
        n1, n2 = split2(unit * line(gain) + line(shift))
        normed[...] = stack(n1, n1, n2, jnp.zeros((8, n1.shape[1]), bf16))
        d_normed[...] = jnp.zeros_like(d_normed)

    blank = jnp.zeros((8, 128), bf16)
    at = pl.ds(pl.multiple_of(step * 128, 128), 128)
    for i, (w, out, bias) in enumerate(((wq, g_wq, g_bq), (wk, g_wk, g_bk), (wv, g_wv, g_bv))):
        g = table[i * ROWS : (i + 1) * ROWS, :]
        g1, g2 = split2(g)
        out[...] = dot(normed[...], stack(g1, g2, g1, blank), TN)
        bias[at] = jnp.sum(g, axis=0)
        d_normed[...] += three((g1, g2), split2(w[...]), NT)
    g_ow[...] = rest[pl.ds(pl.multiple_of(step * width, 128), width), :]

    @pl.when(step == pl.num_programs(0) - 1)
    def _():
        unit, scale = norm_stats(tall(emb[...]))
        d = d_normed[...]
        g_gain[...] = jnp.sum(d * unit, axis=0)
        g_shift[...] = jnp.sum(d, axis=0)
        back = norm_back(d, unit, scale, line(gain))
        for t in range(tiles):
            at = slice(t * 128, (t + 1) * 128)
            base = tiles * width + t * (ROWS + 8)
            g_emb[:, at] = (back[:, at] + rest[base : base + ROWS, :])[:VOCAB]
            for i, out in enumerate((g_ob, g_sg, g_ss, g_db)):
                out[at] = rest[base + ROWS + i, :]
        base = tiles * (width + ROWS + 8)
        for t in range(g_ub.shape[0] // 128):
            g_ub[t * 128 : (t + 1) * 128] = rest[base + t, :]


def finish(emb, gain, shift, table, rest, wq, wk, wv, hidden, chain):
    width = emb.shape[1]
    full = lambda *dims: pl.BlockSpec(dims, lambda i: (0,) * len(dims))
    weight = pl.BlockSpec((width, 128), lambda i: (0, i))
    like = jax.ShapeDtypeStruct
    deps = chain.deps()
    vector, square = like((width,), f32), like((width, width), f32)

    def kernel(*refs):
        finish_kernel(*refs[:8], *refs[8 + len(deps) :])

    out = pl.pallas_call(
        kernel,
        grid=(width // 128,),
        in_specs=[full(VOCAB, width), full(width), full(width)]
        + [pl.BlockSpec((3 * ROWS, 128), lambda i: (i, 0)), full(*rest.shape)]
        + [weight] * 3
        + [ANY] * len(deps),
        out_specs=[weight] * 4 + [full(width)] * 3 + [full(VOCAB, width)] + [full(width)] * 6 + [full(hidden)],
        out_shape=[square] * 4 + [vector] * 3 + [like((VOCAB, width), f32)] + [vector] * 6 + [like((hidden,), f32)],
        scratch_shapes=[pltpu.VMEM((128, width), bf16), pltpu.VMEM((ROWS, width), f32)],
        compiler_params=params(32),
        cost_estimate=cost(),
        name="finish",
    )(emb, gain, shift, table, rest, wq, wk, wv, *deps)
    chain.set(out[0])
    return out


def pack_kernel(where, *refs):
    keep, send, flat = refs[-3:]
    flat[...] = jnp.zeros_like(flat)
    at = 0
    for table in refs[:-3]:
        for g in range(table.shape[0]):
            for i in range(3):
                flat[at : at + ROWS, :] = table[g, i]
                at += ROWS
    half = keep.shape[0]
    keep[...] = flat[pl.ds(pl.multiple_of(where[0] * half, 8), half), :]
    send[...] = flat[pl.ds(pl.multiple_of((1 - where[0]) * half, 8), half), :]


def pack_tables(sides, tables, unit_rows, chain):
    rows = 3 * ROWS * sum(t.shape[0] for t in tables)
    rows += -rows % unit_rows
    full = lambda *dims: pl.BlockSpec(dims, lambda i, w: (0,) * len(dims))
    half = jax.ShapeDtypeStruct((rows // 2, 128), f32)
    out = pl.pallas_call(
        pack_kernel,
        grid_spec=pltpu.PrefetchScalarGridSpec(
            num_scalar_prefetch=1,
            grid=(1,),
            in_specs=[full(*t.shape) for t in tables],
            out_specs=[full(*half.shape)] * 2,
            scratch_shapes=[pltpu.VMEM((rows, 128), f32)],
        ),
        out_shape=[half, half],
        compiler_params=params(16),
        cost_estimate=cost(STEP),
        name="pack",
    )(sides.array, *tables)
    chain.set(out[0])
    return out


def rotated(tq, tk, hot_q, hot, cosq, sinq, cosk, sink):
    q = dot(tq, hot_q)
    k = dot(tk, hot)
    heads = [slice(h * HDIM, (h + 1) * HDIM) for h in range(GROUP)]
    qs = [turn(q[h], cosq, sinq) * (SCALE * LOG2E) for h in heads]
    ks = [turn(k[h], cosk, sink) for h in heads]
    return qs, ks


def shift_rows(shift):
    s1, s2, s3 = split3(shift)
    row = lax.broadcasted_iota(jnp.int32, (HDIM, shift.shape[1]), 0)
    s1, s2, s3 = s1.astype(f32), s2.astype(f32), s3.astype(f32)
    return jnp.where(row == 0, s1, jnp.where(row == 1, s2, jnp.where(row == 2, s3, 0.0))).astype(bf16)


def ones_rows(n):
    return jnp.where(lax.broadcasted_iota(jnp.int32, (HDIM, n), 0) < 3, 1.0, 0.0).astype(bf16)


def forward_kernel(
    here, tq, tk, tv, hot_q, hot, cosq, sinq, cosk, sink, att, logs, counts, q_packs, k_packs, shifts
):
    span = hot_q.shape[-1]
    whole = hot.shape[-1]
    step = min(256, span)
    ids = hot[0, :ROWS, :]
    heads = range(GROUP)
    blocks = [(h, slice(c, c + step)) for h in heads for c in range(0, span, step)]

    qs, ks = rotated(
        tq[...], tk[...], hot_q[0], hot[0], cosq[...], sinq[...], cosk[...], sink[...]
    )
    tail = ones_rows(whole)
    for h in heads:
        q, k = qs[h], ks[h]
        longest = jnp.max(jnp.sum(k * k, axis=0, keepdims=True), axis=1, keepdims=True)
        bound = jnp.sqrt(jnp.sum(q * q, axis=0, keepdims=True) * longest)
        shifts[h] = bound
        q1, q2 = split2(q)
        k1, k2 = split2(k)
        q_packs[h] = jnp.concatenate([q1, q1, q2, shift_rows(-bound)], axis=0)
        k_packs[h] = jnp.concatenate([k1, k2, k1, tail], axis=0)

    score = lambda h, at: dot(k_packs[h], q_packs[h, :, at], TN)
    ahead = score(*blocks[0])
    for i, (h, at) in enumerate(blocks):
        s = ahead
        if i + 1 < len(blocks):
            ahead = score(*blocks[i + 1])
        p1, p2 = split2(jnp.exp2(s))
        counts[0, h, :, at] = dot(ids, p1) + dot(ids, p2)

    low = [jnp.min(jnp.sum(counts[0, h], axis=0, keepdims=True)) for h in heads]

    @pl.when(jnp.logical_not(jnp.minimum(jnp.minimum(low[0], low[1]), jnp.minimum(low[2], low[3])) > 1e-25))
    def _():
        for h, at in blocks:
            qp = q_packs[h, :, at]
            s = dot(k_packs[h, : 3 * HDIM, :], qp[: 3 * HDIM], TN)
            top = jnp.max(s, axis=0, keepdims=True)
            p1, p2 = split2(jnp.exp2(s - top))
            counts[0, h, :, at] = dot(ids, p1) + dot(ids, p2)
            shifts[h, :, at] = top

    for h in heads:
        cnt = counts[0, h]
        total = jnp.sum(cnt, axis=0, keepdims=True)
        cnt = cnt / total
        counts[0, h] = cnt
        logs[0, h] = shifts[h] + jnp.log2(total)
        c1, c2 = split2(cnt)
        rows = slice(h * HDIM, (h + 1) * HDIM)
        att[0, rows, :] = dot(tv[rows, : 3 * ROWS], stack(c1, c1, c2))


def backward_kernel(
    here, tq, tk, tv, hot_q, hot, hot3, cosq, sinq, cosk, sink, logs, counts, datt, *refs
):
    grads, q_packs, k_packs, e_packs, d_q, d_k = refs[-6:]
    span = hot_q.shape[-1]
    whole = hot.shape[-1]
    step = min(256, span)
    heads = range(GROUP)

    @pl.when(pl.program_id(1) == 0)
    def _():
        grads[...] = jnp.zeros_like(grads)

    qs, ks = rotated(
        tq[...], tk[...], hot_q[0], hot[0], cosq[...], sinq[...], cosk[...], sink[...]
    )
    tail = ones_rows(whole)
    gvs = []
    for h in heads:
        q1, q2 = split2(qs[h])
        k1, k2 = split2(ks[h])
        q_packs[h] = jnp.concatenate([q1, q1, q2, shift_rows(-logs[0, h])], axis=0)
        k_packs[h] = jnp.concatenate([k1, k2, k1, tail], axis=0)
    for h in heads:
        rows = slice(h * HDIM, (h + 1) * HDIM)
        d1, d2 = split2(datt[0, rows, :])
        cnt = counts[0, h]
        table = tv[rows, :]
        e = dot(table[:, : 2 * ROWS], d1, TN)
        e = e[:ROWS] + e[ROWS:] + dot(table[:, :ROWS], d2, TN)
        e = e - jnp.sum(e * cnt, axis=0, keepdims=True)
        e_packs[h] = stack(*split3(e), jnp.zeros((8, span), bf16))
        c1, c2 = split2(cnt)
        both = dot(jnp.concatenate([d1, d2], axis=0), c1, NT)
        gvs.append(both[:HDIM] + both[HDIM:] + dot(d1, c2, NT))

    blocks = [(h, c) for h in heads for c in range(0, span, step)]

    def products(h, c):
        at = slice(c, c + step)
        return dot(k_packs[h], q_packs[h, :, at], TN), dot(hot3[0], e_packs[h, :, at])

    ahead = products(*blocks[0])
    for i, (h, c) in enumerate(blocks):
        s, d_probs = ahead
        if i + 1 < len(blocks):
            ahead = products(*blocks[i + 1])
        s1, s2 = split2(jnp.exp2(s) * d_probs)
        at = slice(c, c + step)
        qp = q_packs[h, :, at]
        a = dot(k_packs[h, : 2 * HDIM, :], s1)
        d_q[h, :, at] = a[:HDIM] + a[HDIM:] + dot(k_packs[h, :HDIM, :], s2)
        b = dot(qp[HDIM : 3 * HDIM], s1, NT)
        b = b[:HDIM] + b[HDIM:] + dot(qp[:HDIM], s2, NT)
        if c:
            d_k[h] += b
        else:
            d_k[h] = b

    gqs, gks = [], []
    for h in heads:
        dq = turn_back(d_q[h], cosq[...], sinq[...]) * SCALE
        a = dot(jnp.concatenate(split2(dq), axis=0), hot_q[0, :ROWS, :], NT)
        gqs.append(a[:HDIM] + a[HDIM:])
    for h in heads:
        dk = turn_back(d_k[h], cosk[...], sink[...]) * (1.0 / LOG2E)
        b = dot(jnp.concatenate(split2(dk), axis=0), hot[0, :ROWS, :], NT)
        gks.append(b[:HDIM] + b[HDIM:])
    for i, gs in enumerate((gqs, gks, gvs)):
        grads[0, i] += jnp.concatenate(gs, axis=0).T


def attention_specs(crops, span, whole, first):
    group = lambda *dims: pl.BlockSpec(dims, lambda g, c, w: (first + g,) + (0,) * (len(dims) - 1))
    rope_q = pl.BlockSpec((HALF, span), lambda g, c, w: (0, w[1]))
    rope_k = pl.BlockSpec((HALF, whole), lambda g, c, w: (0, 0))
    return dict(
        table=group(128, 128),
        hot_q=pl.BlockSpec((1, 128, span), lambda g, c, w: (c, 0, w[1])),
        hot=pl.BlockSpec((1, 128, whole), lambda g, c, w: (c, 0, 0)),
        hot3=pl.BlockSpec((1, whole, 128), lambda g, c, w: (c, 0, 0)),
        rope=[rope_q, rope_q, rope_k, rope_k],
        features=pl.BlockSpec((1, 128, span), lambda g, c, w: (c, first + g, 0)),
        logs=pl.BlockSpec((1, GROUP, 1, span), lambda g, c, w: (c, first + g, 0, 0)),
        counts=pl.BlockSpec((1, GROUP, ROWS, span), lambda g, c, w: (c, first + g, 0, 0)),
    )


def attention_forward(here, tq, tk, tv, hot, cos, sin, span):
    crops, _, whole = hot.shape
    s = attention_specs(crops, span, whole, 0)
    like = jax.ShapeDtypeStruct
    return pl.pallas_call(
        forward_kernel,
        grid_spec=pltpu.PrefetchScalarGridSpec(
            num_scalar_prefetch=1,
            grid=(HEADS // GROUP, crops),
            in_specs=[s["table"]] * 3 + [s["hot_q"], s["hot"]] + s["rope"],
            out_specs=[s["features"], s["logs"], s["counts"]],
            scratch_shapes=[
                pltpu.VMEM((GROUP, 128, span), bf16),
                pltpu.VMEM((GROUP, 128, whole), bf16),
                pltpu.VMEM((GROUP, 1, span), f32),
            ],
        ),
        out_shape=[
            like((crops, HEADS * HDIM, span), f32),
            like((crops, HEADS, 1, span), f32),
            like((crops, HEADS, ROWS, span), f32),
        ],
        compiler_params=params(48),
        cost_estimate=cost(),
        name="attend",
    )(here, tq, tk, tv, hot, hot, cos, sin, cos, sin)


def attention_backward(here, tq, tk, tv, hot, hot3, cos, sin, logs, counts, datt, first, groups, chain):
    after = chain.deps()
    crops, _, whole = hot.shape
    span = datt.shape[-1]
    s = attention_specs(crops, span, whole, first)
    return chain.set(pl.pallas_call(
        backward_kernel,
        grid_spec=pltpu.PrefetchScalarGridSpec(
            num_scalar_prefetch=1,
            grid=(groups, crops),
            in_specs=[s["table"]] * 3
            + [s["hot_q"], s["hot"], s["hot3"]]
            + s["rope"]
            + [s["logs"], s["counts"], s["features"]]
            + [ANY] * len(after),
            out_specs=[pl.BlockSpec((1, 3, ROWS, 128), lambda g, c, w: (g, 0, 0, 0))],
            scratch_shapes=[
                pltpu.VMEM((GROUP, 128, span), bf16),
                pltpu.VMEM((GROUP, 128, whole), bf16),
                pltpu.VMEM((GROUP, 128, span), bf16),
                pltpu.VMEM((GROUP, HDIM, span), f32),
                pltpu.VMEM((GROUP, HDIM, whole), f32),
            ],
        ),
        out_shape=[jax.ShapeDtypeStruct((groups, 3, ROWS, 128), f32)],
        compiler_params=params(48),
        cost_estimate=cost(),
        name="attend_back",
    )(here, tq, tk, tv, hot, hot, hot3, cos, sin, cos, sin, logs, counts, datt, *after)[0])


def middle_kernel(att, wo, bo, hot3, packed, gain, shift, after, normed, weight):
    first = (pl.program_id(0) == 0) & (pl.program_id(1) == 0)

    @pl.when(first)
    def _():
        weight[0], weight[1] = split2(wo[...])

    w = (weight[0], weight[1])
    x = dot(hot3[0], packed[...]) + three(split2(att[0]), w, TN) + line(bo)
    after[...] = x
    normed[...] = norm_stats(x)[0] * line(gain) + line(shift)


def middle(here, att, wo, bo, hot3, packed, gain, shift):
    crops, width, span = att.shape
    block = min(256, span)
    steps = span // block
    full = lambda *dims: pl.BlockSpec(dims, lambda c, i, w: (0,) * len(dims))
    rows = pl.BlockSpec((block, width), lambda c, i, w: (c * steps + i, 0))
    out = jax.ShapeDtypeStruct((crops * span, width), f32)
    return pl.pallas_call(
        lambda w, *refs: middle_kernel(*refs),
        grid_spec=pltpu.PrefetchScalarGridSpec(
            num_scalar_prefetch=1,
            grid=(crops, steps),
            in_specs=[
                pl.BlockSpec((1, width, block), lambda c, i, w: (c, 0, i)),
                full(width, width),
                full(width),
                pl.BlockSpec((1, block, 128), lambda c, i, w: (c, w[1] * steps + i, 0)),
                full(128, width),
                full(width),
                full(width),
            ],
            out_specs=[rows, rows],
            scratch_shapes=[pltpu.VMEM((2, width, width), bf16)],
        ),
        out_shape=[out, out],
        compiler_params=params(32),
        cost_estimate=cost(),
        name="middle",
    )(here, att, wo, bo, hot3, packed, gain, shift)


def middle_back_kernel(
    after, d_own, d_swapped, cot, gain, att, wo, hot, clusters, bias_a, bias_b, bias_c, where, cluster, datt, keep, send,
    weight, product, sums, flat,
):
    crops, steps = pl.num_programs(0), pl.num_programs(1)
    step = pl.program_id(0) * steps + pl.program_id(1)
    width = wo.shape[0]
    tiles = width // 128

    @pl.when(step == 0)
    def _():
        weight[0], weight[1] = split2(wo[...])
        product[...] = jnp.zeros_like(product)
        sums[...] = jnp.zeros_like(sums)

    g = cot[...] * clusters[cluster[pl.program_id(0)]]
    unit, scale = norm_stats(after[...])
    d_normed = d_own[...] + d_swapped[...]
    d = g + norm_back(d_normed, unit, scale, line(gain))
    pair = split2(d)
    datt[0] = three((weight[0], weight[1]), pair, NT)
    product[...] += three(split2(att[0]), pair)
    ids = hot[0, :ROWS, :]
    sums[:ROWS] += dot(ids, pair[0]) + dot(ids, pair[1])
    vectors = [jnp.sum(v, axis=0, keepdims=True) for v in (d, d_normed * unit, d_normed, g)]
    sums[ROWS:] += jnp.concatenate(vectors + [jnp.zeros((4, width), f32)], axis=0)

    @pl.when(step == crops * steps - 1)
    def _():
        flat[...] = jnp.zeros_like(flat)
        for t in range(tiles):
            at = slice(t * 128, (t + 1) * 128)
            flat[t * width : (t + 1) * width, :] = product[:, at]
            base = tiles * width + t * (ROWS + 8)
            flat[base : base + ROWS + 8, :] = sums[:, at]
        base = tiles * (width + ROWS + 8)
        biases = jnp.concatenate([bias_a[...], bias_b[...], bias_c[...]], axis=1)
        count = biases.shape[1] // 128
        core = where[0]
        for t in range(count):
            flat[pl.ds(base + core * count + t, 1), :] = biases[:, t * 128 : (t + 1) * 128]
        half = keep.shape[0]
        keep[...] = flat[pl.ds(pl.multiple_of(core * half, 8), half), :]
        send[...] = flat[pl.ds(pl.multiple_of((1 - core) * half, 8), half), :]


def middle_back(sides, cluster, clusters, after, d_own, d_swapped, cot, gain, att, wo, hot, biases, unit_rows, chain):
    crops, width, span = att.shape
    block = min(256, span)
    steps = span // block
    hidden = 2 * sum(b.shape[1] for b in biases)
    rows = width // 128 * (width + ROWS + 8) + hidden // 128
    rows += -rows % unit_rows
    full = lambda *dims: pl.BlockSpec(dims, lambda c, i, w, k: (0,) * len(dims))
    token = pl.BlockSpec((block, width), lambda c, i, w, k: (c * steps + i, 0))
    features = pl.BlockSpec((1, width, block), lambda c, i, w, k: (c, 0, i))
    like = jax.ShapeDtypeStruct
    deps = chain.deps()
    count = len(deps)

    def kernel(w, k, *refs):
        middle_back_kernel(*refs[:12], w, k, *refs[12 + count :])

    out = pl.pallas_call(
        kernel,
        grid_spec=pltpu.PrefetchScalarGridSpec(
            num_scalar_prefetch=2,
            grid=(crops, steps),
            in_specs=[token] * 4
            + [
                full(width),
                features,
                full(width, width),
                pl.BlockSpec((1, 128, block), lambda c, i, w, k: (c, 0, w[1] * steps + i)),
            ]
            + [pl.BlockSpec(memory_space=pltpu.SMEM)]
            + [full(*b.shape) for b in biases]
            + [ANY] * count,
            out_specs=[features, full(rows // 2, 128), full(rows // 2, 128)],
            scratch_shapes=[
                pltpu.VMEM((2, width, width), bf16),
                pltpu.VMEM((width, width), f32),
                pltpu.VMEM((ROWS + 8, width), f32),
                pltpu.VMEM((rows, 128), f32),
            ],
        ),
        out_shape=[like((crops, width, span), f32)] + [like((rows // 2, 128), f32)] * 2,
        compiler_params=params(40),
        cost_estimate=cost(),
        name="middle_back",
    )(sides.array, cluster, after, d_own, d_swapped, cot, gain, att, wo, hot, clusters, *biases, *deps)
    chain.set(out[0])
    return out


BLOCK = 256


def three_wide(a, b, dims=NN):
    (i,), (j,) = dims[0]
    return dot(
        jnp.concatenate([a[0], a[0], a[1]], axis=i), jnp.concatenate([b[0], b[1], b[0]], axis=j), dims
    )


def ff_kernel(fresh, split, unit_at, where, *refs):
    if fresh:
        cluster, cluster_other = refs[:2]
        clusters = refs[6]
        sources = refs[2:6]
        up, up_bias, down = refs[7:10]
        keep, send, bias, h1, h2, p1, p2, nh, nl, gh, gl = refs[-11:]

        @pl.when(pl.program_id(0) == 0)
        def _():
            half = nh.shape[0] // 2
            crops = cluster.shape[0]
            span = half // crops
            for i, source in enumerate(sources[:2]):
                at = slice(i * half, (i + 1) * half)
                nh[at], nl[at] = split2(source[...])
            for i, (source, ids) in enumerate(zip(sources[2:], (cluster, cluster_other))):
                for c in range(crops):
                    at = slice(i * half + c * span, i * half + (c + 1) * span)
                    gh[at], gl[at] = split2(source[c * span : (c + 1) * span] * clusters[ids[c]])

    else:
        nh, nl, gh, gl, up, up_bias, down = refs[:7]
        keep, send, bias, h1, h2, p1, p2 = refs[-7:]
    step = pl.program_id(0)
    count = pl.num_programs(0)
    bias_at = pl.multiple_of(unit_at(where) + step * BLOCK, BLOCK)
    normed, grad = (nh[...], nl[...]), (gh[...], gl[...])
    up2, down2 = split2(up[...]), split2(down[...])
    u = three_wide(normed, up2) + up_bias[pl.ds(bias_at, BLOCK)].reshape(1, BLOCK)
    cdf = 0.5 * (1.0 + lax.erf(u * (0.5**0.5)))
    density = jnp.exp(-0.5 * u * u) * (1.0 / math.sqrt(2.0 * math.pi))
    ff = split2(u * cdf)
    d_pre = three_wide(grad, down2, NT) * (cdf + u * density)
    bias[...] = jnp.sum(d_pre, axis=0, keepdims=True)
    d_pre = split2(d_pre)
    h1[...], h2[...] = ff
    p1[...], p2[...] = d_pre
    g_down = three_wide(ff, grad, TN)
    g_up = three_wide(d_pre, normed, TN).T
    width = g_down.shape[1]

    def put(down_ref, up_ref):
        for t in range(width // 128):
            at = pl.multiple_of((t * count + step) * BLOCK, BLOCK)
            down_ref[pl.ds(at, BLOCK), :] = g_down[:, t * 128 : (t + 1) * 128]
        for t in range(BLOCK // 128):
            at = pl.multiple_of((step * (BLOCK // 128) + t) * width, 128)
            up_ref[pl.ds(at, width), :] = g_up[:, t * 128 : (t + 1) * 128]

    @pl.when(where[split] == 0)
    def _():
        put(keep, send)

    @pl.when(where[split] == 1)
    def _():
        put(send, keep)


def ff_chunk(sides, stage, scalars, sources, up, up_bias, down, first, blocks, buffers, chain):
    fresh = not buffers
    split = sides.at(stage)
    deps = chain.deps()
    width = sources[0].shape[1]
    tokens = sources[0].shape[0] * (2 if fresh else 1)
    hidden = up.shape[1]
    half = hidden // 2 // BLOCK
    slab = blocks * BLOCK * width // 128
    full = lambda *dims: pl.BlockSpec(dims, lambda j, w, *_: (0,) * len(dims))
    column = pl.BlockSpec((tokens, BLOCK), lambda j, w, *_: (0, first + j))
    like = jax.ShapeDtypeStruct
    pair = [like((tokens, width), bf16)] * 4 if fresh else []
    out = pl.pallas_call(
        lambda *refs: ff_kernel(fresh, split, lambda w: (w[0] * half + first) * BLOCK, *refs),
        grid_spec=pltpu.PrefetchScalarGridSpec(
            num_scalar_prefetch=1 + len(scalars),
            grid=(blocks,),
            in_specs=[full(*s.shape) if s.ndim == 2 else pl.BlockSpec(memory_space=pltpu.SMEM) for s in sources]
            + [
                pl.BlockSpec((width, BLOCK), lambda j, w, *_: (0, w[0] * half + first + j)),
                full(hidden),
                pl.BlockSpec((BLOCK, width), lambda j, w, *_: (w[0] * half + first + j, 0)),
            ]
            + [ANY] * (len(buffers) + len(deps)),
            out_specs=[full(slab, 128), full(slab, 128), pl.BlockSpec((1, BLOCK), lambda j, w, *_: (0, j))]
            + [column] * 4
            + [full(tokens, width)] * len(pair),
        ),
        out_shape=[like((slab, 128), f32), like((slab, 128), f32), like((1, blocks * BLOCK), f32)]
        + [like((tokens, hidden // 2), bf16)] * 4
        + pair,
        input_output_aliases={len(scalars) + len(sources) + 4 + i: 3 + i for i in range(len(buffers))},
        compiler_params=params(58),
        cost_estimate=cost(),
        name="feed",
    )(sides.array, *scalars, *sources, up, up_bias, down, *buffers, *deps)
    chain.set(out[0])
    return out


def back_product_kernel(dims, where, a1, a2, w, *refs):
    own, other = refs[-2:]
    step = pl.program_id(0)
    out = three_wide((a1[...], a2[...]), split2(w[...]), dims)
    half = own.shape[0]

    @pl.when(step == 0)
    def _():
        own[...] = out[:half]
        other[...] = out[half:]

    @pl.when(step > 0)
    def _():
        own[...] += out[:half]
        other[...] += out[half:]


def back_product(sides, a, weight, dims, chain):
    tokens, units = a[0].shape
    deps = chain.deps()
    wide = 5 * BLOCK // 2 if units % (5 * BLOCK) == 0 else BLOCK
    steps = units // wide
    up_like = dims is NT
    width = weight.shape[0 if up_like else 1]
    out = jax.ShapeDtypeStruct((tokens // 2, width), f32)
    spec = (
        pl.BlockSpec((width, wide), lambda j, w: (0, w[0] * steps + j))
        if up_like
        else pl.BlockSpec((wide, width), lambda j, w: (w[0] * steps + j, 0))
    )
    out = pl.pallas_call(
        lambda *refs: back_product_kernel(dims, *refs),
        grid_spec=pltpu.PrefetchScalarGridSpec(
            num_scalar_prefetch=1,
            grid=(steps,),
            in_specs=[pl.BlockSpec((tokens, wide), lambda j, w: (0, j))] * 2 + [spec] + [ANY] * len(deps),
            out_specs=[pl.BlockSpec((tokens // 2, width), lambda j, w: (0, 0))] * 2,
        ),
        out_shape=[out, out],
        compiler_params=params(48),
        cost_estimate=cost(),
        name="feed_back" if up_like else "feed_out",
    )(sides.array, *a, weight, *deps)
    chain.set(out[0])
    return out


class Chain:
    def __init__(self):
        self.last = []

    def deps(self):
        return list(self.last)

    def set(self, out):
        self.last = [out]
        return out


def bits_of(axis):
    size = lax.axis_size(axis)
    return [(axis, 1 << i) for i in range(size.bit_length() - 1)]


def swap(x, stage):
    axis, bit = stage
    return lax.ppermute(x, axis, [(i, i ^ bit) for i in range(lax.axis_size(axis))])


def side(stage):
    axis, bit = stage
    return ((lax.axis_index(axis) // bit) % 2).astype(jnp.int32)


class Sides:
    def __init__(self, core_stage, stages):
        self.stages = list(dict.fromkeys(stages))
        self.core_at = 2 + self.stages.index(core_stage)
        self.array = jnp.stack(
            [side(core_stage), lax.axis_index("seq").astype(jnp.int32)] + [side(s) for s in self.stages]
        )

    def at(self, stage):
        return 2 + self.stages.index(stage)


def add_split_kernel(where, k_here, r_here, k_away, r_away, *refs):
    keep, send = refs[-2:]
    keep[...] = k_here[...] + r_here[...]
    send[...] = k_away[...] + r_away[...]


def add_split(kept, received, sides, stage, chain):
    rows, lanes = kept.shape
    half = rows // 2
    at = sides.at(stage)
    if half % 8:
        total = kept + received
        me = side(stage)
        return (
            lax.dynamic_slice_in_dim(total, me * half, half, 0),
            lax.dynamic_slice_in_dim(total, (1 - me) * half, half, 0),
        )
    deps = chain.deps()
    steps = 2 if half % 16 == 0 and half >= 512 else 1
    block = (half // steps, lanes)
    here = pl.BlockSpec(block, lambda i, w: (w[at] * steps + i, 0))
    away = pl.BlockSpec(block, lambda i, w: ((1 - w[at]) * steps + i, 0))
    plain = pl.BlockSpec(block, lambda i, w: (i, 0))
    out = jax.ShapeDtypeStruct((half, lanes), f32)
    keep, send = pl.pallas_call(
        add_split_kernel,
        grid_spec=pltpu.PrefetchScalarGridSpec(
            num_scalar_prefetch=1,
            grid=(steps,),
            in_specs=[here, here, away, away] + [ANY] * len(deps),
            out_specs=[plain, plain],
        ),
        out_shape=[out, out],
        compiler_params=params(16),
        cost_estimate=cost(STEP),
        name="add_split",
    )(sides.array, kept, received, kept, received, *deps)
    chain.set(keep)
    return keep, send


def add_kernel(a, b, *refs):
    refs[-1][...] = a[...] + b[...]


def add(a, b, chain):
    deps = chain.deps()
    full = pl.BlockSpec(a.shape, lambda: (0,) * a.ndim)
    return chain.set(
        pl.pallas_call(
            add_kernel,
            in_specs=[full, full] + [ANY] * len(deps),
            out_specs=full,
            out_shape=jax.ShapeDtypeStruct(a.shape, f32),
            compiler_params=params(16),
            cost_estimate=cost(STEP),
            name="add",
        )(a, b, *deps)
    )


def join_kernel(at, where, x, other, *refs):
    out = refs[-1]
    mine = pl.program_id(0) == where[at]

    @pl.when(mine)
    def _():
        out[...] = x[...]

    @pl.when(jnp.logical_not(mine))
    def _():
        out[...] = other[...]


def join(x, other, sides, stage, chain):
    if x.shape[0] % 8:
        return jnp.where(
            side(stage) == 0, jnp.concatenate([x, other], axis=0), jnp.concatenate([other, x], axis=0)
        )
    deps = chain.deps()
    at = sides.at(stage)
    full = pl.BlockSpec(x.shape, lambda i, w: (0, 0))
    return chain.set(
        pl.pallas_call(
            lambda *refs: join_kernel(at, *refs),
            grid_spec=pltpu.PrefetchScalarGridSpec(
                num_scalar_prefetch=1,
                grid=(2,),
                in_specs=[full, full] + [ANY] * len(deps),
                out_specs=pl.BlockSpec(x.shape, lambda i, w: (i, 0)),
            ),
            out_shape=jax.ShapeDtypeStruct((2 * x.shape[0], x.shape[1]), f32),
            compiler_params=params(16),
            cost_estimate=cost(STEP),
            name="join",
        )(sides.array, x, other, *deps)
    )


class Sum:
    def __init__(self, keep, send, stages, sides, chain):
        self.x, self.stages, self.sides, self.chain = keep, stages, sides, chain
        self.at = 0
        self.coming = swap(send, stages[0])

    def step(self):
        self.at += 1
        n = len(self.stages)
        if self.at < n:
            stage = self.stages[self.at]
            self.x, send = add_split(self.x, self.coming, self.sides, stage, self.chain)
        elif self.at == n:
            stage = self.stages[-1]
            self.x = send = add(self.x, self.coming, self.chain)
        else:
            done, stage = self.stages[2 * n - self.at], self.stages[2 * n - self.at - 1]
            self.x = send = join(self.x, self.coming, self.sides, done, self.chain)
        self.coming = swap(send, stage)

    @property
    def left(self):
        return 2 * len(self.stages) - 1 - self.at

    def whole(self):
        while self.left:
            self.step()
        return join(self.x, self.coming, self.sides, self.stages[0], self.chain)


class Doubling:
    def __init__(self, keep, send, stages, sides, chain):
        self.x, self.stages, self.sides, self.chain = keep, stages, sides, chain
        self.at = 0
        self.coming = swap(send, stages[0])

    def step(self):
        self.at += 1
        self.x = add(self.x, self.coming, self.chain)
        self.coming = swap(self.x, self.stages[self.at % len(self.stages)])

    @property
    def left(self):
        return len(self.stages) - self.at

    def whole(self):
        return join(self.x, self.coming, self.sides, self.stages[0], self.chain)


def place_kernel(split, items, first, blocks, width, half, where, *refs):
    down, up, sems = refs[-3:]
    units = blocks * BLOCK

    def copies(side):
        out = []
        for i, (mine, own) in enumerate(items):
            base = pl.multiple_of((where[0] if mine else 1 - where[0]) * half + first * BLOCK, BLOCK)
            if own == (side == 0):
                for t in range(width // 128):
                    out.append((refs[i].at[pl.ds(t * units, units), :], down.at[pl.ds(base, units), pl.ds(t * 128, 128)]))
            else:
                for t in range(units // 128):
                    at = pl.multiple_of(base + t * 128, 128)
                    out.append((refs[i].at[pl.ds(t * width, width), :], up.at[:, pl.ds(at, 128)]))
        return [pltpu.make_async_copy(a, b, sems.at[n]) for n, (a, b) in enumerate(out)]

    for side in range(2):

        @pl.when(where[split] == side)
        def _():
            moving = copies(side)
            for m in moving:
                m.start()
            for m in moving:
                m.wait()


def place(sides, stage, items, first, blocks, width, hidden, buffers, chain):
    split = sides.at(stage)
    deps = chain.deps()
    kinds = [(mine, own) for _, mine, own in items]
    arrays = [x for x, _, _ in items]
    most = len(items) * max(width, blocks * BLOCK) // 128
    outs = pl.pallas_call(
        lambda *refs: place_kernel(split, kinds, first, blocks, width, hidden // 2, *refs),
        grid_spec=pltpu.PrefetchScalarGridSpec(
            num_scalar_prefetch=1,
            grid=(1,),
            in_specs=[ANY] * (len(arrays) + len(buffers) + len(deps)),
            out_specs=[ANY, ANY],
            scratch_shapes=[pltpu.SemaphoreType.DMA((most,))],
        ),
        out_shape=[
            jax.ShapeDtypeStruct((hidden, width), f32),
            jax.ShapeDtypeStruct((width, hidden), f32),
        ],
        input_output_aliases={1 + len(arrays) + i: i for i in range(len(buffers))},
        compiler_params=params(8),
        cost_estimate=cost(STEP),
        name="place",
    )(sides.array, *arrays, *buffers, *deps)
    chain.set(arrays[0])
    return outs


ROUTES = dict(a="xyzw", b="zyxw", c="xyzw", d="kyzxw", e="kxzwy")

PLAN = " ".join(
    [
        "feed_a", "feed_b", "feed_c", "back", "a", "middle", "attend0", "b", "a", "c", "d", "attend1", "a",
        "b", "attend2", "a", "c", "b", "attend3", "d", "a", "attend4", "tables", "b", "d", "a", "e", "d", "b",
        "c", "e", "d", "c", "b", "e", "d", "a", "c", "d", "e", "c", "b", "d", "Ea", "out", "c", "e", "d", "La",
        "Eb", "finish", "Lb", "Pa", "Ec", "Lc", "Pb", "Pc",
    ]
)


def local(
    token_ids,
    embedding,
    first_gain,
    first_shift,
    query_weight,
    query_bias,
    key_weight,
    key_bias,
    value_weight,
    value_bias,
    out_weight,
    out_bias,
    second_gain,
    second_shift,
    up_weight,
    up_bias,
    down_weight,
    down_bias,
    cotangent,
    crop_cluster,
    cluster_weight,
):
    crops, span = token_ids.shape
    width = embedding.shape[1]
    units = up_weight.shape[1]
    ring = lax.axis_size("seq")
    whole = span * ring
    seq_bits, crop_bits = bits_of("seq"), bits_of("crop")
    core_stage, across, along = crop_bits[0], crop_bits[1:2], crop_bits[2:]
    axes = dict(x=across, y=seq_bits, z=along[:1], w=along[1:], k=[core_stage])
    route = {name: sum((axes[axis] for axis in path), []) for name, path in ROUTES.items()}
    sides = Sides(core_stage, seq_bits + crop_bits)
    chain = Chain()

    if ring == 2:
        ids = [token_ids, swap(token_ids, ("seq", 1))]
    else:
        ids = [lax.all_gather(token_ids, "seq", axis=1, tiled=True)]
    cot = cotangent.reshape(-1, width)
    cot_other = swap(cot, core_stage)
    cluster_other = swap(crop_cluster, core_stage)

    frequency = (10000.0 ** (-2.0 * np.arange(HALF) / HDIM)).astype(np.float32)
    angles = (frequency[:, None] * np.arange(whole, dtype=np.float32)[None, :]).astype(np.float64)
    cos, sin = jnp.asarray(np.cos(angles), f32), jnp.asarray(np.sin(angles), f32)

    tq, tk, tv, packed = project_rows(
        embedding, first_gain, first_shift, query_weight, query_bias, key_weight, key_bias, value_weight, value_bias
    )
    hot, hot3 = spots(sides, ids, whole, [tq])
    att, logs, counts = attention_forward(sides.array, tq, tk, tv, hot, cos, sin, span)
    after_attn, normed = middle(sides.array, att, out_weight, out_bias, hot3, packed, second_gain, second_shift)

    sources = [normed, swap(normed, core_stage), cot, cot_other, cluster_weight]
    scalars = [crop_cluster, cluster_other]
    blocks = units // 2 // BLOCK
    third = 2 * (blocks // 5)
    spans = {}
    first = 0
    for name, count in (("a", third), ("b", third), ("c", blocks - 2 * third)):
        spans[name] = (first, count, route[name])
        first += count
    devices = lax.axis_size("seq") * lax.axis_size("crop")

    sums, biases, tables, early, late, outs, buffers = {}, [], [], {}, {}, [], []

    def step(name):
        total = sums[name]
        if total.left:
            total.step()
            if name in spans and not total.left:
                early[name] = swap(total.x, core_stage)

    def complete(*names):
        while any(sums[name].left for name in names):
            for name in names:
                step(name)

    def put(name, items):
        first, count, stages = spans[name]
        return place(sides, stages[0], items, first, count, width, units, outs, chain)

    for item in PLAN.split():
        kind, name = item.rstrip("01234"), item[-1]
        if item in sums:
            step(item)
        elif kind[0] == "E":
            complete(name)
            outs = put(name, [(early[name], False, True), (sums[name].x, True, True)])
        elif kind[0] == "L":
            complete(name)
            late[name] = swap(sums[name].coming, core_stage)
        elif kind[0] == "P":
            outs = put(name, [(late[name], False, False), (sums[name].coming, True, False)])
        elif kind == "finish":
            complete("d", "e")
            table, rest = sums["e"].whole(), sums["d"].whole()
            g_wq, g_wk, g_wv, g_ow, g_bq, g_bk, g_bv, g_emb, g_gain, g_shift, g_ob, g_sg, g_ss, g_db, g_ub = finish(
                embedding, first_gain, first_shift, table, rest, query_weight, key_weight, value_weight, units, chain
            )
        elif kind.startswith("feed"):
            first, count, stages = spans[name]
            keep, send, bias, *buffers = ff_chunk(
                sides, stages[0], scalars, sources, up_weight, up_bias, down_weight, first, count, buffers, chain
            )
            if len(buffers) > 4:
                sources, scalars, buffers = buffers[4:], [], buffers[:4]
            sums[name] = Sum(keep, send, stages, sides, chain)
            biases.append(bias)
        elif kind == "back":
            h1, h2, p1, p2 = buffers
            d_own, d_other = back_product(sides, (p1, p2), up_weight, NT, chain)
            d_swapped = swap(d_other, core_stage)
        elif kind == "middle":
            d_att, keep, send = middle_back(
                sides, crop_cluster, cluster_weight, after_attn, d_own, d_swapped, cot, second_gain, att, out_weight,
                hot, biases, 8 * devices, chain,
            )
            sums["d"] = Sum(keep, send, route["d"], sides, chain)
        elif kind == "attend":
            tables.append(
                attention_backward(
                    sides.array, tq, tk, tv, hot, hot3, cos, sin, logs, counts, d_att, int(name), 1, chain
                )
            )
        elif kind == "tables":
            sums["e"] = Doubling(*pack_tables(sides, tables, 16, chain), route["e"], sides, chain)
        elif kind == "out":
            o_own, o_other = back_product(sides, (h1, h2), down_weight, NN, chain)
            o_swapped = swap(o_other, core_stage)
            block_out = (after_attn + o_own + o_swapped + down_bias).reshape(cotangent.shape)
    g_dw, g_uw = outs
    return (
        block_out, g_emb, g_gain, g_shift, g_wq, g_bq, g_wk, g_bk, g_wv, g_bv, g_ow, g_ob, g_sg, g_ss, g_uw, g_ub,
        g_dw, g_db,
    )


def solution(mesh):
    in_specs = (
        (P("crop", "seq"),) + (P(),) * 17 + (P("crop", "seq", None), P("crop"), P())
    )
    out_specs = (P("crop", "seq", None),) + (P(),) * 17
    return jax.shard_map(local, mesh=mesh, in_specs=in_specs, out_specs=out_specs, check_vma=False)
```

```python
import math
import jax
import jax.numpy as jnp
import numpy as np
from jax import lax
from jax.experimental import pallas as pl
from jax.experimental.pallas import tpu as pltpu
from jax.sharding import PartitionSpec as P

HEADS = 20
HDIM = 32
HALF = 16
VOCAB = 33
ROWS = 40
GROUP = 4
f32 = jnp.float32
bf16 = jnp.bfloat16
epsilon = 1e-05
LOG2E = 1.0 / math.log(2.0)
SCALE = HDIM**-0.5

NN = (((1,), (0,)), ((), ()))
NT = (((1,), (1,)), ((), ()))
TN = (((0,), (0,)), ((), ()))
ANY = pl.BlockSpec(memory_space=pl.ANY)


def params(mib):
    return pltpu.CompilerParams(vmem_limit_bytes=mib << 20)


def cost(flops=2000000000):
    return pl.CostEstimate(flops=flops, bytes_accessed=0, transcendentals=0)


STEP = 4000000000


def dot(a, b, dims=NN):
    return lax.dot_general(a, b, dims, preferred_element_type=f32)


def split2(x):
    head = x.astype(bf16)
    return head, (x - head.astype(f32)).astype(bf16)


def split3(x):
    head = x.astype(bf16)
    x = x - head.astype(f32)
    mid = x.astype(bf16)
    return head, mid, (x - mid.astype(f32)).astype(bf16)


def three(a, b, dims=NN):
    return dot(a[0], b[0], dims) + dot(a[0], b[1], dims) + dot(a[1], b[0], dims)


def turn(u, cos, sin):
    a, b = u[:HALF], u[HALF:]
    return jnp.concatenate([a * cos - b * sin, b * cos + a * sin], axis=0)


def turn_back(u, cos, sin):
    a, b = u[:HALF], u[HALF:]
    return jnp.concatenate([a * cos + b * sin, b * cos - a * sin], axis=0)


def stack(*rows):
    return jnp.concatenate([r.astype(f32) for r in rows], axis=0).astype(bf16)


def norm_stats(x):
    centred = x - jnp.mean(x, axis=-1, keepdims=True)
    scale = lax.rsqrt(jnp.mean(centred * centred, axis=-1, keepdims=True) + epsilon)
    return centred * scale, scale


def norm_back(d_normed, unit, scale, gain):
    d = d_normed * gain
    d = d - jnp.mean(d, axis=-1, keepdims=True) - unit * jnp.mean(d * unit, axis=-1, keepdims=True)
    return d * scale


def tall(emb):
    return jnp.concatenate([emb, jnp.zeros((ROWS - VOCAB, emb.shape[1]), f32)], axis=0)


def line(v):
    return v[...].reshape(1, -1)


def rows_kernel(emb, gain, shift, wq, bq, wk, bk, wv, bv, tq, tk, tv, packed, normed):
    width = emb.shape[1]
    step = pl.program_id(0)

    @pl.when(step == 0)
    def _():
        rows = tall(emb[...])
        unit, _ = norm_stats(rows)
        normed[...] = stack(*split2(unit * line(gain) + line(shift)))
        packed[...] = stack(*split3(rows), jnp.zeros((8, width), bf16))

    full = normed[...]
    real = lax.broadcasted_iota(jnp.int32, (ROWS, 128), 0) < VOCAB

    def table(w, b):
        w1, w2 = split2(w[...])
        by1 = dot(full, w1)
        t = by1[:ROWS] + (by1[ROWS:] + dot(full[:ROWS], w2))
        bias = b[pl.ds(pl.multiple_of(step * 128, 128), 128)].reshape(1, 128)
        return jnp.where(real, t + bias, 0.0)

    def lay(a, b, c):
        blank = jnp.zeros((8, 128), f32)
        return jnp.concatenate([a.astype(f32), b.astype(f32), c.astype(f32), blank], axis=0).T.astype(bf16)

    tq[...] = lay(*split3(table(wq, bq)))
    tk[...] = lay(*split3(table(wk, bk)))
    v1, v2 = split2(table(wv, bv))
    tv[...] = lay(v1, v2, v1)


def project_rows(emb, gain, shift, wq, bq, wk, bk, wv, bv):
    width = emb.shape[1]
    full = lambda *dims: pl.BlockSpec(dims, lambda i: (0,) * len(dims))
    weight = pl.BlockSpec((width, 128), lambda i: (0, i))
    table = pl.BlockSpec((128, 128), lambda i: (i, 0))
    like = jax.ShapeDtypeStruct
    return pl.pallas_call(
        rows_kernel,
        grid=(width // 128,),
        in_specs=[full(VOCAB, width), full(width), full(width)] + [weight, full(width)] * 3,
        out_specs=[table] * 3 + [full(128, width)],
        out_shape=[like((width, 128), bf16)] * 3 + [like((128, width), bf16)],
        scratch_shapes=[pltpu.VMEM((2 * ROWS, width), bf16)],
        compiler_params=params(60),
        cost_estimate=cost(),
        name="rows",
    )(emb, gain, shift, wq, bq, wk, bk, wv, bv)


def spots_kernel(count, where, *refs):
    ids, (hot, hot3) = refs[:count], refs[-2:]
    crops, span = ids[0].shape
    spot = lax.broadcasted_iota(jnp.int32, (128, span), 0)
    code = jnp.where(
        spot < ROWS, spot, jnp.where(spot < 2 * ROWS, spot - ROWS, jnp.where(spot < 3 * ROWS, spot - 2 * ROWS, -1))
    )
    for n in range(count):
        at = 0 if count == 1 else pl.multiple_of((where[1] if n == 0 else 1 - where[1]) * span, span)
        for c in range(crops):
            spots = jnp.where(ids[n][c : c + 1, :] == code, 1.0, 0.0)
            hot[c, :, pl.ds(at, span)] = spots.astype(bf16)
            hot3[c, pl.ds(at, span), :] = spots.T.astype(bf16)


def spots(sides, ids, whole, deps):
    crops = ids[0].shape[0]
    full = lambda *dims: pl.BlockSpec(dims, lambda i, w: (0,) * len(dims))
    count = len(ids)
    like = jax.ShapeDtypeStruct
    return pl.pallas_call(
        lambda *refs: spots_kernel(count, *refs),
        grid_spec=pltpu.PrefetchScalarGridSpec(
            num_scalar_prefetch=1,
            grid=(1,),
            in_specs=[full(*i.shape) for i in ids] + [ANY] * len(deps),
            out_specs=[full(crops, 128, whole), full(crops, whole, 128)],
        ),
        out_shape=[like((crops, 128, whole), bf16), like((crops, whole, 128), bf16)],
        compiler_params=params(32),
        cost_estimate=cost(),
        name="spots",
    )(sides.array, *ids, *deps)


def finish_kernel(
    emb, gain, shift, table, rest, wq, wk, wv, g_wq, g_wk, g_wv, g_ow, g_bq, g_bk, g_bv, g_emb, g_gain, g_shift, g_ob,
    g_sg, g_ss, g_db, g_ub, normed, d_normed,
):
    step = pl.program_id(0)
    width = emb.shape[1]
    tiles = width // 128

    @pl.when(step == 0)
    def _():
        unit, _ = norm_stats(tall(emb[...]))
        n1, n2 = split2(unit * line(gain) + line(shift))
        normed[...] = stack(n1, n1, n2, jnp.zeros((8, n1.shape[1]), bf16))
        d_normed[...] = jnp.zeros_like(d_normed)

    blank = jnp.zeros((8, 128), bf16)
    at = pl.ds(pl.multiple_of(step * 128, 128), 128)
    for i, (w, out, bias) in enumerate(((wq, g_wq, g_bq), (wk, g_wk, g_bk), (wv, g_wv, g_bv))):
        g = table[i * ROWS : (i + 1) * ROWS, :]
        g1, g2 = split2(g)
        out[...] = dot(normed[...], stack(g1, g2, g1, blank), TN)
        bias[at] = jnp.sum(g, axis=0)
        d_normed[...] += three((g1, g2), split2(w[...]), NT)
    g_ow[...] = rest[pl.ds(pl.multiple_of(step * width, 128), width), :]

    @pl.when(step == pl.num_programs(0) - 1)
    def _():
        unit, scale = norm_stats(tall(emb[...]))
        d = d_normed[...]
        g_gain[...] = jnp.sum(d * unit, axis=0)
        g_shift[...] = jnp.sum(d, axis=0)
        back = norm_back(d, unit, scale, line(gain))
        for t in range(tiles):
            at = slice(t * 128, (t + 1) * 128)
            base = tiles * width + t * (ROWS + 8)
            g_emb[:, at] = (back[:, at] + rest[base : base + ROWS, :])[:VOCAB]
            for i, out in enumerate((g_ob, g_sg, g_ss, g_db)):
                out[at] = rest[base + ROWS + i, :]
        base = tiles * (width + ROWS + 8)
        for t in range(g_ub.shape[0] // 128):
            g_ub[t * 128 : (t + 1) * 128] = rest[base + t, :]


def finish(emb, gain, shift, table, rest, wq, wk, wv, hidden, chain):
    width = emb.shape[1]
    full = lambda *dims: pl.BlockSpec(dims, lambda i: (0,) * len(dims))
    weight = pl.BlockSpec((width, 128), lambda i: (0, i))
    like = jax.ShapeDtypeStruct
    deps = chain.deps()
    vector, square = like((width,), f32), like((width, width), f32)

    def kernel(*refs):
        finish_kernel(*refs[:8], *refs[8 + len(deps) :])

    out = pl.pallas_call(
        kernel,
        grid=(width // 128,),
        in_specs=[full(VOCAB, width), full(width), full(width)]
        + [pl.BlockSpec((3 * ROWS, 128), lambda i: (i, 0)), full(*rest.shape)]
        + [weight] * 3
        + [ANY] * len(deps),
        out_specs=[weight] * 4 + [full(width)] * 3 + [full(VOCAB, width)] + [full(width)] * 6 + [full(hidden)],
        out_shape=[square] * 4 + [vector] * 3 + [like((VOCAB, width), f32)] + [vector] * 6 + [like((hidden,), f32)],
        scratch_shapes=[pltpu.VMEM((128, width), bf16), pltpu.VMEM((ROWS, width), f32)],
        compiler_params=params(32),
        cost_estimate=cost(),
        name="finish",
    )(emb, gain, shift, table, rest, wq, wk, wv, *deps)
    chain.set(out[0])
    return out


def pack_kernel(where, *refs):
    keep, send, flat = refs[-3:]
    flat[...] = jnp.zeros_like(flat)
    at = 0
    for table in refs[:-3]:
        for g in range(table.shape[0]):
            for i in range(3):
                flat[at : at + ROWS, :] = table[g, i]
                at += ROWS
    half = keep.shape[0]
    keep[...] = flat[pl.ds(pl.multiple_of(where[0] * half, 8), half), :]
    send[...] = flat[pl.ds(pl.multiple_of((1 - where[0]) * half, 8), half), :]


def pack_tables(sides, tables, unit_rows, chain):
    rows = 3 * ROWS * sum(t.shape[0] for t in tables)
    rows += -rows % unit_rows
    full = lambda *dims: pl.BlockSpec(dims, lambda i, w: (0,) * len(dims))
    half = jax.ShapeDtypeStruct((rows // 2, 128), f32)
    out = pl.pallas_call(
        pack_kernel,
        grid_spec=pltpu.PrefetchScalarGridSpec(
            num_scalar_prefetch=1,
            grid=(1,),
            in_specs=[full(*t.shape) for t in tables],
            out_specs=[full(*half.shape)] * 2,
            scratch_shapes=[pltpu.VMEM((rows, 128), f32)],
        ),
        out_shape=[half, half],
        compiler_params=params(16),
        cost_estimate=cost(STEP),
        name="pack",
    )(sides.array, *tables)
    chain.set(out[0])
    return out


def rotated(tq, tk, hot_q, hot, cosq, sinq, cosk, sink):
    q = dot(tq, hot_q)
    k = dot(tk, hot)
    heads = [slice(h * HDIM, (h + 1) * HDIM) for h in range(GROUP)]
    qs = [turn(q[h], cosq, sinq) * (SCALE * LOG2E) for h in heads]
    ks = [turn(k[h], cosk, sink) for h in heads]
    return qs, ks


def shift_rows(shift):
    s1, s2, s3 = split3(shift)
    row = lax.broadcasted_iota(jnp.int32, (HDIM, shift.shape[1]), 0)
    s1, s2, s3 = s1.astype(f32), s2.astype(f32), s3.astype(f32)
    return jnp.where(row == 0, s1, jnp.where(row == 1, s2, jnp.where(row == 2, s3, 0.0))).astype(bf16)


def ones_rows(n):
    return jnp.where(lax.broadcasted_iota(jnp.int32, (HDIM, n), 0) < 3, 1.0, 0.0).astype(bf16)


def forward_kernel(
    here, tq, tk, tv, hot_q, hot, cosq, sinq, cosk, sink, att, logs, counts, q_packs, k_packs, shifts
):
    span = hot_q.shape[-1]
    whole = hot.shape[-1]
    step = min(256, span)
    ids = hot[0, :ROWS, :]
    heads = range(GROUP)
    blocks = [(h, slice(c, c + step)) for h in heads for c in range(0, span, step)]

    qs, ks = rotated(
        tq[...], tk[...], hot_q[0], hot[0], cosq[...], sinq[...], cosk[...], sink[...]
    )
    tail = ones_rows(whole)
    for h in heads:
        q, k = qs[h], ks[h]
        longest = jnp.max(jnp.sum(k * k, axis=0, keepdims=True), axis=1, keepdims=True)
        bound = jnp.sqrt(jnp.sum(q * q, axis=0, keepdims=True) * longest)
        shifts[h] = bound
        q1, q2 = split2(q)
        k1, k2 = split2(k)
        q_packs[h] = jnp.concatenate([q1, q1, q2, shift_rows(-bound)], axis=0)
        k_packs[h] = jnp.concatenate([k1, k2, k1, tail], axis=0)

    score = lambda h, at: dot(k_packs[h], q_packs[h, :, at], TN)
    ahead = score(*blocks[0])
    for i, (h, at) in enumerate(blocks):
        s = ahead
        if i + 1 < len(blocks):
            ahead = score(*blocks[i + 1])
        p1, p2 = split2(jnp.exp2(s))
        counts[0, h, :, at] = dot(ids, p1) + dot(ids, p2)

    low = [jnp.min(jnp.sum(counts[0, h], axis=0, keepdims=True)) for h in heads]

    @pl.when(jnp.logical_not(jnp.minimum(jnp.minimum(low[0], low[1]), jnp.minimum(low[2], low[3])) > 1e-25))
    def _():
        for h, at in blocks:
            qp = q_packs[h, :, at]
            s = dot(k_packs[h, : 3 * HDIM, :], qp[: 3 * HDIM], TN)
            top = jnp.max(s, axis=0, keepdims=True)
            p1, p2 = split2(jnp.exp2(s - top))
            counts[0, h, :, at] = dot(ids, p1) + dot(ids, p2)
            shifts[h, :, at] = top

    for h in heads:
        cnt = counts[0, h]
        total = jnp.sum(cnt, axis=0, keepdims=True)
        cnt = cnt / total
        counts[0, h] = cnt
        logs[0, h] = shifts[h] + jnp.log2(total)
        c1, c2 = split2(cnt)
        rows = slice(h * HDIM, (h + 1) * HDIM)
        att[0, rows, :] = dot(tv[rows, : 3 * ROWS], stack(c1, c1, c2))


def backward_kernel(
    here, tq, tk, tv, hot_q, hot, hot3, cosq, sinq, cosk, sink, logs, counts, datt, *refs
):
    grads, q_packs, k_packs, e_packs, d_q, d_k = refs[-6:]
    span = hot_q.shape[-1]
    whole = hot.shape[-1]
    step = min(256, span)
    heads = range(GROUP)

    @pl.when(pl.program_id(1) == 0)
    def _():
        grads[...] = jnp.zeros_like(grads)

    qs, ks = rotated(
        tq[...], tk[...], hot_q[0], hot[0], cosq[...], sinq[...], cosk[...], sink[...]
    )
    tail = ones_rows(whole)
    gvs = []
    for h in heads:
        q1, q2 = split2(qs[h])
        k1, k2 = split2(ks[h])
        q_packs[h] = jnp.concatenate([q1, q1, q2, shift_rows(-logs[0, h])], axis=0)
        k_packs[h] = jnp.concatenate([k1, k2, k1, tail], axis=0)
    for h in heads:
        rows = slice(h * HDIM, (h + 1) * HDIM)
        d1, d2 = split2(datt[0, rows, :])
        cnt = counts[0, h]
        table = tv[rows, :]
        e = dot(table[:, : 2 * ROWS], d1, TN)
        e = e[:ROWS] + e[ROWS:] + dot(table[:, :ROWS], d2, TN)
        e = e - jnp.sum(e * cnt, axis=0, keepdims=True)
        e_packs[h] = stack(*split3(e), jnp.zeros((8, span), bf16))
        c1, c2 = split2(cnt)
        both = dot(jnp.concatenate([d1, d2], axis=0), c1, NT)
        gvs.append(both[:HDIM] + both[HDIM:] + dot(d1, c2, NT))

    blocks = [(h, c) for h in heads for c in range(0, span, step)]

    def products(h, c):
        at = slice(c, c + step)
        return dot(k_packs[h], q_packs[h, :, at], TN), dot(hot3[0], e_packs[h, :, at])

    ahead = products(*blocks[0])
    for i, (h, c) in enumerate(blocks):
        s, d_probs = ahead
        if i + 1 < len(blocks):
            ahead = products(*blocks[i + 1])
        s1, s2 = split2(jnp.exp2(s) * d_probs)
        at = slice(c, c + step)
        qp = q_packs[h, :, at]
        a = dot(k_packs[h, : 2 * HDIM, :], s1)
        d_q[h, :, at] = a[:HDIM] + a[HDIM:] + dot(k_packs[h, :HDIM, :], s2)
        b = dot(qp[HDIM : 3 * HDIM], s1, NT)
        b = b[:HDIM] + b[HDIM:] + dot(qp[:HDIM], s2, NT)
        if c:
            d_k[h] += b
        else:
            d_k[h] = b

    gqs, gks = [], []
    for h in heads:
        dq = turn_back(d_q[h], cosq[...], sinq[...]) * SCALE
        a = dot(jnp.concatenate(split2(dq), axis=0), hot_q[0, :ROWS, :], NT)
        gqs.append(a[:HDIM] + a[HDIM:])
    for h in heads:
        dk = turn_back(d_k[h], cosk[...], sink[...]) * (1.0 / LOG2E)
        b = dot(jnp.concatenate(split2(dk), axis=0), hot[0, :ROWS, :], NT)
        gks.append(b[:HDIM] + b[HDIM:])
    for i, gs in enumerate((gqs, gks, gvs)):
        grads[0, i] += jnp.concatenate(gs, axis=0).T


def attention_specs(crops, span, whole, first):
    group = lambda *dims: pl.BlockSpec(dims, lambda g, c, w: (first + g,) + (0,) * (len(dims) - 1))
    rope_q = pl.BlockSpec((HALF, span), lambda g, c, w: (0, w[1]))
    rope_k = pl.BlockSpec((HALF, whole), lambda g, c, w: (0, 0))
    return dict(
        table=group(128, 128),
        hot_q=pl.BlockSpec((1, 128, span), lambda g, c, w: (c, 0, w[1])),
        hot=pl.BlockSpec((1, 128, whole), lambda g, c, w: (c, 0, 0)),
        hot3=pl.BlockSpec((1, whole, 128), lambda g, c, w: (c, 0, 0)),
        rope=[rope_q, rope_q, rope_k, rope_k],
        features=pl.BlockSpec((1, 128, span), lambda g, c, w: (c, first + g, 0)),
        logs=pl.BlockSpec((1, GROUP, 1, span), lambda g, c, w: (c, first + g, 0, 0)),
        counts=pl.BlockSpec((1, GROUP, ROWS, span), lambda g, c, w: (c, first + g, 0, 0)),
    )


def attention_forward(here, tq, tk, tv, hot, cos, sin, span):
    crops, _, whole = hot.shape
    s = attention_specs(crops, span, whole, 0)
    like = jax.ShapeDtypeStruct
    return pl.pallas_call(
        forward_kernel,
        grid_spec=pltpu.PrefetchScalarGridSpec(
            num_scalar_prefetch=1,
            grid=(HEADS // GROUP, crops),
            in_specs=[s["table"]] * 3 + [s["hot_q"], s["hot"]] + s["rope"],
            out_specs=[s["features"], s["logs"], s["counts"]],
            scratch_shapes=[
                pltpu.VMEM((GROUP, 128, span), bf16),
                pltpu.VMEM((GROUP, 128, whole), bf16),
                pltpu.VMEM((GROUP, 1, span), f32),
            ],
        ),
        out_shape=[
            like((crops, HEADS * HDIM, span), f32),
            like((crops, HEADS, 1, span), f32),
            like((crops, HEADS, ROWS, span), f32),
        ],
        compiler_params=params(48),
        cost_estimate=cost(),
        name="attend",
    )(here, tq, tk, tv, hot, hot, cos, sin, cos, sin)


def attention_backward(here, tq, tk, tv, hot, hot3, cos, sin, logs, counts, datt, first, groups, chain):
    after = chain.deps()
    crops, _, whole = hot.shape
    span = datt.shape[-1]
    s = attention_specs(crops, span, whole, first)
    return chain.set(pl.pallas_call(
        backward_kernel,
        grid_spec=pltpu.PrefetchScalarGridSpec(
            num_scalar_prefetch=1,
            grid=(groups, crops),
            in_specs=[s["table"]] * 3
            + [s["hot_q"], s["hot"], s["hot3"]]
            + s["rope"]
            + [s["logs"], s["counts"], s["features"]]
            + [ANY] * len(after),
            out_specs=[pl.BlockSpec((1, 3, ROWS, 128), lambda g, c, w: (g, 0, 0, 0))],
            scratch_shapes=[
                pltpu.VMEM((GROUP, 128, span), bf16),
                pltpu.VMEM((GROUP, 128, whole), bf16),
                pltpu.VMEM((GROUP, 128, span), bf16),
                pltpu.VMEM((GROUP, HDIM, span), f32),
                pltpu.VMEM((GROUP, HDIM, whole), f32),
            ],
        ),
        out_shape=[jax.ShapeDtypeStruct((groups, 3, ROWS, 128), f32)],
        compiler_params=params(48),
        cost_estimate=cost(),
        name="attend_back",
    )(here, tq, tk, tv, hot, hot, hot3, cos, sin, cos, sin, logs, counts, datt, *after)[0])


def middle_kernel(att, wo, bo, hot3, packed, gain, shift, after, normed, weight):
    first = (pl.program_id(0) == 0) & (pl.program_id(1) == 0)

    @pl.when(first)
    def _():
        weight[0], weight[1] = split2(wo[...])

    w = (weight[0], weight[1])
    x = dot(hot3[0], packed[...]) + three(split2(att[0]), w, TN) + line(bo)
    after[...] = x
    normed[...] = norm_stats(x)[0] * line(gain) + line(shift)


def middle(here, att, wo, bo, hot3, packed, gain, shift):
    crops, width, span = att.shape
    block = min(256, span)
    steps = span // block
    full = lambda *dims: pl.BlockSpec(dims, lambda c, i, w: (0,) * len(dims))
    rows = pl.BlockSpec((block, width), lambda c, i, w: (c * steps + i, 0))
    out = jax.ShapeDtypeStruct((crops * span, width), f32)
    return pl.pallas_call(
        lambda w, *refs: middle_kernel(*refs),
        grid_spec=pltpu.PrefetchScalarGridSpec(
            num_scalar_prefetch=1,
            grid=(crops, steps),
            in_specs=[
                pl.BlockSpec((1, width, block), lambda c, i, w: (c, 0, i)),
                full(width, width),
                full(width),
                pl.BlockSpec((1, block, 128), lambda c, i, w: (c, w[1] * steps + i, 0)),
                full(128, width),
                full(width),
                full(width),
            ],
            out_specs=[rows, rows],
            scratch_shapes=[pltpu.VMEM((2, width, width), bf16)],
        ),
        out_shape=[out, out],
        compiler_params=params(32),
        cost_estimate=cost(),
        name="middle",
    )(here, att, wo, bo, hot3, packed, gain, shift)


def middle_back_kernel(
    after, d_own, d_swapped, cot, gain, att, wo, hot, clusters, bias_a, bias_b, bias_c, where, cluster, datt, keep, send,
    weight, product, sums, flat,
):
    crops, steps = pl.num_programs(0), pl.num_programs(1)
    step = pl.program_id(0) * steps + pl.program_id(1)
    width = wo.shape[0]
    tiles = width // 128

    @pl.when(step == 0)
    def _():
        weight[0], weight[1] = split2(wo[...])
        product[...] = jnp.zeros_like(product)
        sums[...] = jnp.zeros_like(sums)

    g = cot[...] * clusters[cluster[pl.program_id(0)]]
    unit, scale = norm_stats(after[...])
    d_normed = d_own[...] + d_swapped[...]
    d = g + norm_back(d_normed, unit, scale, line(gain))
    pair = split2(d)
    datt[0] = three((weight[0], weight[1]), pair, NT)
    product[...] += three(split2(att[0]), pair)
    ids = hot[0, :ROWS, :]
    sums[:ROWS] += dot(ids, pair[0]) + dot(ids, pair[1])
    vectors = [jnp.sum(v, axis=0, keepdims=True) for v in (d, d_normed * unit, d_normed, g)]
    sums[ROWS:] += jnp.concatenate(vectors + [jnp.zeros((4, width), f32)], axis=0)

    @pl.when(step == crops * steps - 1)
    def _():
        flat[...] = jnp.zeros_like(flat)
        for t in range(tiles):
            at = slice(t * 128, (t + 1) * 128)
            flat[t * width : (t + 1) * width, :] = product[:, at]
            base = tiles * width + t * (ROWS + 8)
            flat[base : base + ROWS + 8, :] = sums[:, at]
        base = tiles * (width + ROWS + 8)
        biases = jnp.concatenate([bias_a[...], bias_b[...], bias_c[...]], axis=1)
        count = biases.shape[1] // 128
        core = where[0]
        for t in range(count):
            flat[pl.ds(base + core * count + t, 1), :] = biases[:, t * 128 : (t + 1) * 128]
        half = keep.shape[0]
        keep[...] = flat[pl.ds(pl.multiple_of(core * half, 8), half), :]
        send[...] = flat[pl.ds(pl.multiple_of((1 - core) * half, 8), half), :]


def middle_back(sides, cluster, clusters, after, d_own, d_swapped, cot, gain, att, wo, hot, biases, unit_rows, chain):
    crops, width, span = att.shape
    block = min(256, span)
    steps = span // block
    hidden = 2 * sum(b.shape[1] for b in biases)
    rows = width // 128 * (width + ROWS + 8) + hidden // 128
    rows += -rows % unit_rows
    full = lambda *dims: pl.BlockSpec(dims, lambda c, i, w, k: (0,) * len(dims))
    token = pl.BlockSpec((block, width), lambda c, i, w, k: (c * steps + i, 0))
    features = pl.BlockSpec((1, width, block), lambda c, i, w, k: (c, 0, i))
    like = jax.ShapeDtypeStruct
    deps = chain.deps()
    count = len(deps)

    def kernel(w, k, *refs):
        middle_back_kernel(*refs[:12], w, k, *refs[12 + count :])

    out = pl.pallas_call(
        kernel,
        grid_spec=pltpu.PrefetchScalarGridSpec(
            num_scalar_prefetch=2,
            grid=(crops, steps),
            in_specs=[token] * 4
            + [
                full(width),
                features,
                full(width, width),
                pl.BlockSpec((1, 128, block), lambda c, i, w, k: (c, 0, w[1] * steps + i)),
            ]
            + [pl.BlockSpec(memory_space=pltpu.SMEM)]
            + [full(*b.shape) for b in biases]
            + [ANY] * count,
            out_specs=[features, full(rows // 2, 128), full(rows // 2, 128)],
            scratch_shapes=[
                pltpu.VMEM((2, width, width), bf16),
                pltpu.VMEM((width, width), f32),
                pltpu.VMEM((ROWS + 8, width), f32),
                pltpu.VMEM((rows, 128), f32),
            ],
        ),
        out_shape=[like((crops, width, span), f32)] + [like((rows // 2, 128), f32)] * 2,
        compiler_params=params(40),
        cost_estimate=cost(),
        name="middle_back",
    )(sides.array, cluster, after, d_own, d_swapped, cot, gain, att, wo, hot, clusters, *biases, *deps)
    chain.set(out[0])
    return out


BLOCK = 256


def three_wide(a, b, dims=NN):
    (i,), (j,) = dims[0]
    return dot(
        jnp.concatenate([a[0], a[0], a[1]], axis=i), jnp.concatenate([b[0], b[1], b[0]], axis=j), dims
    )


def ff_kernel(fresh, split, unit_at, where, *refs):
    if fresh:
        cluster, cluster_other = refs[:2]
        clusters = refs[6]
        sources = refs[2:6]
        up, up_bias, down = refs[7:10]
        keep, send, bias, h1, h2, p1, p2, nh, nl, gh, gl = refs[-11:]

        @pl.when(pl.program_id(0) == 0)
        def _():
            half = nh.shape[0] // 2
            crops = cluster.shape[0]
            span = half // crops
            for i, source in enumerate(sources[:2]):
                at = slice(i * half, (i + 1) * half)
                nh[at], nl[at] = split2(source[...])
            for i, (source, ids) in enumerate(zip(sources[2:], (cluster, cluster_other))):
                for c in range(crops):
                    at = slice(i * half + c * span, i * half + (c + 1) * span)
                    gh[at], gl[at] = split2(source[c * span : (c + 1) * span] * clusters[ids[c]])

    else:
        nh, nl, gh, gl, up, up_bias, down = refs[:7]
        keep, send, bias, h1, h2, p1, p2 = refs[-7:]
    step = pl.program_id(0)
    bias_at = pl.multiple_of(unit_at(where) + step * BLOCK, BLOCK)
    normed, grad = (nh[...], nl[...]), (gh[...], gl[...])
    up2, down2 = split2(up[...]), split2(down[...])
    u = three_wide(normed, up2) + up_bias[pl.ds(bias_at, BLOCK)].reshape(1, BLOCK)
    cdf = 0.5 * (1.0 + lax.erf(u * (0.5**0.5)))
    density = jnp.exp(-0.5 * u * u) * (1.0 / math.sqrt(2.0 * math.pi))
    ff = split2(u * cdf)
    d_pre = three_wide(grad, down2, NT) * (cdf + u * density)
    bias[...] = jnp.sum(d_pre, axis=0, keepdims=True)
    d_pre = split2(d_pre)
    h1[...], h2[...] = ff
    p1[...], p2[...] = d_pre
    g_down = three_wide(ff, grad, TN)
    g_up = three_wide(d_pre, normed, TN).T
    width = g_down.shape[1]

    def put(down_ref, up_ref):
        for t in range(width // 128):
            down_ref[t * BLOCK : (t + 1) * BLOCK, :] = g_down[:, t * 128 : (t + 1) * 128]
        for t in range(BLOCK // 128):
            up_ref[t * width : (t + 1) * width, :] = g_up[:, t * 128 : (t + 1) * 128]

    @pl.when(where[split] == 0)
    def _():
        put(keep, send)

    @pl.when(where[split] == 1)
    def _():
        put(send, keep)


def ff_chunk(sides, stage, scalars, sources, up, up_bias, down, first, blocks, buffers, chain):
    fresh = not buffers
    split = sides.at(stage)
    deps = chain.deps()
    width = sources[0].shape[1]
    tokens = sources[0].shape[0] * (2 if fresh else 1)
    hidden = up.shape[1]
    half = hidden // 2 // BLOCK
    slab = blocks * BLOCK * width // 128
    full = lambda *dims: pl.BlockSpec(dims, lambda j, w, *_: (0,) * len(dims))
    column = pl.BlockSpec((tokens, BLOCK), lambda j, w, *_: (0, first + j))
    like = jax.ShapeDtypeStruct
    pair = [like((tokens, width), bf16)] * 4 if fresh else []
    out = pl.pallas_call(
        lambda *refs: ff_kernel(fresh, split, lambda w: (w[0] * half + first) * BLOCK, *refs),
        grid_spec=pltpu.PrefetchScalarGridSpec(
            num_scalar_prefetch=1 + len(scalars),
            grid=(blocks,),
            in_specs=[full(*s.shape) if s.ndim == 2 else pl.BlockSpec(memory_space=pltpu.SMEM) for s in sources]
            + [
                pl.BlockSpec((width, BLOCK), lambda j, w, *_: (0, w[0] * half + first + j)),
                full(hidden),
                pl.BlockSpec((BLOCK, width), lambda j, w, *_: (w[0] * half + first + j, 0)),
            ]
            + [ANY] * (len(buffers) + len(deps)),
            out_specs=[pl.BlockSpec((slab // blocks, 128), lambda j, w, *_: (j, 0))] * 2
            + [pl.BlockSpec((1, BLOCK), lambda j, w, *_: (0, j))]
            + [column] * 4
            + [full(tokens, width)] * len(pair),
        ),
        out_shape=[like((slab, 128), f32), like((slab, 128), f32), like((1, blocks * BLOCK), f32)]
        + [like((tokens, hidden // 2), bf16)] * 4
        + pair,
        input_output_aliases={len(scalars) + len(sources) + 4 + i: 3 + i for i in range(len(buffers))},
        compiler_params=params(58),
        cost_estimate=cost(),
        name="feed",
    )(sides.array, *scalars, *sources, up, up_bias, down, *buffers, *deps)
    chain.set(out[0])
    return out


def back_product_kernel(dims, where, a1, a2, w, *refs):
    own, other = refs[-2:]
    step = pl.program_id(0)
    out = three_wide((a1[...], a2[...]), split2(w[...]), dims)
    half = own.shape[0]

    @pl.when(step == 0)
    def _():
        own[...] = out[:half]
        other[...] = out[half:]

    @pl.when(step > 0)
    def _():
        own[...] += out[:half]
        other[...] += out[half:]


def back_product(sides, a, weight, dims, chain):
    tokens, units = a[0].shape
    deps = chain.deps()
    wide = 5 * BLOCK // 2 if units % (5 * BLOCK) == 0 else BLOCK
    steps = units // wide
    up_like = dims is NT
    width = weight.shape[0 if up_like else 1]
    out = jax.ShapeDtypeStruct((tokens // 2, width), f32)
    spec = (
        pl.BlockSpec((width, wide), lambda j, w: (0, w[0] * steps + j))
        if up_like
        else pl.BlockSpec((wide, width), lambda j, w: (w[0] * steps + j, 0))
    )
    out = pl.pallas_call(
        lambda *refs: back_product_kernel(dims, *refs),
        grid_spec=pltpu.PrefetchScalarGridSpec(
            num_scalar_prefetch=1,
            grid=(steps,),
            in_specs=[pl.BlockSpec((tokens, wide), lambda j, w: (0, j))] * 2 + [spec] + [ANY] * len(deps),
            out_specs=[pl.BlockSpec((tokens // 2, width), lambda j, w: (0, 0))] * 2,
        ),
        out_shape=[out, out],
        compiler_params=params(48),
        cost_estimate=cost(),
        name="feed_back" if up_like else "feed_out",
    )(sides.array, *a, weight, *deps)
    chain.set(out[0])
    return out


class Chain:
    def __init__(self):
        self.last = []

    def deps(self):
        return list(self.last)

    def set(self, out):
        self.last = [out]
        return out


def bits_of(axis):
    size = lax.axis_size(axis)
    return [(axis, 1 << i) for i in range(size.bit_length() - 1)]


def swap(x, stage):
    axis, bit = stage
    return lax.ppermute(x, axis, [(i, i ^ bit) for i in range(lax.axis_size(axis))])


def side(stage):
    axis, bit = stage
    return ((lax.axis_index(axis) // bit) % 2).astype(jnp.int32)


class Sides:
    def __init__(self, core_stage, stages):
        self.stages = list(dict.fromkeys(stages))
        self.core_at = 2 + self.stages.index(core_stage)
        self.array = jnp.stack(
            [side(core_stage), lax.axis_index("seq").astype(jnp.int32)] + [side(s) for s in self.stages]
        )

    def at(self, stage):
        return 2 + self.stages.index(stage)


def add_split_kernel(where, k_here, r_here, k_away, r_away, *refs):
    keep, send = refs[-2:]
    keep[...] = k_here[...] + r_here[...]
    send[...] = k_away[...] + r_away[...]


def add_split(kept, received, sides, stage, chain):
    rows, lanes = kept.shape
    half = rows // 2
    at = sides.at(stage)
    if half % 8:
        total = kept + received
        me = side(stage)
        return (
            lax.dynamic_slice_in_dim(total, me * half, half, 0),
            lax.dynamic_slice_in_dim(total, (1 - me) * half, half, 0),
        )
    deps = chain.deps()
    steps = 2 if half % 16 == 0 and half >= 512 else 1
    block = (half // steps, lanes)
    here = pl.BlockSpec(block, lambda i, w: (w[at] * steps + i, 0))
    away = pl.BlockSpec(block, lambda i, w: ((1 - w[at]) * steps + i, 0))
    plain = pl.BlockSpec(block, lambda i, w: (i, 0))
    out = jax.ShapeDtypeStruct((half, lanes), f32)
    keep, send = pl.pallas_call(
        add_split_kernel,
        grid_spec=pltpu.PrefetchScalarGridSpec(
            num_scalar_prefetch=1,
            grid=(steps,),
            in_specs=[here, here, away, away] + [ANY] * len(deps),
            out_specs=[plain, plain],
        ),
        out_shape=[out, out],
        compiler_params=params(16),
        cost_estimate=cost(STEP),
        name="add_split",
    )(sides.array, kept, received, kept, received, *deps)
    chain.set(keep)
    return keep, send


def add_kernel(a, b, *refs):
    refs[-1][...] = a[...] + b[...]


def add(a, b, chain):
    deps = chain.deps()
    full = pl.BlockSpec(a.shape, lambda: (0,) * a.ndim)
    return chain.set(
        pl.pallas_call(
            add_kernel,
            in_specs=[full, full] + [ANY] * len(deps),
            out_specs=full,
            out_shape=jax.ShapeDtypeStruct(a.shape, f32),
            compiler_params=params(16),
            cost_estimate=cost(STEP),
            name="add",
        )(a, b, *deps)
    )


def join_kernel(at, where, x, other, *refs):
    out = refs[-1]
    mine = pl.program_id(0) == where[at]

    @pl.when(mine)
    def _():
        out[...] = x[...]

    @pl.when(jnp.logical_not(mine))
    def _():
        out[...] = other[...]


def join(x, other, sides, stage, chain):
    if x.shape[0] % 8:
        return jnp.where(
            side(stage) == 0, jnp.concatenate([x, other], axis=0), jnp.concatenate([other, x], axis=0)
        )
    deps = chain.deps()
    at = sides.at(stage)
    full = pl.BlockSpec(x.shape, lambda i, w: (0, 0))
    return chain.set(
        pl.pallas_call(
            lambda *refs: join_kernel(at, *refs),
            grid_spec=pltpu.PrefetchScalarGridSpec(
                num_scalar_prefetch=1,
                grid=(2,),
                in_specs=[full, full] + [ANY] * len(deps),
                out_specs=pl.BlockSpec(x.shape, lambda i, w: (i, 0)),
            ),
            out_shape=jax.ShapeDtypeStruct((2 * x.shape[0], x.shape[1]), f32),
            compiler_params=params(16),
            cost_estimate=cost(STEP),
            name="join",
        )(sides.array, x, other, *deps)
    )


class Sum:
    def __init__(self, keep, send, stages, sides, chain):
        self.x, self.stages, self.sides, self.chain = keep, stages, sides, chain
        self.at = 0
        self.coming = swap(send, stages[0])

    def step(self):
        self.at += 1
        n = len(self.stages)
        if self.at < n:
            stage = self.stages[self.at]
            self.x, send = add_split(self.x, self.coming, self.sides, stage, self.chain)
        elif self.at == n:
            stage = self.stages[-1]
            self.x = send = add(self.x, self.coming, self.chain)
        else:
            done, stage = self.stages[2 * n - self.at], self.stages[2 * n - self.at - 1]
            self.x = send = join(self.x, self.coming, self.sides, done, self.chain)
        self.coming = swap(send, stage)

    @property
    def left(self):
        return 2 * len(self.stages) - 1 - self.at

    def whole(self):
        while self.left:
            self.step()
        return join(self.x, self.coming, self.sides, self.stages[0], self.chain)


class Doubling:
    def __init__(self, keep, send, stages, sides, chain):
        self.x, self.stages, self.sides, self.chain = keep, stages, sides, chain
        self.at = 0
        self.coming = swap(send, stages[0])

    def step(self):
        self.at += 1
        self.x = add(self.x, self.coming, self.chain)
        self.coming = swap(self.x, self.stages[self.at % len(self.stages)])

    @property
    def left(self):
        return len(self.stages) - self.at

    def whole(self):
        return join(self.x, self.coming, self.sides, self.stages[0], self.chain)


def place_kernel(split, items, first, blocks, width, half, where, *refs):
    down, up, sems = refs[-3:]
    tiles = width // 128

    def copies(side):
        out = []
        for i, (mine, own) in enumerate(items):
            base = pl.multiple_of((where[0] if mine else 1 - where[0]) * half + first * BLOCK, BLOCK)
            if own == (side == 0):
                for n in range(blocks * tiles):
                    rows = pl.ds(pl.multiple_of(base + n // tiles * BLOCK, BLOCK), BLOCK)
                    out.append((refs[i].at[pl.ds(n * BLOCK, BLOCK), :], down.at[rows, pl.ds(n % tiles * 128, 128)]))
            else:
                for n in range(blocks * BLOCK // 128):
                    at = pl.multiple_of(base + n * 128, 128)
                    out.append((refs[i].at[pl.ds(n * width, width), :], up.at[:, pl.ds(at, 128)]))
        return [pltpu.make_async_copy(a, b, sems.at[n]) for n, (a, b) in enumerate(out)]

    for side in range(2):

        @pl.when(where[split] == side)
        def _():
            moving = copies(side)
            for m in moving:
                m.start()
            for m in moving:
                m.wait()


def place(sides, stage, items, first, blocks, width, hidden, buffers, chain):
    split = sides.at(stage)
    deps = chain.deps()
    kinds = [(mine, own) for _, mine, own in items]
    arrays = [x for x, _, _ in items]
    most = len(items) * blocks * max(width, BLOCK) // 128
    outs = pl.pallas_call(
        lambda *refs: place_kernel(split, kinds, first, blocks, width, hidden // 2, *refs),
        grid_spec=pltpu.PrefetchScalarGridSpec(
            num_scalar_prefetch=1,
            grid=(1,),
            in_specs=[ANY] * (len(arrays) + len(buffers) + len(deps)),
            out_specs=[ANY, ANY],
            scratch_shapes=[pltpu.SemaphoreType.DMA((most,))],
        ),
        out_shape=[
            jax.ShapeDtypeStruct((hidden, width), f32),
            jax.ShapeDtypeStruct((width, hidden), f32),
        ],
        input_output_aliases={1 + len(arrays) + i: i for i in range(len(buffers))},
        compiler_params=params(8),
        cost_estimate=cost(STEP),
        name="place",
    )(sides.array, *arrays, *buffers, *deps)
    chain.set(arrays[0])
    return outs


ROUTES = dict(a="yzxw", b="xyzw", c="zyxw", d="kzxyw", e="kyxzw")

PLAN = " ".join(
    [
        "feed_a", "feed_b", "feed_c", "back", "a", "c", "b", "middle", "a", "attend0", "b", "d", "a", "c",
        "attend1", "c", "b", "attend2", "attend3", "d", "a", "b", "c", "d", "attend4", "b", "tables", "a", "e",
        "d", "d", "a", "e", "c", "b", "d", "e", "c", "out", "d", "a", "e", "b", "d", "c", "Ea", "e", "d",
        "finish", "Ec", "Eb", "La", "Lb", "Pb", "Pa", "Lc", "Pc",
    ]
)


def local(
    token_ids,
    embedding,
    first_gain,
    first_shift,
    query_weight,
    query_bias,
    key_weight,
    key_bias,
    value_weight,
    value_bias,
    out_weight,
    out_bias,
    second_gain,
    second_shift,
    up_weight,
    up_bias,
    down_weight,
    down_bias,
    cotangent,
    crop_cluster,
    cluster_weight,
):
    crops, span = token_ids.shape
    width = embedding.shape[1]
    units = up_weight.shape[1]
    ring = lax.axis_size("seq")
    whole = span * ring
    seq_bits, crop_bits = bits_of("seq"), bits_of("crop")
    core_stage, across, along = crop_bits[0], crop_bits[1:2], crop_bits[2:]
    axes = dict(x=across, y=seq_bits, z=along[:1], w=along[1:], k=[core_stage])
    route = {name: sum((axes[axis] for axis in path), []) for name, path in ROUTES.items()}
    sides = Sides(core_stage, seq_bits + crop_bits)
    chain = Chain()

    if ring == 2:
        ids = [token_ids, swap(token_ids, ("seq", 1))]
    else:
        ids = [lax.all_gather(token_ids, "seq", axis=1, tiled=True)]
    cot = cotangent.reshape(-1, width)
    cot_other = swap(cot, core_stage)
    cluster_other = swap(crop_cluster, core_stage)

    frequency = (10000.0 ** (-2.0 * np.arange(HALF) / HDIM)).astype(np.float32)
    angles = (frequency[:, None] * np.arange(whole, dtype=np.float32)[None, :]).astype(np.float64)
    cos, sin = jnp.asarray(np.cos(angles), f32), jnp.asarray(np.sin(angles), f32)

    tq, tk, tv, packed = project_rows(
        embedding, first_gain, first_shift, query_weight, query_bias, key_weight, key_bias, value_weight, value_bias
    )
    hot, hot3 = spots(sides, ids, whole, [tq])
    att, logs, counts = attention_forward(sides.array, tq, tk, tv, hot, cos, sin, span)
    after_attn, normed = middle(sides.array, att, out_weight, out_bias, hot3, packed, second_gain, second_shift)

    sources = [normed, swap(normed, core_stage), cot, cot_other, cluster_weight]
    scalars = [crop_cluster, cluster_other]
    blocks = units // 2 // BLOCK
    third = 2 * (blocks // 5)
    spans = {}
    first = 0
    for name, count in (("a", third), ("b", third), ("c", blocks - 2 * third)):
        spans[name] = (first, count, route[name])
        first += count
    devices = lax.axis_size("seq") * lax.axis_size("crop")

    sums, biases, tables, early, late, outs, buffers = {}, [], [], {}, {}, [], []

    def step(name):
        total = sums[name]
        if total.left:
            total.step()
            if name in spans and not total.left:
                early[name] = swap(total.x, core_stage)

    def complete(*names):
        while any(sums[name].left for name in names):
            for name in names:
                step(name)

    def put(name, items):
        first, count, stages = spans[name]
        return place(sides, stages[0], items, first, count, width, units, outs, chain)

    for item in PLAN.split():
        kind, name = item.rstrip("01234"), item[-1]
        if item in sums:
            step(item)
        elif kind[0] == "E":
            complete(name)
            outs = put(name, [(early[name], False, True), (sums[name].x, True, True)])
        elif kind[0] == "L":
            complete(name)
            late[name] = swap(sums[name].coming, core_stage)
        elif kind[0] == "P":
            outs = put(name, [(late[name], False, False), (sums[name].coming, True, False)])
        elif kind == "finish":
            complete("d", "e")
            table, rest = sums["e"].whole(), sums["d"].whole()
            g_wq, g_wk, g_wv, g_ow, g_bq, g_bk, g_bv, g_emb, g_gain, g_shift, g_ob, g_sg, g_ss, g_db, g_ub = finish(
                embedding, first_gain, first_shift, table, rest, query_weight, key_weight, value_weight, units, chain
            )
        elif kind.startswith("feed"):
            first, count, stages = spans[name]
            keep, send, bias, *buffers = ff_chunk(
                sides, stages[0], scalars, sources, up_weight, up_bias, down_weight, first, count, buffers, chain
            )
            if len(buffers) > 4:
                sources, scalars, buffers = buffers[4:], [], buffers[:4]
            sums[name] = Sum(keep, send, stages, sides, chain)
            biases.append(bias)
        elif kind == "back":
            h1, h2, p1, p2 = buffers
            d_own, d_other = back_product(sides, (p1, p2), up_weight, NT, chain)
            d_swapped = swap(d_other, core_stage)
        elif kind == "middle":
            d_att, keep, send = middle_back(
                sides, crop_cluster, cluster_weight, after_attn, d_own, d_swapped, cot, second_gain, att, out_weight,
                hot, biases, 8 * devices, chain,
            )
            sums["d"] = Sum(keep, send, route["d"], sides, chain)
        elif kind == "attend":
            tables.append(
                attention_backward(
                    sides.array, tq, tk, tv, hot, hot3, cos, sin, logs, counts, d_att, int(name), 1, chain
                )
            )
        elif kind == "tables":
            sums["e"] = Doubling(*pack_tables(sides, tables, 16, chain), route["e"], sides, chain)
        elif kind == "out":
            o_own, o_other = back_product(sides, (h1, h2), down_weight, NN, chain)
            o_swapped = swap(o_other, core_stage)
            block_out = (after_attn + o_own + o_swapped + down_bias).reshape(cotangent.shape)
    g_dw, g_uw = outs
    return (
        block_out, g_emb, g_gain, g_shift, g_wq, g_bq, g_wk, g_bk, g_wv, g_bv, g_ow, g_ob, g_sg, g_ss, g_uw, g_ub,
        g_dw, g_db,
    )


def solution(mesh):
    in_specs = (
        (P("crop", "seq"),) + (P(),) * 17 + (P("crop", "seq", None), P("crop"), P())
    )
    out_specs = (P("crop", "seq", None),) + (P(),) * 17
    return jax.shard_map(local, mesh=mesh, in_specs=in_specs, out_specs=out_specs, check_vma=False)
```

```python
import math
import jax
import jax.numpy as jnp
import numpy as np
from jax import lax
from jax.experimental import pallas as pl
from jax.experimental.pallas import tpu as pltpu
from jax.sharding import PartitionSpec as P

HEADS = 20
HDIM = 32
HALF = 16
VOCAB = 33
ROWS = 40
GROUP = 4
f32 = jnp.float32
bf16 = jnp.bfloat16
epsilon = 1e-05
LOG2E = 1.0 / math.log(2.0)
SCALE = HDIM**-0.5

NN = (((1,), (0,)), ((), ()))
NT = (((1,), (1,)), ((), ()))
TN = (((0,), (0,)), ((), ()))
ANY = pl.BlockSpec(memory_space=pl.ANY)


def params(mib):
    return pltpu.CompilerParams(vmem_limit_bytes=mib << 20)


def cost(flops=500000000):
    return pl.CostEstimate(flops=flops, bytes_accessed=0, transcendentals=0)


STEP = 10000000000


def dot(a, b, dims=NN):
    return lax.dot_general(a, b, dims, preferred_element_type=f32)


def split2(x):
    head = x.astype(bf16)
    return head, (x - head.astype(f32)).astype(bf16)


def split3(x):
    head = x.astype(bf16)
    x = x - head.astype(f32)
    mid = x.astype(bf16)
    return head, mid, (x - mid.astype(f32)).astype(bf16)


def three(a, b, dims=NN):
    return dot(a[0], b[0], dims) + dot(a[0], b[1], dims) + dot(a[1], b[0], dims)


def turn(u, cos, sin):
    a, b = u[:HALF], u[HALF:]
    return jnp.concatenate([a * cos - b * sin, b * cos + a * sin], axis=0)


def turn_back(u, cos, sin):
    a, b = u[:HALF], u[HALF:]
    return jnp.concatenate([a * cos + b * sin, b * cos - a * sin], axis=0)


def stack(*rows):
    return jnp.concatenate([r.astype(f32) for r in rows], axis=0).astype(bf16)


def norm_stats(x):
    centred = x - jnp.mean(x, axis=-1, keepdims=True)
    scale = lax.rsqrt(jnp.mean(centred * centred, axis=-1, keepdims=True) + epsilon)
    return centred * scale, scale


def norm_back(d_normed, unit, scale, gain):
    d = d_normed * gain
    d = d - jnp.mean(d, axis=-1, keepdims=True) - unit * jnp.mean(d * unit, axis=-1, keepdims=True)
    return d * scale


def tall(emb):
    return jnp.concatenate([emb, jnp.zeros((ROWS - VOCAB, emb.shape[1]), f32)], axis=0)


def line(v):
    return v[...].reshape(1, -1)


def rows_kernel(emb, gain, shift, wq, bq, wk, bk, wv, bv, tq, tk, tv, packed, normed):
    width = emb.shape[1]
    step = pl.program_id(0)

    @pl.when(step == 0)
    def _():
        rows = tall(emb[...])
        unit, _ = norm_stats(rows)
        normed[...] = stack(*split2(unit * line(gain) + line(shift)))
        packed[...] = stack(*split3(rows), jnp.zeros((8, width), bf16))

    full = normed[...]
    real = lax.broadcasted_iota(jnp.int32, (ROWS, 128), 0) < VOCAB

    def table(w, b):
        w1, w2 = split2(w[...])
        by1 = dot(full, w1)
        t = by1[:ROWS] + (by1[ROWS:] + dot(full[:ROWS], w2))
        bias = b[pl.ds(pl.multiple_of(step * 128, 128), 128)].reshape(1, 128)
        return jnp.where(real, t + bias, 0.0)

    def lay(a, b, c):
        blank = jnp.zeros((8, 128), f32)
        return jnp.concatenate([a.astype(f32), b.astype(f32), c.astype(f32), blank], axis=0).T.astype(bf16)

    q, k, v = table(wq, bq), table(wk, bk), table(wv, bv)
    tq[...] = lay(*split3(q))
    tk[...] = lay(*split3(k))
    v1, v2 = split2(v)
    tv[...] = lay(v1, v2, v1)


def project_rows(emb, gain, shift, wq, bq, wk, bk, wv, bv):
    width = emb.shape[1]
    full = lambda *dims: pl.BlockSpec(dims, lambda i: (0,) * len(dims))
    weight = pl.BlockSpec((width, 128), lambda i: (0, i))
    table = pl.BlockSpec((128, 128), lambda i: (i, 0))
    like = jax.ShapeDtypeStruct
    return pl.pallas_call(
        rows_kernel,
        grid=(width // 128,),
        in_specs=[full(VOCAB, width), full(width), full(width)] + [weight, full(width)] * 3,
        out_specs=[table] * 3 + [full(128, width)],
        out_shape=[like((width, 128), bf16)] * 3 + [like((128, width), bf16)],
        scratch_shapes=[pltpu.VMEM((2 * ROWS, width), bf16)],
        compiler_params=params(60),
        cost_estimate=cost(),
        name="rows",
    )(emb, gain, shift, wq, bq, wk, bk, wv, bv)


def spots_kernel(count, where, *refs):
    ids, (hot, hot3) = refs[:count], refs[-2:]
    crops, span = ids[0].shape
    spot = lax.broadcasted_iota(jnp.int32, (128, span), 0)
    code = jnp.where(
        spot < ROWS, spot, jnp.where(spot < 2 * ROWS, spot - ROWS, jnp.where(spot < 3 * ROWS, spot - 2 * ROWS, -1))
    )
    for n in range(count):
        at = 0 if count == 1 else pl.multiple_of((where[1] if n == 0 else 1 - where[1]) * span, span)
        for c in range(crops):
            spots = jnp.where(ids[n][c : c + 1, :] == code, 1.0, 0.0)
            hot[c, :, pl.ds(at, span)] = spots.astype(bf16)
            hot3[c, pl.ds(at, span), :] = spots.T.astype(bf16)


def spots(sides, ids, whole, deps):
    crops = ids[0].shape[0]
    full = lambda *dims: pl.BlockSpec(dims, lambda i, w: (0,) * len(dims))
    count = len(ids)
    like = jax.ShapeDtypeStruct
    return pl.pallas_call(
        lambda *refs: spots_kernel(count, *refs),
        grid_spec=pltpu.PrefetchScalarGridSpec(
            num_scalar_prefetch=1,
            grid=(1,),
            in_specs=[full(*i.shape) for i in ids] + [ANY] * len(deps),
            out_specs=[full(crops, 128, whole), full(crops, whole, 128)],
        ),
        out_shape=[like((crops, 128, whole), bf16), like((crops, whole, 128), bf16)],
        compiler_params=params(32),
        cost_estimate=cost(),
        name="spots",
    )(sides.array, *ids, *deps)


def finish_kernel(
    emb, gain, shift, table, rest, wq, wk, wv, g_wq, g_wk, g_wv, g_ow, g_bq, g_bk, g_bv, g_emb, g_gain, g_shift, g_ob,
    g_sg, g_ss, g_db, g_ub, normed, d_normed,
):
    step = pl.program_id(0)
    width = emb.shape[1]
    tiles = width // 128

    @pl.when(step == 0)
    def _():
        unit, _ = norm_stats(tall(emb[...]))
        n1, n2 = split2(unit * line(gain) + line(shift))
        normed[...] = stack(n1, n1, n2, jnp.zeros((8, n1.shape[1]), bf16))
        d_normed[...] = jnp.zeros_like(d_normed)

    blank = jnp.zeros((8, 128), bf16)
    at = pl.ds(pl.multiple_of(step * 128, 128), 128)
    for i, (w, out, bias) in enumerate(((wq, g_wq, g_bq), (wk, g_wk, g_bk), (wv, g_wv, g_bv))):
        g = table[i * ROWS : (i + 1) * ROWS, :]
        g1, g2 = split2(g)
        out[...] = dot(normed[...], stack(g1, g2, g1, blank), TN)
        bias[at] = jnp.sum(g, axis=0)
        d_normed[...] += three((g1, g2), split2(w[...]), NT)
    g_ow[...] = rest[pl.ds(pl.multiple_of(step * width, 128), width), :]

    @pl.when(step == pl.num_programs(0) - 1)
    def _():
        unit, scale = norm_stats(tall(emb[...]))
        d = d_normed[...]
        g_gain[...] = jnp.sum(d * unit, axis=0)
        g_shift[...] = jnp.sum(d, axis=0)
        back = norm_back(d, unit, scale, line(gain))
        for t in range(tiles):
            at = slice(t * 128, (t + 1) * 128)
            base = tiles * width + t * (ROWS + 8)
            g_emb[:, at] = (back[:, at] + rest[base : base + ROWS, :])[:VOCAB]
            for i, out in enumerate((g_ob, g_sg, g_ss, g_db)):
                out[at] = rest[base + ROWS + i, :]
        base = tiles * (width + ROWS + 8)
        for t in range(g_ub.shape[0] // 128):
            g_ub[t * 128 : (t + 1) * 128] = rest[base + t, :]


def finish(emb, gain, shift, table, rest, wq, wk, wv, hidden, chain):
    width = emb.shape[1]
    full = lambda *dims: pl.BlockSpec(dims, lambda i: (0,) * len(dims))
    weight = pl.BlockSpec((width, 128), lambda i: (0, i))
    like = jax.ShapeDtypeStruct
    deps = chain.deps()
    vector, square = like((width,), f32), like((width, width), f32)

    def kernel(*refs):
        finish_kernel(*refs[:8], *refs[8 + len(deps) :])

    out = pl.pallas_call(
        kernel,
        grid=(width // 128,),
        in_specs=[full(VOCAB, width), full(width), full(width)]
        + [pl.BlockSpec((3 * ROWS, 128), lambda i: (i, 0)), full(*rest.shape)]
        + [weight] * 3
        + [ANY] * len(deps),
        out_specs=[weight] * 4 + [full(width)] * 3 + [full(VOCAB, width)] + [full(width)] * 6 + [full(hidden)],
        out_shape=[square] * 4 + [vector] * 3 + [like((VOCAB, width), f32)] + [vector] * 6 + [like((hidden,), f32)],
        scratch_shapes=[pltpu.VMEM((128, width), bf16), pltpu.VMEM((ROWS, width), f32)],
        compiler_params=params(32),
        cost_estimate=cost(),
        name="finish",
    )(emb, gain, shift, table, rest, wq, wk, wv, *deps)
    chain.set(out[0])
    return out


def pack_kernel(where, *refs):
    keep, send, flat = refs[-3:]
    flat[...] = jnp.zeros_like(flat)
    at = 0
    for table in refs[:-3]:
        for g in range(table.shape[0]):
            for i in range(3):
                flat[at : at + ROWS, :] = table[g, i]
                at += ROWS
    half = keep.shape[0]
    keep[...] = flat[pl.ds(pl.multiple_of(where[0] * half, 8), half), :]
    send[...] = flat[pl.ds(pl.multiple_of((1 - where[0]) * half, 8), half), :]


def pack_tables(sides, tables, unit_rows, chain):
    rows = 3 * ROWS * sum(t.shape[0] for t in tables)
    rows += -rows % unit_rows
    full = lambda *dims: pl.BlockSpec(dims, lambda i, w: (0,) * len(dims))
    half = jax.ShapeDtypeStruct((rows // 2, 128), f32)
    out = pl.pallas_call(
        pack_kernel,
        grid_spec=pltpu.PrefetchScalarGridSpec(
            num_scalar_prefetch=1,
            grid=(1,),
            in_specs=[full(*t.shape) for t in tables],
            out_specs=[full(*half.shape)] * 2,
            scratch_shapes=[pltpu.VMEM((rows, 128), f32)],
        ),
        out_shape=[half, half],
        compiler_params=params(16),
        cost_estimate=cost(STEP),
        name="pack",
    )(sides.array, *tables)
    chain.set(out[0])
    return out


def rotated(tq, tk, hot_q, hot, cosq, sinq, cosk, sink):
    q = dot(tq, hot_q)
    k = dot(tk, hot)
    heads = [slice(h * HDIM, (h + 1) * HDIM) for h in range(GROUP)]
    qs = [turn(q[h], cosq, sinq) * (SCALE * LOG2E) for h in heads]
    ks = [turn(k[h], cosk, sink) for h in heads]
    return qs, ks


def shift_rows(shift):
    s1, s2, s3 = split3(shift)
    row = lax.broadcasted_iota(jnp.int32, (HDIM, shift.shape[1]), 0)
    s1, s2, s3 = s1.astype(f32), s2.astype(f32), s3.astype(f32)
    return jnp.where(row == 0, s1, jnp.where(row == 1, s2, jnp.where(row == 2, s3, 0.0))).astype(bf16)


def ones_rows(n):
    return jnp.where(lax.broadcasted_iota(jnp.int32, (HDIM, n), 0) < 3, 1.0, 0.0).astype(bf16)


def forward_kernel(
    here, tq, tk, tv, hot_q, hot, cosq, sinq, cosk, sink, att, logs, counts, q_packs, k_packs, shifts
):
    span = hot_q.shape[-1]
    whole = hot.shape[-1]
    step = min(256, span)
    ids = hot[0, :ROWS, :]
    heads = range(GROUP)
    blocks = [(h, slice(c, c + step)) for h in heads for c in range(0, span, step)]

    qs, ks = rotated(
        tq[...], tk[...], hot_q[0], hot[0], cosq[...], sinq[...], cosk[...], sink[...]
    )
    tail = ones_rows(whole)
    for h in heads:
        q, k = qs[h], ks[h]
        longest = jnp.max(jnp.sum(k * k, axis=0, keepdims=True), axis=1, keepdims=True)
        bound = jnp.sqrt(jnp.sum(q * q, axis=0, keepdims=True) * longest)
        shifts[h] = bound
        q1, q2 = split2(q)
        k1, k2 = split2(k)
        q_packs[h] = jnp.concatenate([q1, q1, q2, shift_rows(-bound)], axis=0)
        k_packs[h] = jnp.concatenate([k1, k2, k1, tail], axis=0)

    score = lambda h, at: dot(k_packs[h], q_packs[h, :, at], TN)
    ahead = score(*blocks[0])
    for i, (h, at) in enumerate(blocks):
        s = ahead
        if i + 1 < len(blocks):
            ahead = score(*blocks[i + 1])
        p1, p2 = split2(jnp.exp2(s))
        counts[0, h, :, at] = dot(ids, p1) + dot(ids, p2)

    low = [jnp.min(jnp.sum(counts[0, h], axis=0, keepdims=True)) for h in heads]

    @pl.when(jnp.logical_not(jnp.minimum(jnp.minimum(low[0], low[1]), jnp.minimum(low[2], low[3])) > 1e-25))
    def _():
        for h, at in blocks:
            qp = q_packs[h, :, at]
            s = dot(k_packs[h, : 3 * HDIM, :], qp[: 3 * HDIM], TN)
            top = jnp.max(s, axis=0, keepdims=True)
            p1, p2 = split2(jnp.exp2(s - top))
            counts[0, h, :, at] = dot(ids, p1) + dot(ids, p2)
            shifts[h, :, at] = top

    for h in heads:
        cnt = counts[0, h]
        total = jnp.sum(cnt, axis=0, keepdims=True)
        cnt = cnt / total
        counts[0, h] = cnt
        logs[0, h] = shifts[h] + jnp.log2(total)
        c1, c2 = split2(cnt)
        rows = slice(h * HDIM, (h + 1) * HDIM)
        att[0, rows, :] = dot(tv[rows, : 3 * ROWS], stack(c1, c1, c2))


def backward_kernel(
    here, tq, tk, tv, hot_q, hot, hot3, cosq, sinq, cosk, sink, logs, counts, datt, *refs
):
    grads, q_packs, k_packs, e_packs, d_q, d_k = refs[-6:]
    span = hot_q.shape[-1]
    whole = hot.shape[-1]
    step = min(256, span)
    heads = range(GROUP)

    @pl.when(pl.program_id(1) == 0)
    def _():
        grads[...] = jnp.zeros_like(grads)

    qs, ks = rotated(
        tq[...], tk[...], hot_q[0], hot[0], cosq[...], sinq[...], cosk[...], sink[...]
    )
    tail = ones_rows(whole)
    gvs = []
    for h in heads:
        q1, q2 = split2(qs[h])
        k1, k2 = split2(ks[h])
        q_packs[h] = jnp.concatenate([q1, q1, q2, shift_rows(-logs[0, h])], axis=0)
        k_packs[h] = jnp.concatenate([k1, k2, k1, tail], axis=0)
    for h in heads:
        rows = slice(h * HDIM, (h + 1) * HDIM)
        d1, d2 = split2(datt[0, rows, :])
        cnt = counts[0, h]
        table = tv[rows, :]
        e = dot(table[:, : 2 * ROWS], d1, TN)
        e = e[:ROWS] + e[ROWS:] + dot(table[:, :ROWS], d2, TN)
        e = e - jnp.sum(e * cnt, axis=0, keepdims=True)
        e_packs[h] = stack(*split3(e), jnp.zeros((8, span), bf16))
        c1, c2 = split2(cnt)
        both = dot(jnp.concatenate([d1, d2], axis=0), c1, NT)
        gvs.append(both[:HDIM] + both[HDIM:] + dot(d1, c2, NT))

    blocks = [(h, c) for h in heads for c in range(0, span, step)]

    def products(h, c):
        at = slice(c, c + step)
        return dot(k_packs[h], q_packs[h, :, at], TN), dot(hot3[0], e_packs[h, :, at])

    ahead = products(*blocks[0])
    for i, (h, c) in enumerate(blocks):
        s, d_probs = ahead
        if i + 1 < len(blocks):
            ahead = products(*blocks[i + 1])
        s1, s2 = split2(jnp.exp2(s) * d_probs)
        at = slice(c, c + step)
        qp = q_packs[h, :, at]
        a = dot(k_packs[h, : 2 * HDIM, :], s1)
        d_q[h, :, at] = a[:HDIM] + a[HDIM:] + dot(k_packs[h, :HDIM, :], s2)
        b = dot(qp[HDIM : 3 * HDIM], s1, NT)
        b = b[:HDIM] + b[HDIM:] + dot(qp[:HDIM], s2, NT)
        if c:
            d_k[h] += b
        else:
            d_k[h] = b

    gqs, gks = [], []
    for h in heads:
        dq = turn_back(d_q[h], cosq[...], sinq[...]) * SCALE
        a = dot(jnp.concatenate(split2(dq), axis=0), hot_q[0, :ROWS, :], NT)
        gqs.append(a[:HDIM] + a[HDIM:])
    for h in heads:
        dk = turn_back(d_k[h], cosk[...], sink[...]) * (1.0 / LOG2E)
        b = dot(jnp.concatenate(split2(dk), axis=0), hot[0, :ROWS, :], NT)
        gks.append(b[:HDIM] + b[HDIM:])
    for i, gs in enumerate((gqs, gks, gvs)):
        grads[0, i] += jnp.concatenate(gs, axis=0).T


def attention_specs(crops, span, whole, first):
    group = lambda *dims: pl.BlockSpec(dims, lambda g, c, w: (first + g,) + (0,) * (len(dims) - 1))
    rope_q = pl.BlockSpec((HALF, span), lambda g, c, w: (0, w[1]))
    rope_k = pl.BlockSpec((HALF, whole), lambda g, c, w: (0, 0))
    return dict(
        table=group(128, 128),
        hot_q=pl.BlockSpec((1, 128, span), lambda g, c, w: (c, 0, w[1])),
        hot=pl.BlockSpec((1, 128, whole), lambda g, c, w: (c, 0, 0)),
        hot3=pl.BlockSpec((1, whole, 128), lambda g, c, w: (c, 0, 0)),
        rope=[rope_q, rope_q, rope_k, rope_k],
        features=pl.BlockSpec((1, 128, span), lambda g, c, w: (c, first + g, 0)),
        logs=pl.BlockSpec((1, GROUP, 1, span), lambda g, c, w: (c, first + g, 0, 0)),
        counts=pl.BlockSpec((1, GROUP, ROWS, span), lambda g, c, w: (c, first + g, 0, 0)),
    )


def attention_forward(here, tq, tk, tv, hot, cos, sin, span):
    crops, _, whole = hot.shape
    s = attention_specs(crops, span, whole, 0)
    like = jax.ShapeDtypeStruct
    return pl.pallas_call(
        forward_kernel,
        grid_spec=pltpu.PrefetchScalarGridSpec(
            num_scalar_prefetch=1,
            grid=(HEADS // GROUP, crops),
            in_specs=[s["table"]] * 3 + [s["hot_q"], s["hot"]] + s["rope"],
            out_specs=[s["features"], s["logs"], s["counts"]],
            scratch_shapes=[
                pltpu.VMEM((GROUP, 128, span), bf16),
                pltpu.VMEM((GROUP, 128, whole), bf16),
                pltpu.VMEM((GROUP, 1, span), f32),
            ],
        ),
        out_shape=[
            like((crops, HEADS * HDIM, span), f32),
            like((crops, HEADS, 1, span), f32),
            like((crops, HEADS, ROWS, span), f32),
        ],
        compiler_params=params(48),
        cost_estimate=cost(),
        name="attend",
    )(here, tq, tk, tv, hot, hot, cos, sin, cos, sin)


def attention_backward(here, tq, tk, tv, hot, hot3, cos, sin, logs, counts, datt, first, groups, chain):
    after = chain.deps()
    crops, _, whole = hot.shape
    span = datt.shape[-1]
    s = attention_specs(crops, span, whole, first)
    return chain.set(pl.pallas_call(
        backward_kernel,
        grid_spec=pltpu.PrefetchScalarGridSpec(
            num_scalar_prefetch=1,
            grid=(groups, crops),
            in_specs=[s["table"]] * 3
            + [s["hot_q"], s["hot"], s["hot3"]]
            + s["rope"]
            + [s["logs"], s["counts"], s["features"]]
            + [ANY] * len(after),
            out_specs=[pl.BlockSpec((1, 3, ROWS, 128), lambda g, c, w: (g, 0, 0, 0))],
            scratch_shapes=[
                pltpu.VMEM((GROUP, 128, span), bf16),
                pltpu.VMEM((GROUP, 128, whole), bf16),
                pltpu.VMEM((GROUP, 128, span), bf16),
                pltpu.VMEM((GROUP, HDIM, span), f32),
                pltpu.VMEM((GROUP, HDIM, whole), f32),
            ],
        ),
        out_shape=[jax.ShapeDtypeStruct((groups, 3, ROWS, 128), f32)],
        compiler_params=params(48),
        cost_estimate=cost(),
        name="attend_back",
    )(here, tq, tk, tv, hot, hot, hot3, cos, sin, cos, sin, logs, counts, datt, *after)[0])


def middle_kernel(att, wo, bo, hot3, packed, gain, shift, after, normed, weight):
    first = (pl.program_id(0) == 0) & (pl.program_id(1) == 0)

    @pl.when(first)
    def _():
        weight[0], weight[1] = split2(wo[...])

    w = (weight[0], weight[1])
    x = dot(hot3[0], packed[...]) + three(split2(att[0]), w, TN) + line(bo)
    after[...] = x
    normed[...] = norm_stats(x)[0] * line(gain) + line(shift)


def middle(here, att, wo, bo, hot3, packed, gain, shift):
    crops, width, span = att.shape
    block = min(256, span)
    steps = span // block
    full = lambda *dims: pl.BlockSpec(dims, lambda c, i, w: (0,) * len(dims))
    rows = pl.BlockSpec((block, width), lambda c, i, w: (c * steps + i, 0))
    out = jax.ShapeDtypeStruct((crops * span, width), f32)
    return pl.pallas_call(
        lambda w, *refs: middle_kernel(*refs),
        grid_spec=pltpu.PrefetchScalarGridSpec(
            num_scalar_prefetch=1,
            grid=(crops, steps),
            in_specs=[
                pl.BlockSpec((1, width, block), lambda c, i, w: (c, 0, i)),
                full(width, width),
                full(width),
                pl.BlockSpec((1, block, 128), lambda c, i, w: (c, w[1] * steps + i, 0)),
                full(128, width),
                full(width),
                full(width),
            ],
            out_specs=[rows, rows],
            scratch_shapes=[pltpu.VMEM((2, width, width), bf16)],
        ),
        out_shape=[out, out],
        compiler_params=params(32),
        cost_estimate=cost(),
        name="middle",
    )(here, att, wo, bo, hot3, packed, gain, shift)


def middle_back_kernel(
    after, d_own, d_swapped, cot, gain, att, wo, hot, clusters, biases, where, cluster, datt, keep, send,
    weight, product, sums, flat,
):
    crops, steps = pl.num_programs(0), pl.num_programs(1)
    step = pl.program_id(0) * steps + pl.program_id(1)
    width = wo.shape[0]
    tiles = width // 128

    @pl.when(step == 0)
    def _():
        weight[0], weight[1] = split2(wo[...])
        product[...] = jnp.zeros_like(product)
        sums[...] = jnp.zeros_like(sums)

    g = cot[...] * clusters[cluster[pl.program_id(0)]]
    unit, scale = norm_stats(after[...])
    d_normed = d_own[...] + d_swapped[...]
    d = g + norm_back(d_normed, unit, scale, line(gain))
    pair = split2(d)
    datt[0] = three((weight[0], weight[1]), pair, NT)
    product[...] += three(split2(att[0]), pair)
    ids = hot[0, :ROWS, :]
    sums[:ROWS] += dot(ids, pair[0]) + dot(ids, pair[1])
    vectors = [jnp.sum(v, axis=0, keepdims=True) for v in (d, d_normed * unit, d_normed, g)]
    sums[ROWS:] += jnp.concatenate(vectors + [jnp.zeros((4, width), f32)], axis=0)

    @pl.when(step == crops * steps - 1)
    def _():
        flat[...] = jnp.zeros_like(flat)
        for t in range(tiles):
            at = slice(t * 128, (t + 1) * 128)
            flat[t * width : (t + 1) * width, :] = product[:, at]
            base = tiles * width + t * (ROWS + 8)
            flat[base : base + ROWS + 8, :] = sums[:, at]
        base = tiles * (width + ROWS + 8)
        row = jnp.concatenate([b[...] for b in biases], axis=1)
        count = row.shape[1] // 128
        core = where[0]
        for t in range(count):
            flat[pl.ds(base + core * count + t, 1), :] = row[:, t * 128 : (t + 1) * 128]
        half = keep.shape[0]
        keep[...] = flat[pl.ds(pl.multiple_of(core * half, 8), half), :]
        send[...] = flat[pl.ds(pl.multiple_of((1 - core) * half, 8), half), :]


def middle_back(sides, cluster, clusters, after, d_own, d_swapped, cot, gain, att, wo, hot, biases, unit_rows, chain):
    crops, width, span = att.shape
    block = min(256, span)
    steps = span // block
    hidden = 2 * sum(b.shape[1] for b in biases)
    rows = width // 128 * (width + ROWS + 8) + hidden // 128
    rows += -rows % unit_rows
    full = lambda *dims: pl.BlockSpec(dims, lambda c, i, w, k: (0,) * len(dims))
    token = pl.BlockSpec((block, width), lambda c, i, w, k: (c * steps + i, 0))
    features = pl.BlockSpec((1, width, block), lambda c, i, w, k: (c, 0, i))
    like = jax.ShapeDtypeStruct
    deps = chain.deps()
    count = len(deps)

    def kernel(w, k, *refs):
        n = 9 + len(biases)
        middle_back_kernel(*refs[:9], refs[9:n], w, k, *refs[n + count :])

    out = pl.pallas_call(
        kernel,
        grid_spec=pltpu.PrefetchScalarGridSpec(
            num_scalar_prefetch=2,
            grid=(crops, steps),
            in_specs=[token] * 4
            + [
                full(width),
                features,
                full(width, width),
                pl.BlockSpec((1, 128, block), lambda c, i, w, k: (c, 0, w[1] * steps + i)),
            ]
            + [pl.BlockSpec(memory_space=pltpu.SMEM)]
            + [full(*b.shape) for b in biases]
            + [ANY] * count,
            out_specs=[features, full(rows // 2, 128), full(rows // 2, 128)],
            scratch_shapes=[
                pltpu.VMEM((2, width, width), bf16),
                pltpu.VMEM((width, width), f32),
                pltpu.VMEM((ROWS + 8, width), f32),
                pltpu.VMEM((rows, 128), f32),
            ],
        ),
        out_shape=[like((crops, width, span), f32)] + [like((rows // 2, 128), f32)] * 2,
        compiler_params=params(40),
        cost_estimate=cost(),
        name="middle_back",
    )(sides.array, cluster, after, d_own, d_swapped, cot, gain, att, wo, hot, clusters, *biases, *deps)
    chain.set(out[0])
    return out


BLOCK = 256


def three_wide(a, b, dims=NN):
    (i,), (j,) = dims[0]
    return dot(
        jnp.concatenate([a[0], a[0], a[1]], axis=i), jnp.concatenate([b[0], b[1], b[0]], axis=j), dims
    )


def ff_kernel(parts, unit_at, where, *refs):
    ends = 2 * len(parts)
    cluster, cluster_other = refs[:2]
    sources, clusters = refs[2:6], refs[6]
    up, up_bias, down = refs[7:10]
    outs, (bias, h1, h2, p1, p2, nh, nl, gh, gl) = refs[-9 - ends : -9], refs[-9:]

    @pl.when(pl.program_id(0) == 0)
    def _():
        half = nh.shape[0] // 2
        crops = cluster.shape[0]
        span = half // crops
        for i, source in enumerate(sources[:2]):
            at = slice(i * half, (i + 1) * half)
            nh[at], nl[at] = split2(source[...])
        for i, (source, ids) in enumerate(zip(sources[2:], (cluster, cluster_other))):
            for c in range(crops):
                at = slice(i * half + c * span, i * half + (c + 1) * span)
                gh[at], gl[at] = split2(source[c * span : (c + 1) * span] * clusters[ids[c]])

    step = pl.program_id(0)
    bias_at = pl.multiple_of(unit_at(where) + step * BLOCK, BLOCK)
    normed, grad = (nh[...], nl[...]), (gh[...], gl[...])
    up2, down2 = split2(up[...]), split2(down[...])
    u = three_wide(normed, up2) + up_bias[pl.ds(bias_at, BLOCK)].reshape(1, BLOCK)
    cdf = 0.5 * (1.0 + lax.erf(u * (0.5**0.5)))
    density = jnp.exp(-0.5 * u * u) * (1.0 / math.sqrt(2.0 * math.pi))
    ff = split2(u * cdf)
    d_pre = three_wide(grad, down2, NT) * (cdf + u * density)
    bias[...] = jnp.sum(d_pre, axis=0, keepdims=True)
    d_pre = split2(d_pre)
    h1[...], h2[...] = ff
    p1[...], p2[...] = d_pre
    g_down = three_wide(ff, grad, TN)
    g_up = three_wide(d_pre, normed, TN).T
    width = g_down.shape[1]

    def put(down_ref, up_ref):
        for t in range(width // 128):
            down_ref[t * BLOCK : (t + 1) * BLOCK, :] = g_down[:, t * 128 : (t + 1) * 128]
        for t in range(BLOCK // 128):
            up_ref[t * width : (t + 1) * width, :] = g_up[:, t * 128 : (t + 1) * 128]

    begin = 0
    for n, (split, blocks) in enumerate(parts):
        keep, send = outs[2 * n : 2 * n + 2]
        here = (step >= begin) & (step < begin + blocks)
        begin += blocks

        @pl.when(here & (where[split] == 0))
        def _():
            put(keep, send)

        @pl.when(here & (where[split] == 1))
        def _():
            put(send, keep)


def ff_chunk(sides, parts, scalars, sources, up, up_bias, down, first, buffers, chain):
    blocks = sum(count for _, count in parts)
    splits = [(sides.at(stage), count) for stage, count in parts]
    deps = chain.deps()
    width = sources[0].shape[1]
    tokens = 2 * sources[0].shape[0]
    hidden = up.shape[1]
    half = hidden // 2 // BLOCK
    slab = BLOCK * width // 128
    full = lambda *dims: pl.BlockSpec(dims, lambda j, w, *_: (0,) * len(dims))
    column = pl.BlockSpec((tokens, BLOCK), lambda j, w, *_: (0, first + j))
    like = jax.ShapeDtypeStruct
    slabs, begin = [], 0
    for _, count in parts:
        at = lambda j, w, *_, begin=begin, count=count: (jnp.clip(j - begin, 0, count - 1), 0)
        slabs += [pl.BlockSpec((slab, 128), at)] * 2
        begin += count
    out = pl.pallas_call(
        lambda *refs: ff_kernel(splits, lambda w: (w[0] * half + first) * BLOCK, *refs),
        grid_spec=pltpu.PrefetchScalarGridSpec(
            num_scalar_prefetch=1 + len(scalars),
            grid=(blocks,),
            in_specs=[full(*s.shape) if s.ndim == 2 else pl.BlockSpec(memory_space=pltpu.SMEM) for s in sources]
            + [
                pl.BlockSpec((width, BLOCK), lambda j, w, *_: (0, w[0] * half + first + j)),
                full(hidden),
                pl.BlockSpec((BLOCK, width), lambda j, w, *_: (w[0] * half + first + j, 0)),
            ]
            + [ANY] * (len(buffers) + len(deps)),
            out_specs=slabs
            + [pl.BlockSpec((1, BLOCK), lambda j, w, *_: (0, j))]
            + [column] * 4,
            scratch_shapes=[pltpu.VMEM((tokens, width), bf16)] * 4,
        ),
        out_shape=[like((slab * count, 128), f32) for _, count in parts for _ in range(2)]
        + [like((1, blocks * BLOCK), f32)]
        + [like((tokens, hidden // 2), bf16)] * 4,
        input_output_aliases={len(scalars) + len(sources) + 4 + i: 2 * len(parts) + 1 + i for i in range(len(buffers))},
        compiler_params=params(58),
        cost_estimate=cost(),
        name="feed",
    )(sides.array, *scalars, *sources, up, up_bias, down, *buffers, *deps)
    chain.set(out[0])
    return out


def back_product_kernel(dims, where, a1, a2, w, *refs):
    own, other = refs[-2:]
    step = pl.program_id(0)
    out = three_wide((a1[...], a2[...]), split2(w[...]), dims)
    half = own.shape[0]

    @pl.when(step == 0)
    def _():
        own[...] = out[:half]
        other[...] = out[half:]

    @pl.when(step > 0)
    def _():
        own[...] += out[:half]
        other[...] += out[half:]


def back_product(sides, a, weight, dims, chain):
    tokens, units = a[0].shape
    deps = chain.deps()
    wide = 5 * BLOCK // 2 if units % (5 * BLOCK) == 0 else BLOCK
    steps = units // wide
    up_like = dims is NT
    width = weight.shape[0 if up_like else 1]
    out = jax.ShapeDtypeStruct((tokens // 2, width), f32)
    spec = (
        pl.BlockSpec((width, wide), lambda j, w: (0, w[0] * steps + j))
        if up_like
        else pl.BlockSpec((wide, width), lambda j, w: (w[0] * steps + j, 0))
    )
    out = pl.pallas_call(
        lambda *refs: back_product_kernel(dims, *refs),
        grid_spec=pltpu.PrefetchScalarGridSpec(
            num_scalar_prefetch=1,
            grid=(steps,),
            in_specs=[pl.BlockSpec((tokens, wide), lambda j, w: (0, j))] * 2 + [spec] + [ANY] * len(deps),
            out_specs=[pl.BlockSpec((tokens // 2, width), lambda j, w: (0, 0))] * 2,
        ),
        out_shape=[out, out],
        compiler_params=params(48),
        cost_estimate=cost(),
        name="feed_back" if up_like else "feed_out",
    )(sides.array, *a, weight, *deps)
    chain.set(out[0])
    return out


class Chain:
    def __init__(self):
        self.last = []

    def deps(self):
        return list(self.last)

    def set(self, out):
        self.last = [out]
        return out


def bits_of(axis):
    size = lax.axis_size(axis)
    return [(axis, 1 << i) for i in range(size.bit_length() - 1)]


def swap(x, stage):
    axis, bit = stage
    return lax.ppermute(x, axis, [(i, i ^ bit) for i in range(lax.axis_size(axis))])


def side(stage):
    axis, bit = stage
    return ((lax.axis_index(axis) // bit) % 2).astype(jnp.int32)


class Sides:
    def __init__(self, core_stage, stages):
        self.stages = list(dict.fromkeys(stages))
        self.core_at = 2 + self.stages.index(core_stage)
        self.array = jnp.stack(
            [side(core_stage), lax.axis_index("seq").astype(jnp.int32)] + [side(s) for s in self.stages]
        )

    def at(self, stage):
        return 2 + self.stages.index(stage)


def add_split_kernel(where, k_here, r_here, k_away, r_away, *refs):
    keep, send = refs[-2:]
    keep[...] = k_here[...] + r_here[...]
    send[...] = k_away[...] + r_away[...]


def add_split(kept, received, sides, stage, chain):
    rows, lanes = kept.shape
    half = rows // 2
    at = sides.at(stage)
    if half % 8:
        total = kept + received
        me = side(stage)
        return (
            lax.dynamic_slice_in_dim(total, me * half, half, 0),
            lax.dynamic_slice_in_dim(total, (1 - me) * half, half, 0),
        )
    deps = chain.deps()
    steps = 2 if half % 16 == 0 and half >= 512 else 1
    block = (half // steps, lanes)
    here = pl.BlockSpec(block, lambda i, w: (w[at] * steps + i, 0))
    away = pl.BlockSpec(block, lambda i, w: ((1 - w[at]) * steps + i, 0))
    plain = pl.BlockSpec(block, lambda i, w: (i, 0))
    out = jax.ShapeDtypeStruct((half, lanes), f32)
    keep, send = pl.pallas_call(
        add_split_kernel,
        grid_spec=pltpu.PrefetchScalarGridSpec(
            num_scalar_prefetch=1,
            grid=(steps,),
            in_specs=[here, here, away, away] + [ANY] * len(deps),
            out_specs=[plain, plain],
        ),
        out_shape=[out, out],
        compiler_params=params(16),
        cost_estimate=cost(STEP),
        name="add_split",
    )(sides.array, kept, received, kept, received, *deps)
    chain.set(keep)
    return keep, send


def add_kernel(a, b, *refs):
    refs[-1][...] = a[...] + b[...]


def add(a, b, chain):
    deps = chain.deps()
    full = pl.BlockSpec(a.shape, lambda: (0,) * a.ndim)
    return chain.set(
        pl.pallas_call(
            add_kernel,
            in_specs=[full, full] + [ANY] * len(deps),
            out_specs=full,
            out_shape=jax.ShapeDtypeStruct(a.shape, f32),
            compiler_params=params(16),
            cost_estimate=cost(STEP),
            name="add",
        )(a, b, *deps)
    )


def join_kernel(at, where, x, other, *refs):
    out = refs[-1]
    mine = pl.program_id(0) == where[at]

    @pl.when(mine)
    def _():
        out[...] = x[...]

    @pl.when(jnp.logical_not(mine))
    def _():
        out[...] = other[...]


def join(x, other, sides, stage, chain):
    if x.shape[0] % 8:
        return jnp.where(
            side(stage) == 0, jnp.concatenate([x, other], axis=0), jnp.concatenate([other, x], axis=0)
        )
    deps = chain.deps()
    at = sides.at(stage)
    full = pl.BlockSpec(x.shape, lambda i, w: (0, 0))
    return chain.set(
        pl.pallas_call(
            lambda *refs: join_kernel(at, *refs),
            grid_spec=pltpu.PrefetchScalarGridSpec(
                num_scalar_prefetch=1,
                grid=(2,),
                in_specs=[full, full] + [ANY] * len(deps),
                out_specs=pl.BlockSpec(x.shape, lambda i, w: (i, 0)),
            ),
            out_shape=jax.ShapeDtypeStruct((2 * x.shape[0], x.shape[1]), f32),
            compiler_params=params(16),
            cost_estimate=cost(STEP),
            name="join",
        )(sides.array, x, other, *deps)
    )


class Sum:
    def __init__(self, keep, send, stages, sides, chain, flat=1):
        self.x, self.stages, self.sides, self.chain = keep, stages, sides, chain
        self.cut = len(stages) - flat
        self.moves = list(range(len(stages))) + list(reversed(range(self.cut)))
        self.at = 0
        self.coming = swap(send, stages[0])

    def step(self):
        done = self.at
        self.at += 1
        stage = self.stages[self.moves[self.at]]
        if self.at < self.cut:
            self.x, send = add_split(self.x, self.coming, self.sides, stage, self.chain)
        elif done < len(self.stages):
            self.x = send = add(self.x, self.coming, self.chain)
        else:
            self.x = send = join(self.x, self.coming, self.sides, self.stages[self.moves[done]], self.chain)
        self.coming = swap(send, stage)

    @property
    def left(self):
        return len(self.moves) - 1 - self.at

    def whole(self):
        return join(self.x, self.coming, self.sides, self.stages[0], self.chain)


def place_kernel(split, items, first, blocks, width, half, where, *refs):
    down, up, sems = refs[-3:]
    tiles = width // 128

    def copies(side):
        out = []
        for i, (mine, own) in enumerate(items):
            base = pl.multiple_of((where[0] if mine else 1 - where[0]) * half + first * BLOCK, BLOCK)
            if own == (side == 0):
                for n in range(blocks * tiles):
                    rows = pl.ds(pl.multiple_of(base + n // tiles * BLOCK, BLOCK), BLOCK)
                    out.append((refs[i].at[pl.ds(n * BLOCK, BLOCK), :], down.at[rows, pl.ds(n % tiles * 128, 128)]))
            else:
                for n in range(blocks * BLOCK // 128):
                    at = pl.multiple_of(base + n * 128, 128)
                    out.append((refs[i].at[pl.ds(n * width, width), :], up.at[:, pl.ds(at, 128)]))
        return [pltpu.make_async_copy(a, b, sems.at[n]) for n, (a, b) in enumerate(out)]

    for side in range(2):

        @pl.when(where[split] == side)
        def _():
            moving = copies(side)
            for m in moving:
                m.start()
            for m in moving:
                m.wait()


def place(sides, stage, items, first, blocks, width, hidden, buffers, chain):
    split = sides.at(stage)
    deps = chain.deps()
    kinds = [(mine, own) for _, mine, own in items]
    arrays = [x for x, _, _ in items]
    most = len(items) * blocks * max(width, BLOCK) // 128
    outs = pl.pallas_call(
        lambda *refs: place_kernel(split, kinds, first, blocks, width, hidden // 2, *refs),
        grid_spec=pltpu.PrefetchScalarGridSpec(
            num_scalar_prefetch=1,
            grid=(1,),
            in_specs=[ANY] * (len(arrays) + len(buffers) + len(deps)),
            out_specs=[ANY, ANY],
            scratch_shapes=[pltpu.SemaphoreType.DMA((most,))],
        ),
        out_shape=[
            jax.ShapeDtypeStruct((hidden, width), f32),
            jax.ShapeDtypeStruct((width, hidden), f32),
        ],
        input_output_aliases={1 + len(arrays) + i: i for i in range(len(buffers))},
        compiler_params=params(8),
        cost_estimate=cost(STEP),
        name="place",
    )(sides.array, *arrays, *buffers, *deps)
    chain.set(arrays[0])
    return outs


FLAT = dict(a=1, b=1, c=2, d=2)
ROUTES = dict(a="xyzw", b="zxyw", c="yzxw", d="kyzwx", e="kxzwy")

PLAN = " ".join(
    [
        "feed_a", "feed_bc", "back", "a", "middle", "attend0", "b", "a", "d", "c", "attend1", "a", "b", "d",
        "attend2", "b", "attend3", "c", "d", "a", "attend4", "tables", "b", "e", "c", "d", "a", "e", "b", "d",
        "e", "c", "d", "a", "b", "e", "c", "d", "e", "Ec", "out", "La", "Lc", "finish", "Eb", "Lb", "Pa", "Pb",
        "Ea", "Pc",
    ]
)


def local(
    token_ids,
    embedding,
    first_gain,
    first_shift,
    query_weight,
    query_bias,
    key_weight,
    key_bias,
    value_weight,
    value_bias,
    out_weight,
    out_bias,
    second_gain,
    second_shift,
    up_weight,
    up_bias,
    down_weight,
    down_bias,
    cotangent,
    crop_cluster,
    cluster_weight,
):
    crops, span = token_ids.shape
    width = embedding.shape[1]
    units = up_weight.shape[1]
    ring = lax.axis_size("seq")
    whole = span * ring
    seq_bits, crop_bits = bits_of("seq"), bits_of("crop")
    core_stage, across, along = crop_bits[0], crop_bits[1:2], crop_bits[2:]
    axes = dict(x=across, y=seq_bits, z=along[:1], w=along[1:], k=[core_stage])
    route = {name: sum((axes[axis] for axis in path), []) for name, path in ROUTES.items()}
    sides = Sides(core_stage, seq_bits + crop_bits)
    chain = Chain()

    if ring == 2:
        ids = [token_ids, swap(token_ids, ("seq", 1))]
    else:
        ids = [lax.all_gather(token_ids, "seq", axis=1, tiled=True)]
    cot = cotangent.reshape(-1, width)
    cot_other = swap(cot, core_stage)
    cluster_other = swap(crop_cluster, core_stage)

    frequency = (10000.0 ** (-2.0 * np.arange(HALF) / HDIM)).astype(np.float32)
    angles = (frequency[:, None] * np.arange(whole, dtype=np.float32)[None, :]).astype(np.float64)
    cos, sin = jnp.asarray(np.cos(angles), f32), jnp.asarray(np.sin(angles), f32)

    tq, tk, tv, packed = project_rows(
        embedding, first_gain, first_shift, query_weight, query_bias, key_weight, key_bias, value_weight, value_bias
    )
    hot, hot3 = spots(sides, ids, whole, [tq])
    att, logs, counts = attention_forward(sides.array, tq, tk, tv, hot, cos, sin, span)
    after_attn, normed = middle(sides.array, att, out_weight, out_bias, hot3, packed, second_gain, second_shift)

    sources = [normed, swap(normed, core_stage), cot, cot_other, cluster_weight]
    scalars = [crop_cluster, cluster_other]
    blocks = units // 2 // BLOCK
    third = 2 * (blocks // 5)
    spans = {}
    first = 0
    for name, count in (("a", third), ("b", third), ("c", blocks - 2 * third)):
        spans[name] = (first, count, route[name])
        first += count
    devices = lax.axis_size("seq") * lax.axis_size("crop")

    sums, biases, tables, early, late, outs, buffers = {}, [], [], {}, {}, [], []

    def step(name):
        total = sums[name]
        if total.left:
            total.step()
            if name in spans and not total.left:
                early[name] = swap(total.x, core_stage)

    def complete(*names):
        while any(sums[name].left for name in names):
            for name in names:
                step(name)

    def put(name, items):
        first, count, stages = spans[name]
        return place(sides, stages[0], items, first, count, width, units, outs, chain)

    for item in PLAN.split():
        kind, name = item.rstrip("01234"), item[-1]
        if item in sums:
            step(item)
        elif kind[0] == "E":
            complete(name)
            outs = put(name, [(early[name], False, True), (sums[name].x, True, True)])
        elif kind[0] == "L":
            complete(name)
            late[name] = swap(sums[name].coming, core_stage)
        elif kind[0] == "P":
            outs = put(name, [(late[name], False, False), (sums[name].coming, True, False)])
        elif kind == "finish":
            complete("d", "e")
            table, rest = sums["e"].whole(), sums["d"].whole()
            g_wq, g_wk, g_wv, g_ow, g_bq, g_bk, g_bv, g_emb, g_gain, g_shift, g_ob, g_sg, g_ss, g_db, g_ub = finish(
                embedding, first_gain, first_shift, table, rest, query_weight, key_weight, value_weight, units, chain
            )
        elif kind.startswith("feed"):
            names = item[5:]
            out = ff_chunk(
                sides, [(route[n][0], spans[n][1]) for n in names], scalars, sources, up_weight, up_bias, down_weight,
                spans[names[0]][0], buffers, chain,
            )
            for n in names:
                keep, send, *out = out
                sums[n] = Sum(keep, send, route[n], sides, chain, FLAT[n])
            bias, *buffers = out
            biases.append(bias)
        elif kind == "back":
            h1, h2, p1, p2 = buffers
            d_own, d_other = back_product(sides, (p1, p2), up_weight, NT, chain)
            d_swapped = swap(d_other, core_stage)
        elif kind == "middle":
            d_att, keep, send = middle_back(
                sides, crop_cluster, cluster_weight, after_attn, d_own, d_swapped, cot, second_gain, att, out_weight,
                hot, biases, 8 * devices, chain,
            )
            sums["d"] = Sum(keep, send, route["d"], sides, chain, FLAT["d"])
        elif kind == "attend":
            tables.append(
                attention_backward(
                    sides.array, tq, tk, tv, hot, hot3, cos, sin, logs, counts, d_att, int(name), 1, chain
                )
            )
        elif kind == "tables":
            sums["e"] = Sum(*pack_tables(sides, tables, 16, chain), route["e"], sides, chain, len(route["e"]) - 1)
        elif kind == "out":
            o_own, o_other = back_product(sides, (h1, h2), down_weight, NN, chain)
            o_swapped = swap(o_other, core_stage)
            block_out = (after_attn + o_own + o_swapped + down_bias).reshape(cotangent.shape)
    g_dw, g_uw = outs
    return (
        block_out, g_emb, g_gain, g_shift, g_wq, g_bq, g_wk, g_bk, g_wv, g_bv, g_ow, g_ob, g_sg, g_ss, g_uw, g_ub,
        g_dw, g_db,
    )


def solution(mesh):
    in_specs = (
        (P("crop", "seq"),) + (P(),) * 17 + (P("crop", "seq", None), P("crop"), P())
    )
    out_specs = (P("crop", "seq", None),) + (P(),) * 17
    return jax.shard_map(local, mesh=mesh, in_specs=in_specs, out_specs=out_specs, check_vma=False)
```

```python
import math
import jax
import jax.numpy as jnp
import numpy as np
from jax import lax
from jax.experimental import pallas as pl
from jax.experimental.pallas import tpu as pltpu
from jax.sharding import PartitionSpec as P

HEADS = 20
HDIM = 32
HALF = 16
VOCAB = 33
ROWS = 40
GROUP = 4
f32 = jnp.float32
bf16 = jnp.bfloat16
epsilon = 1e-05
LOG2E = 1.0 / math.log(2.0)
SCALE = HDIM**-0.5

NN = (((1,), (0,)), ((), ()))
NT = (((1,), (1,)), ((), ()))
TN = (((0,), (0,)), ((), ()))
ANY = pl.BlockSpec(memory_space=pl.ANY)


def params(mib):
    return pltpu.CompilerParams(vmem_limit_bytes=mib << 20)


def cost(flops=2000000000):
    return pl.CostEstimate(flops=flops, bytes_accessed=0, transcendentals=0)


STEP = 10000000000


def dot(a, b, dims=NN):
    return lax.dot_general(a, b, dims, preferred_element_type=f32)


def split2(x):
    head = x.astype(bf16)
    return head, (x - head.astype(f32)).astype(bf16)


def split3(x):
    head = x.astype(bf16)
    x = x - head.astype(f32)
    mid = x.astype(bf16)
    return head, mid, (x - mid.astype(f32)).astype(bf16)


def three(a, b, dims=NN):
    return dot(a[0], b[0], dims) + dot(a[0], b[1], dims) + dot(a[1], b[0], dims)


def turn(u, cos, sin):
    a, b = u[:HALF], u[HALF:]
    return jnp.concatenate([a * cos - b * sin, b * cos + a * sin], axis=0)


def turn_back(u, cos, sin):
    a, b = u[:HALF], u[HALF:]
    return jnp.concatenate([a * cos + b * sin, b * cos - a * sin], axis=0)


def stack(*rows):
    return jnp.concatenate([r.astype(f32) for r in rows], axis=0).astype(bf16)


def norm_stats(x):
    centred = x - jnp.mean(x, axis=-1, keepdims=True)
    scale = lax.rsqrt(jnp.mean(centred * centred, axis=-1, keepdims=True) + epsilon)
    return centred * scale, scale


def norm_back(d_normed, unit, scale, gain):
    d = d_normed * gain
    d = d - jnp.mean(d, axis=-1, keepdims=True) - unit * jnp.mean(d * unit, axis=-1, keepdims=True)
    return d * scale


def tall(emb):
    return jnp.concatenate([emb, jnp.zeros((ROWS - VOCAB, emb.shape[1]), f32)], axis=0)


def line(v):
    return v[...].reshape(1, -1)


def rows_kernel(emb, gain, shift, wq, bq, wk, bk, wv, bv, tq, tk, tv, packed, normed):
    width = emb.shape[1]
    step = pl.program_id(0)

    @pl.when(step == 0)
    def _():
        rows = tall(emb[...])
        unit, _ = norm_stats(rows)
        normed[...] = stack(*split2(unit * line(gain) + line(shift)))
        packed[...] = stack(*split3(rows), jnp.zeros((8, width), bf16))

    full = normed[...]
    real = lax.broadcasted_iota(jnp.int32, (ROWS, 128), 0) < VOCAB

    def table(w, b):
        w1, w2 = split2(w[...])
        by1 = dot(full, w1)
        t = by1[:ROWS] + (by1[ROWS:] + dot(full[:ROWS], w2))
        bias = b[pl.ds(pl.multiple_of(step * 128, 128), 128)].reshape(1, 128)
        return jnp.where(real, t + bias, 0.0)

    def lay(a, b, c):
        blank = jnp.zeros((8, 128), f32)
        return jnp.concatenate([a.astype(f32), b.astype(f32), c.astype(f32), blank], axis=0).T.astype(bf16)

    q, k, v = table(wq, bq), table(wk, bk), table(wv, bv)
    tq[...] = lay(*split3(q))
    tk[...] = lay(*split3(k))
    v1, v2 = split2(v)
    tv[...] = lay(v1, v2, v1)


def project_rows(emb, gain, shift, wq, bq, wk, bk, wv, bv):
    width = emb.shape[1]
    full = lambda *dims: pl.BlockSpec(dims, lambda i: (0,) * len(dims))
    weight = pl.BlockSpec((width, 128), lambda i: (0, i))
    table = pl.BlockSpec((128, 128), lambda i: (i, 0))
    like = jax.ShapeDtypeStruct
    return pl.pallas_call(
        rows_kernel,
        grid=(width // 128,),
        in_specs=[full(VOCAB, width), full(width), full(width)] + [weight, full(width)] * 3,
        out_specs=[table] * 3 + [full(128, width)],
        out_shape=[like((width, 128), bf16)] * 3 + [like((128, width), bf16)],
        scratch_shapes=[pltpu.VMEM((2 * ROWS, width), bf16)],
        compiler_params=params(60),
        cost_estimate=cost(),
        name="rows",
    )(emb, gain, shift, wq, bq, wk, bk, wv, bv)


def spots_kernel(count, where, *refs):
    ids, (hot, hot3) = refs[:count], refs[-2:]
    crops, span = ids[0].shape
    spot = lax.broadcasted_iota(jnp.int32, (128, span), 0)
    code = jnp.where(
        spot < ROWS, spot, jnp.where(spot < 2 * ROWS, spot - ROWS, jnp.where(spot < 3 * ROWS, spot - 2 * ROWS, -1))
    )
    for n in range(count):
        at = 0 if count == 1 else pl.multiple_of((where[1] if n == 0 else 1 - where[1]) * span, span)
        for c in range(crops):
            spots = jnp.where(ids[n][c : c + 1, :] == code, 1.0, 0.0)
            hot[c, :, pl.ds(at, span)] = spots.astype(bf16)
            hot3[c, pl.ds(at, span), :] = spots.T.astype(bf16)


def spots(sides, ids, whole, deps):
    crops = ids[0].shape[0]
    full = lambda *dims: pl.BlockSpec(dims, lambda i, w: (0,) * len(dims))
    count = len(ids)
    like = jax.ShapeDtypeStruct
    return pl.pallas_call(
        lambda *refs: spots_kernel(count, *refs),
        grid_spec=pltpu.PrefetchScalarGridSpec(
            num_scalar_prefetch=1,
            grid=(1,),
            in_specs=[full(*i.shape) for i in ids] + [ANY] * len(deps),
            out_specs=[full(crops, 128, whole), full(crops, whole, 128)],
        ),
        out_shape=[like((crops, 128, whole), bf16), like((crops, whole, 128), bf16)],
        compiler_params=params(32),
        cost_estimate=cost(),
        name="spots",
    )(sides.array, *ids, *deps)


def finish_kernel(
    emb, gain, shift, table, rest, wq, wk, wv, g_wq, g_wk, g_wv, g_ow, g_bq, g_bk, g_bv, g_emb, g_gain, g_shift, g_ob,
    g_sg, g_ss, g_db, g_ub, normed, d_normed,
):
    step = pl.program_id(0)
    width = emb.shape[1]
    tiles = width // 128

    @pl.when(step == 0)
    def _():
        unit, _ = norm_stats(tall(emb[...]))
        n1, n2 = split2(unit * line(gain) + line(shift))
        normed[...] = stack(n1, n1, n2, jnp.zeros((8, n1.shape[1]), bf16))
        d_normed[...] = jnp.zeros_like(d_normed)

    blank = jnp.zeros((8, 128), bf16)
    at = pl.ds(pl.multiple_of(step * 128, 128), 128)
    for i, (w, out, bias) in enumerate(((wq, g_wq, g_bq), (wk, g_wk, g_bk), (wv, g_wv, g_bv))):
        g = table[i * ROWS : (i + 1) * ROWS, :]
        g1, g2 = split2(g)
        out[...] = dot(normed[...], stack(g1, g2, g1, blank), TN)
        bias[at] = jnp.sum(g, axis=0)
        d_normed[...] += three((g1, g2), split2(w[...]), NT)
    g_ow[...] = rest[pl.ds(pl.multiple_of(step * width, 128), width), :]

    @pl.when(step == pl.num_programs(0) - 1)
    def _():
        unit, scale = norm_stats(tall(emb[...]))
        d = d_normed[...]
        g_gain[...] = jnp.sum(d * unit, axis=0)
        g_shift[...] = jnp.sum(d, axis=0)
        back = norm_back(d, unit, scale, line(gain))
        for t in range(tiles):
            at = slice(t * 128, (t + 1) * 128)
            base = tiles * width + t * (ROWS + 8)
            g_emb[:, at] = (back[:, at] + rest[base : base + ROWS, :])[:VOCAB]
            for i, out in enumerate((g_ob, g_sg, g_ss, g_db)):
                out[at] = rest[base + ROWS + i, :]
        base = tiles * (width + ROWS + 8)
        for t in range(g_ub.shape[0] // 128):
            g_ub[t * 128 : (t + 1) * 128] = rest[base + t, :]


def finish(emb, gain, shift, table, rest, wq, wk, wv, hidden, chain):
    width = emb.shape[1]
    full = lambda *dims: pl.BlockSpec(dims, lambda i: (0,) * len(dims))
    weight = pl.BlockSpec((width, 128), lambda i: (0, i))
    like = jax.ShapeDtypeStruct
    deps = chain.deps()
    vector, square = like((width,), f32), like((width, width), f32)

    def kernel(*refs):
        finish_kernel(*refs[:8], *refs[8 + len(deps) :])

    out = pl.pallas_call(
        kernel,
        grid=(width // 128,),
        in_specs=[full(VOCAB, width), full(width), full(width)]
        + [pl.BlockSpec((3 * ROWS, 128), lambda i: (i, 0)), full(*rest.shape)]
        + [weight] * 3
        + [ANY] * len(deps),
        out_specs=[weight] * 4 + [full(width)] * 3 + [full(VOCAB, width)] + [full(width)] * 6 + [full(hidden)],
        out_shape=[square] * 4 + [vector] * 3 + [like((VOCAB, width), f32)] + [vector] * 6 + [like((hidden,), f32)],
        scratch_shapes=[pltpu.VMEM((128, width), bf16), pltpu.VMEM((ROWS, width), f32)],
        compiler_params=params(32),
        cost_estimate=cost(),
        name="finish",
    )(emb, gain, shift, table, rest, wq, wk, wv, *deps)
    chain.set(out[0])
    return out


def pack_kernel(where, *refs):
    keep, send, flat = refs[-3:]
    flat[...] = jnp.zeros_like(flat)
    at = 0
    for table in refs[:-3]:
        for g in range(table.shape[0]):
            for i in range(3):
                flat[at : at + ROWS, :] = table[g, i]
                at += ROWS
    half = keep.shape[0]
    keep[...] = flat[pl.ds(pl.multiple_of(where[0] * half, 8), half), :]
    send[...] = flat[pl.ds(pl.multiple_of((1 - where[0]) * half, 8), half), :]


def pack_tables(sides, tables, unit_rows, chain):
    rows = 3 * ROWS * sum(t.shape[0] for t in tables)
    rows += -rows % unit_rows
    full = lambda *dims: pl.BlockSpec(dims, lambda i, w: (0,) * len(dims))
    half = jax.ShapeDtypeStruct((rows // 2, 128), f32)
    out = pl.pallas_call(
        pack_kernel,
        grid_spec=pltpu.PrefetchScalarGridSpec(
            num_scalar_prefetch=1,
            grid=(1,),
            in_specs=[full(*t.shape) for t in tables],
            out_specs=[full(*half.shape)] * 2,
            scratch_shapes=[pltpu.VMEM((rows, 128), f32)],
        ),
        out_shape=[half, half],
        compiler_params=params(16),
        cost_estimate=cost(STEP),
        name="pack",
    )(sides.array, *tables)
    chain.set(out[0])
    return out


def rotated(tq, tk, hot_q, hot, cosq, sinq, cosk, sink):
    q = dot(tq, hot_q)
    k = dot(tk, hot)
    heads = [slice(h * HDIM, (h + 1) * HDIM) for h in range(GROUP)]
    qs = [turn(q[h], cosq, sinq) * (SCALE * LOG2E) for h in heads]
    ks = [turn(k[h], cosk, sink) for h in heads]
    return qs, ks


def shift_rows(shift):
    s1, s2, s3 = split3(shift)
    row = lax.broadcasted_iota(jnp.int32, (HDIM, shift.shape[1]), 0)
    s1, s2, s3 = s1.astype(f32), s2.astype(f32), s3.astype(f32)
    return jnp.where(row == 0, s1, jnp.where(row == 1, s2, jnp.where(row == 2, s3, 0.0))).astype(bf16)


def ones_rows(n):
    return jnp.where(lax.broadcasted_iota(jnp.int32, (HDIM, n), 0) < 3, 1.0, 0.0).astype(bf16)


def forward_kernel(
    here, tq, tk, tv, hot_q, hot, cosq, sinq, cosk, sink, att, logs, counts, q_packs, k_packs, shifts
):
    span = hot_q.shape[-1]
    whole = hot.shape[-1]
    step = min(256, span)
    ids = hot[0, :ROWS, :]
    heads = range(GROUP)
    blocks = [(h, slice(c, c + step)) for h in heads for c in range(0, span, step)]

    qs, ks = rotated(
        tq[...], tk[...], hot_q[0], hot[0], cosq[...], sinq[...], cosk[...], sink[...]
    )
    tail = ones_rows(whole)
    for h in heads:
        q, k = qs[h], ks[h]
        longest = jnp.max(jnp.sum(k * k, axis=0, keepdims=True), axis=1, keepdims=True)
        bound = jnp.sqrt(jnp.sum(q * q, axis=0, keepdims=True) * longest)
        shifts[h] = bound
        q1, q2 = split2(q)
        k1, k2 = split2(k)
        q_packs[h] = jnp.concatenate([q1, q1, q2, shift_rows(-bound)], axis=0)
        k_packs[h] = jnp.concatenate([k1, k2, k1, tail], axis=0)

    score = lambda h, at: dot(k_packs[h], q_packs[h, :, at], TN)
    ahead = score(*blocks[0])
    for i, (h, at) in enumerate(blocks):
        s = ahead
        if i + 1 < len(blocks):
            ahead = score(*blocks[i + 1])
        p1, p2 = split2(jnp.exp2(s))
        counts[0, h, :, at] = dot(ids, p1) + dot(ids, p2)

    low = [jnp.min(jnp.sum(counts[0, h], axis=0, keepdims=True)) for h in heads]

    @pl.when(jnp.logical_not(jnp.minimum(jnp.minimum(low[0], low[1]), jnp.minimum(low[2], low[3])) > 1e-25))
    def _():
        for h, at in blocks:
            qp = q_packs[h, :, at]
            s = dot(k_packs[h, : 3 * HDIM, :], qp[: 3 * HDIM], TN)
            top = jnp.max(s, axis=0, keepdims=True)
            p1, p2 = split2(jnp.exp2(s - top))
            counts[0, h, :, at] = dot(ids, p1) + dot(ids, p2)
            shifts[h, :, at] = top

    for h in heads:
        cnt = counts[0, h]
        total = jnp.sum(cnt, axis=0, keepdims=True)
        cnt = cnt / total
        counts[0, h] = cnt
        logs[0, h] = shifts[h] + jnp.log2(total)
        c1, c2 = split2(cnt)
        rows = slice(h * HDIM, (h + 1) * HDIM)
        att[0, rows, :] = dot(tv[rows, : 3 * ROWS], stack(c1, c1, c2))


def backward_kernel(
    here, tq, tk, tv, hot_q, hot, hot3, cosq, sinq, cosk, sink, logs, counts, datt, *refs
):
    grads, q_packs, k_packs, e_packs, d_q, d_k = refs[-6:]
    span = hot_q.shape[-1]
    whole = hot.shape[-1]
    step = min(256, span)
    heads = range(GROUP)

    @pl.when(pl.program_id(1) == 0)
    def _():
        grads[...] = jnp.zeros_like(grads)

    qs, ks = rotated(
        tq[...], tk[...], hot_q[0], hot[0], cosq[...], sinq[...], cosk[...], sink[...]
    )
    tail = ones_rows(whole)
    gvs = []
    for h in heads:
        q1, q2 = split2(qs[h])
        k1, k2 = split2(ks[h])
        q_packs[h] = jnp.concatenate([q1, q1, q2, shift_rows(-logs[0, h])], axis=0)
        k_packs[h] = jnp.concatenate([k1, k2, k1, tail], axis=0)
    for h in heads:
        rows = slice(h * HDIM, (h + 1) * HDIM)
        d1, d2 = split2(datt[0, rows, :])
        cnt = counts[0, h]
        table = tv[rows, :]
        e = dot(table[:, : 2 * ROWS], d1, TN)
        e = e[:ROWS] + e[ROWS:] + dot(table[:, :ROWS], d2, TN)
        e = e - jnp.sum(e * cnt, axis=0, keepdims=True)
        e_packs[h] = stack(*split3(e), jnp.zeros((8, span), bf16))
        c1, c2 = split2(cnt)
        both = dot(jnp.concatenate([d1, d2], axis=0), c1, NT)
        gvs.append(both[:HDIM] + both[HDIM:] + dot(d1, c2, NT))

    blocks = [(h, c) for h in heads for c in range(0, span, step)]

    def products(h, c):
        at = slice(c, c + step)
        return dot(k_packs[h], q_packs[h, :, at], TN), dot(hot3[0], e_packs[h, :, at])

    ahead = products(*blocks[0])
    for i, (h, c) in enumerate(blocks):
        s, d_probs = ahead
        if i + 1 < len(blocks):
            ahead = products(*blocks[i + 1])
        s1, s2 = split2(jnp.exp2(s) * d_probs)
        at = slice(c, c + step)
        qp = q_packs[h, :, at]
        a = dot(k_packs[h, : 2 * HDIM, :], s1)
        d_q[h, :, at] = a[:HDIM] + a[HDIM:] + dot(k_packs[h, :HDIM, :], s2)
        b = dot(qp[HDIM : 3 * HDIM], s1, NT)
        b = b[:HDIM] + b[HDIM:] + dot(qp[:HDIM], s2, NT)
        if c:
            d_k[h] += b
        else:
            d_k[h] = b

    gqs, gks = [], []
    for h in heads:
        dq = turn_back(d_q[h], cosq[...], sinq[...]) * SCALE
        a = dot(jnp.concatenate(split2(dq), axis=0), hot_q[0, :ROWS, :], NT)
        gqs.append(a[:HDIM] + a[HDIM:])
    for h in heads:
        dk = turn_back(d_k[h], cosk[...], sink[...]) * (1.0 / LOG2E)
        b = dot(jnp.concatenate(split2(dk), axis=0), hot[0, :ROWS, :], NT)
        gks.append(b[:HDIM] + b[HDIM:])
    for i, gs in enumerate((gqs, gks, gvs)):
        grads[0, i] += jnp.concatenate(gs, axis=0).T


def attention_specs(crops, span, whole, first):
    group = lambda *dims: pl.BlockSpec(dims, lambda g, c, w: (first + g,) + (0,) * (len(dims) - 1))
    rope_q = pl.BlockSpec((HALF, span), lambda g, c, w: (0, w[1]))
    rope_k = pl.BlockSpec((HALF, whole), lambda g, c, w: (0, 0))
    return dict(
        table=group(128, 128),
        hot_q=pl.BlockSpec((1, 128, span), lambda g, c, w: (c, 0, w[1])),
        hot=pl.BlockSpec((1, 128, whole), lambda g, c, w: (c, 0, 0)),
        hot3=pl.BlockSpec((1, whole, 128), lambda g, c, w: (c, 0, 0)),
        rope=[rope_q, rope_q, rope_k, rope_k],
        features=pl.BlockSpec((1, 128, span), lambda g, c, w: (c, first + g, 0)),
        logs=pl.BlockSpec((1, GROUP, 1, span), lambda g, c, w: (c, first + g, 0, 0)),
        counts=pl.BlockSpec((1, GROUP, ROWS, span), lambda g, c, w: (c, first + g, 0, 0)),
    )


def attention_forward(here, tq, tk, tv, hot, cos, sin, span):
    crops, _, whole = hot.shape
    s = attention_specs(crops, span, whole, 0)
    like = jax.ShapeDtypeStruct
    return pl.pallas_call(
        forward_kernel,
        grid_spec=pltpu.PrefetchScalarGridSpec(
            num_scalar_prefetch=1,
            grid=(HEADS // GROUP, crops),
            in_specs=[s["table"]] * 3 + [s["hot_q"], s["hot"]] + s["rope"],
            out_specs=[s["features"], s["logs"], s["counts"]],
            scratch_shapes=[
                pltpu.VMEM((GROUP, 128, span), bf16),
                pltpu.VMEM((GROUP, 128, whole), bf16),
                pltpu.VMEM((GROUP, 1, span), f32),
            ],
        ),
        out_shape=[
            like((crops, HEADS * HDIM, span), f32),
            like((crops, HEADS, 1, span), f32),
            like((crops, HEADS, ROWS, span), f32),
        ],
        compiler_params=params(48),
        cost_estimate=cost(),
        name="attend",
    )(here, tq, tk, tv, hot, hot, cos, sin, cos, sin)


def attention_backward(here, tq, tk, tv, hot, hot3, cos, sin, logs, counts, datt, first, groups, chain):
    after = chain.deps()
    crops, _, whole = hot.shape
    span = datt.shape[-1]
    s = attention_specs(crops, span, whole, first)
    return chain.set(pl.pallas_call(
        backward_kernel,
        grid_spec=pltpu.PrefetchScalarGridSpec(
            num_scalar_prefetch=1,
            grid=(groups, crops),
            in_specs=[s["table"]] * 3
            + [s["hot_q"], s["hot"], s["hot3"]]
            + s["rope"]
            + [s["logs"], s["counts"], s["features"]]
            + [ANY] * len(after),
            out_specs=[pl.BlockSpec((1, 3, ROWS, 128), lambda g, c, w: (g, 0, 0, 0))],
            scratch_shapes=[
                pltpu.VMEM((GROUP, 128, span), bf16),
                pltpu.VMEM((GROUP, 128, whole), bf16),
                pltpu.VMEM((GROUP, 128, span), bf16),
                pltpu.VMEM((GROUP, HDIM, span), f32),
                pltpu.VMEM((GROUP, HDIM, whole), f32),
            ],
        ),
        out_shape=[jax.ShapeDtypeStruct((groups, 3, ROWS, 128), f32)],
        compiler_params=params(48),
        cost_estimate=cost(),
        name="attend_back",
    )(here, tq, tk, tv, hot, hot, hot3, cos, sin, cos, sin, logs, counts, datt, *after)[0])


def middle_kernel(att, wo, bo, hot3, packed, gain, shift, after, normed, weight):
    first = (pl.program_id(0) == 0) & (pl.program_id(1) == 0)

    @pl.when(first)
    def _():
        weight[0], weight[1] = split2(wo[...])

    w = (weight[0], weight[1])
    x = dot(hot3[0], packed[...]) + three(split2(att[0]), w, TN) + line(bo)
    after[...] = x
    normed[...] = norm_stats(x)[0] * line(gain) + line(shift)


def middle(here, att, wo, bo, hot3, packed, gain, shift):
    crops, width, span = att.shape
    block = min(256, span)
    steps = span // block
    full = lambda *dims: pl.BlockSpec(dims, lambda c, i, w: (0,) * len(dims))
    rows = pl.BlockSpec((block, width), lambda c, i, w: (c * steps + i, 0))
    out = jax.ShapeDtypeStruct((crops * span, width), f32)
    return pl.pallas_call(
        lambda w, *refs: middle_kernel(*refs),
        grid_spec=pltpu.PrefetchScalarGridSpec(
            num_scalar_prefetch=1,
            grid=(crops, steps),
            in_specs=[
                pl.BlockSpec((1, width, block), lambda c, i, w: (c, 0, i)),
                full(width, width),
                full(width),
                pl.BlockSpec((1, block, 128), lambda c, i, w: (c, w[1] * steps + i, 0)),
                full(128, width),
                full(width),
                full(width),
            ],
            out_specs=[rows, rows],
            scratch_shapes=[pltpu.VMEM((2, width, width), bf16)],
        ),
        out_shape=[out, out],
        compiler_params=params(32),
        cost_estimate=cost(),
        name="middle",
    )(here, att, wo, bo, hot3, packed, gain, shift)


def middle_back_kernel(
    after, d_own, d_swapped, cot, gain, att, wo, hot, clusters, biases, where, cluster, datt, keep, send,
    weight, product, sums, flat,
):
    crops, steps = pl.num_programs(0), pl.num_programs(1)
    step = pl.program_id(0) * steps + pl.program_id(1)
    width = wo.shape[0]
    tiles = width // 128

    @pl.when(step == 0)
    def _():
        weight[0], weight[1] = split2(wo[...])
        product[...] = jnp.zeros_like(product)
        sums[...] = jnp.zeros_like(sums)

    g = cot[...] * clusters[cluster[pl.program_id(0)]]
    unit, scale = norm_stats(after[...])
    d_normed = d_own[...] + d_swapped[...]
    d = g + norm_back(d_normed, unit, scale, line(gain))
    pair = split2(d)
    datt[0] = three((weight[0], weight[1]), pair, NT)
    product[...] += three(split2(att[0]), pair)
    ids = hot[0, :ROWS, :]
    sums[:ROWS] += dot(ids, pair[0]) + dot(ids, pair[1])
    vectors = [jnp.sum(v, axis=0, keepdims=True) for v in (d, d_normed * unit, d_normed, g)]
    sums[ROWS:] += jnp.concatenate(vectors + [jnp.zeros((4, width), f32)], axis=0)

    @pl.when(step == crops * steps - 1)
    def _():
        flat[...] = jnp.zeros_like(flat)
        for t in range(tiles):
            at = slice(t * 128, (t + 1) * 128)
            flat[t * width : (t + 1) * width, :] = product[:, at]
            base = tiles * width + t * (ROWS + 8)
            flat[base : base + ROWS + 8, :] = sums[:, at]
        base = tiles * (width + ROWS + 8)
        row = jnp.concatenate([b[...] for b in biases], axis=1)
        count = row.shape[1] // 128
        core = where[0]
        for t in range(count):
            flat[pl.ds(base + core * count + t, 1), :] = row[:, t * 128 : (t + 1) * 128]
        half = keep.shape[0]
        keep[...] = flat[pl.ds(pl.multiple_of(core * half, 8), half), :]
        send[...] = flat[pl.ds(pl.multiple_of((1 - core) * half, 8), half), :]


def middle_back(sides, cluster, clusters, after, d_own, d_swapped, cot, gain, att, wo, hot, biases, unit_rows, chain):
    crops, width, span = att.shape
    block = min(256, span)
    steps = span // block
    hidden = 2 * sum(b.shape[1] for b in biases)
    rows = width // 128 * (width + ROWS + 8) + hidden // 128
    rows += -rows % unit_rows
    full = lambda *dims: pl.BlockSpec(dims, lambda c, i, w, k: (0,) * len(dims))
    token = pl.BlockSpec((block, width), lambda c, i, w, k: (c * steps + i, 0))
    features = pl.BlockSpec((1, width, block), lambda c, i, w, k: (c, 0, i))
    like = jax.ShapeDtypeStruct
    deps = chain.deps()
    count = len(deps)

    def kernel(w, k, *refs):
        n = 9 + len(biases)
        middle_back_kernel(*refs[:9], refs[9:n], w, k, *refs[n + count :])

    out = pl.pallas_call(
        kernel,
        grid_spec=pltpu.PrefetchScalarGridSpec(
            num_scalar_prefetch=2,
            grid=(crops, steps),
            in_specs=[token] * 4
            + [
                full(width),
                features,
                full(width, width),
                pl.BlockSpec((1, 128, block), lambda c, i, w, k: (c, 0, w[1] * steps + i)),
            ]
            + [pl.BlockSpec(memory_space=pltpu.SMEM)]
            + [full(*b.shape) for b in biases]
            + [ANY] * count,
            out_specs=[features, full(rows // 2, 128), full(rows // 2, 128)],
            scratch_shapes=[
                pltpu.VMEM((2, width, width), bf16),
                pltpu.VMEM((width, width), f32),
                pltpu.VMEM((ROWS + 8, width), f32),
                pltpu.VMEM((rows, 128), f32),
            ],
        ),
        out_shape=[like((crops, width, span), f32)] + [like((rows // 2, 128), f32)] * 2,
        compiler_params=params(40),
        cost_estimate=cost(),
        name="middle_back",
    )(sides.array, cluster, after, d_own, d_swapped, cot, gain, att, wo, hot, clusters, *biases, *deps)
    chain.set(out[0])
    return out


BLOCK = 256


def three_wide(a, b, dims=NN):
    (i,), (j,) = dims[0]
    return dot(
        jnp.concatenate([a[0], a[0], a[1]], axis=i), jnp.concatenate([b[0], b[1], b[0]], axis=j), dims
    )


def ff_kernel(parts, unit_at, where, *refs):
    ends = 2 * len(parts)
    cluster, cluster_other = refs[:2]
    sources, clusters = refs[2:6], refs[6]
    up, up_bias, down = refs[7:10]
    outs, (bias, h1, h2, p1, p2, nh, nl, gh, gl) = refs[-9 - ends : -9], refs[-9:]

    @pl.when(pl.program_id(0) == 0)
    def _():
        half = nh.shape[0] // 2
        crops = cluster.shape[0]
        span = half // crops
        for i, source in enumerate(sources[:2]):
            at = slice(i * half, (i + 1) * half)
            nh[at], nl[at] = split2(source[...])
        for i, (source, ids) in enumerate(zip(sources[2:], (cluster, cluster_other))):
            for c in range(crops):
                at = slice(i * half + c * span, i * half + (c + 1) * span)
                gh[at], gl[at] = split2(source[c * span : (c + 1) * span] * clusters[ids[c]])

    step = pl.program_id(0)
    bias_at = pl.multiple_of(unit_at(where) + step * BLOCK, BLOCK)
    normed, grad = (nh[...], nl[...]), (gh[...], gl[...])
    up2, down2 = split2(up[...]), split2(down[...])
    u = three_wide(normed, up2) + up_bias[pl.ds(bias_at, BLOCK)].reshape(1, BLOCK)
    cdf = 0.5 * (1.0 + lax.erf(u * (0.5**0.5)))
    density = jnp.exp(-0.5 * u * u) * (1.0 / math.sqrt(2.0 * math.pi))
    ff = split2(u * cdf)
    d_pre = three_wide(grad, down2, NT) * (cdf + u * density)
    bias[...] = jnp.sum(d_pre, axis=0, keepdims=True)
    d_pre = split2(d_pre)
    h1[...], h2[...] = ff
    p1[...], p2[...] = d_pre
    g_down = three_wide(ff, grad, TN)
    g_up = three_wide(d_pre, normed, TN).T
    width = g_down.shape[1]

    def put(down_ref, up_ref):
        for t in range(width // 128):
            down_ref[t * BLOCK : (t + 1) * BLOCK, :] = g_down[:, t * 128 : (t + 1) * 128]
        for t in range(BLOCK // 128):
            up_ref[t * width : (t + 1) * width, :] = g_up[:, t * 128 : (t + 1) * 128]

    begin = 0
    for n, (split, blocks) in enumerate(parts):
        keep, send = outs[2 * n : 2 * n + 2]
        here = (step >= begin) & (step < begin + blocks)
        begin += blocks

        @pl.when(here & (where[split] == 0))
        def _():
            put(keep, send)

        @pl.when(here & (where[split] == 1))
        def _():
            put(send, keep)


def ff_chunk(sides, parts, scalars, sources, up, up_bias, down, first, buffers, chain):
    blocks = sum(count for _, count in parts)
    splits = [(sides.at(stage), count) for stage, count in parts]
    deps = chain.deps()
    width = sources[0].shape[1]
    tokens = 2 * sources[0].shape[0]
    hidden = up.shape[1]
    half = hidden // 2 // BLOCK
    slab = BLOCK * width // 128
    full = lambda *dims: pl.BlockSpec(dims, lambda j, w, *_: (0,) * len(dims))
    column = pl.BlockSpec((tokens, BLOCK), lambda j, w, *_: (0, first + j))
    like = jax.ShapeDtypeStruct
    slabs, begin = [], 0
    for _, count in parts:
        at = lambda j, w, *_, begin=begin, count=count: (jnp.clip(j - begin, 0, count - 1), 0)
        slabs += [pl.BlockSpec((slab, 128), at)] * 2
        begin += count
    out = pl.pallas_call(
        lambda *refs: ff_kernel(splits, lambda w: (w[0] * half + first) * BLOCK, *refs),
        grid_spec=pltpu.PrefetchScalarGridSpec(
            num_scalar_prefetch=1 + len(scalars),
            grid=(blocks,),
            in_specs=[full(*s.shape) if s.ndim == 2 else pl.BlockSpec(memory_space=pltpu.SMEM) for s in sources]
            + [
                pl.BlockSpec((width, BLOCK), lambda j, w, *_: (0, w[0] * half + first + j)),
                full(hidden),
                pl.BlockSpec((BLOCK, width), lambda j, w, *_: (w[0] * half + first + j, 0)),
            ]
            + [ANY] * (len(buffers) + len(deps)),
            out_specs=slabs
            + [pl.BlockSpec((1, BLOCK), lambda j, w, *_: (0, j))]
            + [column] * 4,
            scratch_shapes=[pltpu.VMEM((tokens, width), bf16)] * 4,
        ),
        out_shape=[like((slab * count, 128), f32) for _, count in parts for _ in range(2)]
        + [like((1, blocks * BLOCK), f32)]
        + [like((tokens, hidden // 2), bf16)] * 4,
        input_output_aliases={len(scalars) + len(sources) + 4 + i: 2 * len(parts) + 1 + i for i in range(len(buffers))},
        compiler_params=params(58),
        cost_estimate=cost(),
        name="feed",
    )(sides.array, *scalars, *sources, up, up_bias, down, *buffers, *deps)
    chain.set(out[0])
    return out


def back_product_kernel(dims, where, a1, a2, w, *refs):
    own, other = refs[-2:]
    step = pl.program_id(0)
    out = three_wide((a1[...], a2[...]), split2(w[...]), dims)
    half = own.shape[0]

    @pl.when(step == 0)
    def _():
        own[...] = out[:half]
        other[...] = out[half:]

    @pl.when(step > 0)
    def _():
        own[...] += out[:half]
        other[...] += out[half:]


def back_product(sides, a, weight, dims, chain):
    tokens, units = a[0].shape
    deps = chain.deps()
    wide = 5 * BLOCK // 2 if units % (5 * BLOCK) == 0 else BLOCK
    steps = units // wide
    up_like = dims is NT
    width = weight.shape[0 if up_like else 1]
    out = jax.ShapeDtypeStruct((tokens // 2, width), f32)
    spec = (
        pl.BlockSpec((width, wide), lambda j, w: (0, w[0] * steps + j))
        if up_like
        else pl.BlockSpec((wide, width), lambda j, w: (w[0] * steps + j, 0))
    )
    out = pl.pallas_call(
        lambda *refs: back_product_kernel(dims, *refs),
        grid_spec=pltpu.PrefetchScalarGridSpec(
            num_scalar_prefetch=1,
            grid=(steps,),
            in_specs=[pl.BlockSpec((tokens, wide), lambda j, w: (0, j))] * 2 + [spec] + [ANY] * len(deps),
            out_specs=[pl.BlockSpec((tokens // 2, width), lambda j, w: (0, 0))] * 2,
        ),
        out_shape=[out, out],
        compiler_params=params(48),
        cost_estimate=cost(),
        name="feed_back" if up_like else "feed_out",
    )(sides.array, *a, weight, *deps)
    chain.set(out[0])
    return out


class Chain:
    def __init__(self):
        self.last = []

    def deps(self):
        return list(self.last)

    def set(self, out):
        self.last = [out]
        return out


def bits_of(axis):
    size = lax.axis_size(axis)
    return [(axis, 1 << i) for i in range(size.bit_length() - 1)]


def swap(x, stage):
    axis, bit = stage
    return lax.ppermute(x, axis, [(i, i ^ bit) for i in range(lax.axis_size(axis))])


def side(stage):
    axis, bit = stage
    return ((lax.axis_index(axis) // bit) % 2).astype(jnp.int32)


class Sides:
    def __init__(self, core_stage, stages):
        self.stages = list(dict.fromkeys(stages))
        self.core_at = 2 + self.stages.index(core_stage)
        self.array = jnp.stack(
            [side(core_stage), lax.axis_index("seq").astype(jnp.int32)] + [side(s) for s in self.stages]
        )

    def at(self, stage):
        return 2 + self.stages.index(stage)


def add_split_kernel(where, k_here, r_here, k_away, r_away, *refs):
    keep, send = refs[-2:]
    keep[...] = k_here[...] + r_here[...]
    send[...] = k_away[...] + r_away[...]


def add_split(kept, received, sides, stage, chain):
    rows, lanes = kept.shape
    half = rows // 2
    at = sides.at(stage)
    if half % 8:
        total = kept + received
        me = side(stage)
        return (
            lax.dynamic_slice_in_dim(total, me * half, half, 0),
            lax.dynamic_slice_in_dim(total, (1 - me) * half, half, 0),
        )
    deps = chain.deps()
    steps = 2 if half % 16 == 0 and half >= 512 else 1
    block = (half // steps, lanes)
    here = pl.BlockSpec(block, lambda i, w: (w[at] * steps + i, 0))
    away = pl.BlockSpec(block, lambda i, w: ((1 - w[at]) * steps + i, 0))
    plain = pl.BlockSpec(block, lambda i, w: (i, 0))
    out = jax.ShapeDtypeStruct((half, lanes), f32)
    keep, send = pl.pallas_call(
        add_split_kernel,
        grid_spec=pltpu.PrefetchScalarGridSpec(
            num_scalar_prefetch=1,
            grid=(steps,),
            in_specs=[here, here, away, away] + [ANY] * len(deps),
            out_specs=[plain, plain],
        ),
        out_shape=[out, out],
        compiler_params=params(16),
        cost_estimate=cost(STEP),
        name="add_split",
    )(sides.array, kept, received, kept, received, *deps)
    chain.set(keep)
    return keep, send


def add_kernel(a, b, *refs):
    refs[-1][...] = a[...] + b[...]


def add(a, b, chain):
    deps = chain.deps()
    full = pl.BlockSpec(a.shape, lambda: (0,) * a.ndim)
    return chain.set(
        pl.pallas_call(
            add_kernel,
            in_specs=[full, full] + [ANY] * len(deps),
            out_specs=full,
            out_shape=jax.ShapeDtypeStruct(a.shape, f32),
            compiler_params=params(16),
            cost_estimate=cost(STEP),
            name="add",
        )(a, b, *deps)
    )


def join_kernel(at, where, x, other, *refs):
    out = refs[-1]
    mine = pl.program_id(0) == where[at]

    @pl.when(mine)
    def _():
        out[...] = x[...]

    @pl.when(jnp.logical_not(mine))
    def _():
        out[...] = other[...]


def join(x, other, sides, stage, chain):
    if x.shape[0] % 8:
        return jnp.where(
            side(stage) == 0, jnp.concatenate([x, other], axis=0), jnp.concatenate([other, x], axis=0)
        )
    deps = chain.deps()
    at = sides.at(stage)
    full = pl.BlockSpec(x.shape, lambda i, w: (0, 0))
    return chain.set(
        pl.pallas_call(
            lambda *refs: join_kernel(at, *refs),
            grid_spec=pltpu.PrefetchScalarGridSpec(
                num_scalar_prefetch=1,
                grid=(2,),
                in_specs=[full, full] + [ANY] * len(deps),
                out_specs=pl.BlockSpec(x.shape, lambda i, w: (i, 0)),
            ),
            out_shape=jax.ShapeDtypeStruct((2 * x.shape[0], x.shape[1]), f32),
            compiler_params=params(16),
            cost_estimate=cost(STEP),
            name="join",
        )(sides.array, x, other, *deps)
    )


class Sum:
    def __init__(self, keep, send, stages, sides, chain, flat=1):
        self.x, self.stages, self.sides, self.chain = keep, stages, sides, chain
        self.cut = len(stages) - flat
        self.moves = list(range(len(stages))) + list(reversed(range(self.cut)))
        self.at = 0
        self.coming = swap(send, stages[0])

    def step(self):
        done = self.at
        self.at += 1
        stage = self.stages[self.moves[self.at]]
        if self.at < self.cut:
            self.x, send = add_split(self.x, self.coming, self.sides, stage, self.chain)
        elif done < len(self.stages):
            self.x = send = add(self.x, self.coming, self.chain)
        else:
            self.x = send = join(self.x, self.coming, self.sides, self.stages[self.moves[done]], self.chain)
        self.coming = swap(send, stage)

    @property
    def left(self):
        return len(self.moves) - 1 - self.at

    def whole(self):
        return join(self.x, self.coming, self.sides, self.stages[0], self.chain)


def place_kernel(split, items, first, blocks, width, half, where, *refs):
    down, up, sems = refs[-3:]
    tiles = width // 128

    def copies(side):
        out = []
        for i, (mine, own) in enumerate(items):
            base = pl.multiple_of((where[0] if mine else 1 - where[0]) * half + first * BLOCK, BLOCK)
            if own == (side == 0):
                for n in range(blocks * tiles):
                    rows = pl.ds(pl.multiple_of(base + n // tiles * BLOCK, BLOCK), BLOCK)
                    out.append((refs[i].at[pl.ds(n * BLOCK, BLOCK), :], down.at[rows, pl.ds(n % tiles * 128, 128)]))
            else:
                for n in range(blocks * BLOCK // 128):
                    at = pl.multiple_of(base + n * 128, 128)
                    out.append((refs[i].at[pl.ds(n * width, width), :], up.at[:, pl.ds(at, 128)]))
        return [pltpu.make_async_copy(a, b, sems.at[n]) for n, (a, b) in enumerate(out)]

    for side in range(2):

        @pl.when(where[split] == side)
        def _():
            moving = copies(side)
            for m in moving:
                m.start()
            for m in moving:
                m.wait()


def place(sides, stage, items, first, blocks, width, hidden, buffers, chain):
    split = sides.at(stage)
    deps = chain.deps()
    kinds = [(mine, own) for _, mine, own in items]
    arrays = [x for x, _, _ in items]
    most = len(items) * blocks * max(width, BLOCK) // 128
    outs = pl.pallas_call(
        lambda *refs: place_kernel(split, kinds, first, blocks, width, hidden // 2, *refs),
        grid_spec=pltpu.PrefetchScalarGridSpec(
            num_scalar_prefetch=1,
            grid=(1,),
            in_specs=[ANY] * (len(arrays) + len(buffers) + len(deps)),
            out_specs=[ANY, ANY],
            scratch_shapes=[pltpu.SemaphoreType.DMA((most,))],
        ),
        out_shape=[
            jax.ShapeDtypeStruct((hidden, width), f32),
            jax.ShapeDtypeStruct((width, hidden), f32),
        ],
        input_output_aliases={1 + len(arrays) + i: i for i in range(len(buffers))},
        compiler_params=params(8),
        cost_estimate=cost(STEP),
        name="place",
    )(sides.array, *arrays, *buffers, *deps)
    chain.set(arrays[0])
    return outs


FLAT = dict(a=1, b=1, c=2, d=2)
ROUTES = dict(a="xyzw", b="zxyw", c="yzxw", d="kyzwx", e="kxzwy")

PLAN = " ".join(
    [
        "feed_a", "feed_bc", "back", "a", "middle", "attend0", "b", "a", "d", "c", "attend1", "a", "b", "d",
        "attend2", "b", "attend3", "c", "d", "a", "attend4", "tables", "b", "e", "c", "d", "a", "e", "b", "d",
        "e", "c", "d", "a", "e", "b", "c", "d", "Ec", "out", "e", "finish", "La", "Eb", "Lb", "Lc", "Pa", "Ea",
        "Pb", "Pc",
    ]
)


def local(
    token_ids,
    embedding,
    first_gain,
    first_shift,
    query_weight,
    query_bias,
    key_weight,
    key_bias,
    value_weight,
    value_bias,
    out_weight,
    out_bias,
    second_gain,
    second_shift,
    up_weight,
    up_bias,
    down_weight,
    down_bias,
    cotangent,
    crop_cluster,
    cluster_weight,
):
    crops, span = token_ids.shape
    width = embedding.shape[1]
    units = up_weight.shape[1]
    ring = lax.axis_size("seq")
    whole = span * ring
    seq_bits, crop_bits = bits_of("seq"), bits_of("crop")
    core_stage, across, along = crop_bits[0], crop_bits[1:2], crop_bits[2:]
    axes = dict(x=across, y=seq_bits, z=along[:1], w=along[1:], k=[core_stage])
    route = {name: sum((axes[axis] for axis in path), []) for name, path in ROUTES.items()}
    sides = Sides(core_stage, seq_bits + crop_bits)
    chain = Chain()

    if ring == 2:
        ids = [token_ids, swap(token_ids, ("seq", 1))]
    else:
        ids = [lax.all_gather(token_ids, "seq", axis=1, tiled=True)]
    cot = cotangent.reshape(-1, width)
    cot_other = swap(cot, core_stage)
    cluster_other = swap(crop_cluster, core_stage)

    frequency = (10000.0 ** (-2.0 * np.arange(HALF) / HDIM)).astype(np.float32)
    angles = (frequency[:, None] * np.arange(whole, dtype=np.float32)[None, :]).astype(np.float64)
    cos, sin = jnp.asarray(np.cos(angles), f32), jnp.asarray(np.sin(angles), f32)

    tq, tk, tv, packed = project_rows(
        embedding, first_gain, first_shift, query_weight, query_bias, key_weight, key_bias, value_weight, value_bias
    )
    hot, hot3 = spots(sides, ids, whole, [tq])
    att, logs, counts = attention_forward(sides.array, tq, tk, tv, hot, cos, sin, span)
    after_attn, normed = middle(sides.array, att, out_weight, out_bias, hot3, packed, second_gain, second_shift)

    sources = [normed, swap(normed, core_stage), cot, cot_other, cluster_weight]
    scalars = [crop_cluster, cluster_other]
    blocks = units // 2 // BLOCK
    third = 2 * (blocks // 5)
    spans = {}
    first = 0
    for name, count in (("a", third), ("b", third), ("c", blocks - 2 * third)):
        spans[name] = (first, count, route[name])
        first += count
    devices = lax.axis_size("seq") * lax.axis_size("crop")

    sums, biases, tables, early, late, outs, buffers = {}, [], [], {}, {}, [], []

    def step(name):
        total = sums[name]
        if total.left:
            total.step()
            if name in spans and not total.left:
                early[name] = swap(total.x, core_stage)

    def complete(*names):
        while any(sums[name].left for name in names):
            for name in names:
                step(name)

    def put(name, items):
        first, count, stages = spans[name]
        return place(sides, stages[0], items, first, count, width, units, outs, chain)

    for item in PLAN.split():
        kind, name = item.rstrip("01234"), item[-1]
        if item in sums:
            step(item)
        elif kind[0] == "E":
            complete(name)
            outs = put(name, [(early[name], False, True), (sums[name].x, True, True)])
        elif kind[0] == "L":
            complete(name)
            late[name] = swap(sums[name].coming, core_stage)
        elif kind[0] == "P":
            outs = put(name, [(late[name], False, False), (sums[name].coming, True, False)])
        elif kind == "finish":
            complete("d", "e")
            table, rest = sums["e"].whole(), sums["d"].whole()
            g_wq, g_wk, g_wv, g_ow, g_bq, g_bk, g_bv, g_emb, g_gain, g_shift, g_ob, g_sg, g_ss, g_db, g_ub = finish(
                embedding, first_gain, first_shift, table, rest, query_weight, key_weight, value_weight, units, chain
            )
        elif kind.startswith("feed"):
            names = item[5:]
            out = ff_chunk(
                sides, [(route[n][0], spans[n][1]) for n in names], scalars, sources, up_weight, up_bias, down_weight,
                spans[names[0]][0], buffers, chain,
            )
            for n in names:
                keep, send, *out = out
                sums[n] = Sum(keep, send, route[n], sides, chain, FLAT[n])
            bias, *buffers = out
            biases.append(bias)
        elif kind == "back":
            h1, h2, p1, p2 = buffers
            d_own, d_other = back_product(sides, (p1, p2), up_weight, NT, chain)
            d_swapped = swap(d_other, core_stage)
        elif kind == "middle":
            d_att, keep, send = middle_back(
                sides, crop_cluster, cluster_weight, after_attn, d_own, d_swapped, cot, second_gain, att, out_weight,
                hot, biases, 8 * devices, chain,
            )
            sums["d"] = Sum(keep, send, route["d"], sides, chain, FLAT["d"])
        elif kind == "attend":
            tables.append(
                attention_backward(
                    sides.array, tq, tk, tv, hot, hot3, cos, sin, logs, counts, d_att, int(name), 1, chain
                )
            )
        elif kind == "tables":
            sums["e"] = Sum(*pack_tables(sides, tables, 16, chain), route["e"], sides, chain, len(route["e"]) - 1)
        elif kind == "out":
            o_own, o_other = back_product(sides, (h1, h2), down_weight, NN, chain)
            o_swapped = swap(o_other, core_stage)
            block_out = (after_attn + o_own + o_swapped + down_bias).reshape(cotangent.shape)
    g_dw, g_uw = outs
    return (
        block_out, g_emb, g_gain, g_shift, g_wq, g_bq, g_wk, g_bk, g_wv, g_bv, g_ow, g_ob, g_sg, g_ss, g_uw, g_ub,
        g_dw, g_db,
    )


def solution(mesh):
    in_specs = (
        (P("crop", "seq"),) + (P(),) * 17 + (P("crop", "seq", None), P("crop"), P())
    )
    out_specs = (P("crop", "seq", None),) + (P(),) * 17
    return jax.shard_map(local, mesh=mesh, in_specs=in_specs, out_specs=out_specs, check_vma=False)
```
